32 devices in a mesh: dp: 4 (over z), rows: 8 (over y, x, core).
Axes of the slice: x: 2, y: 2, z: 4, core: 2. Of those that a mesh axis runs over, the one named last changes fastest.
Arguments:
- item_ids: int32 [2, 32, 512], P(None, ('dp', 'rows')), may hold values from 0 to 200703, as said below
- targets: int32 [2, 32, 512], P(None, ('dp', 'rows')), may hold values from 0 to 200703, as said below
- lengths: int32 [2, 32], P(None, ('dp', 'rows')), may hold values from 1 to 512, as said below
- correction: float32 [2, 32, 512], P(None, ('dp', 'rows')), may hold values from -9 to -6
- item_row: int32 [200704], replicated, may hold values from 0 to 200703, as said below
- item_table: float32 [200704, 256], P(('dp', 'rows')), may hold values from -0.6 to 0.6
- qkv_weight: float32 [256, 1536], replicated, may hold values from -0.375 to 0.375
- out_weight: float32 [512, 256], replicated, may hold values from -1 to 1
- up_weight: float32 [256, 1024], replicated, may hold values from -0.375 to 0.375
- down_weight: float32 [1024, 256], replicated, may hold values from -0.1875 to 0.1875
- positions: float32 [512, 256], replicated, may hold values from -0.6 to 0.6
- gains: float32 [3, 256], replicated, may hold values from 0.5 to 1.5
- item_table_first: float32 [200704, 256], P(('dp', 'rows')), may hold values from -0.00015258789 to 0.00015258789
- qkv_weight_first: float32 [256, 1536], replicated, may hold values from -0.0004272461 to 0.0004272461
- out_weight_first: float32 [512, 256], replicated, may hold values from -0.0004272461 to 0.0004272461
- up_weight_first: float32 [256, 1024], replicated, may hold values from -0.0004272461 to 0.0004272461
- down_weight_first: float32 [1024, 256], replicated, may hold values from -0.0004272461 to 0.0004272461
- positions_first: float32 [512, 256], replicated, may hold values from -7.6293945e-05 to 7.6293945e-05
- gains_first: float32 [3, 256], replicated, may hold values from -0.0017089844 to 0.0017089844
- item_table_second: float32 [200704, 256], P(('dp', 'rows')), may hold values from 5.960465e-11 to 2.384186e-10
- qkv_weight_second: float32 [256, 1536], replicated, may hold values from 4.2385526e-10 to 1.695421e-09
- out_weight_second: float32 [512, 256], replicated, may hold values from 4.2385526e-10 to 1.695421e-09
- up_weight_second: float32 [256, 1024], replicated, may hold values from 4.2385526e-10 to 1.695421e-09
- down_weight_second: float32 [1024, 256], replicated, may hold values from 4.2385526e-10 to 1.695421e-09
- positions_second: float32 [512, 256], replicated, may hold values from 1.4901162e-11 to 5.960465e-11
- gains_second: float32 [3, 256], replicated, may hold values from 6.781684e-09 to 2.7126736e-08
Outputs:
- new_item_table: float32 [200704, 256], P(('dp', 'rows'))
- new_qkv_weight: float32 [256, 1536], replicated
- new_out_weight: float32 [512, 256], replicated
- new_up_weight: float32 [256, 1024], replicated
- new_down_weight: float32 [1024, 256], replicated
- new_positions: float32 [512, 256], replicated
- new_gains: float32 [3, 256], replicated
- new_item_table_first: float32 [200704, 256], P(('dp', 'rows'))
- new_qkv_weight_first: float32 [256, 1536], replicated
- new_out_weight_first: float32 [512, 256], replicated
- new_up_weight_first: float32 [256, 1024], replicated
- new_down_weight_first: float32 [1024, 256], replicated
- new_positions_first: float32 [512, 256], replicated
- new_gains_first: float32 [3, 256], replicated
- new_item_table_second: float32 [200704, 256], P(('dp', 'rows'))
- new_qkv_weight_second: float32 [256, 1536], replicated
- new_out_weight_second: float32 [512, 256], replicated
- new_up_weight_second: float32 [256, 1024], replicated
- new_down_weight_second: float32 [1024, 256], replicated
- new_positions_second: float32 [512, 256], replicated
- new_gains_second: float32 [3, 256], replicated
- loss_sum: float32 [], replicated
- valid_count: float32 [], replicated
- grad_norm: float32 [], replicated
The draws below stay inside these ranges and needn't reach their ends.
Inputs may be any that keep to these rules, and one draw needn't show every extreme that they name: Owner block o holds table rows o * 6272 to (o + 1) * 6272 - 1, and device o in the order dp then rows holds it. Among the item_ids and targets of the histories of one device (both micro-batches), the entries at positions below their history's length whose table row lies in one owner block number at most 98; in every draw some owner block gets exactly 98 from every device. `targets`: counted together with item_ids in the bound stated there. `lengths`: some history has all 512 positions. A permutation: item i is stored in table row item_row[i].
All inputs are finite; a program needn't handle non-finite values.
Results may differ from the reference program's by a relative error of at most 0.012.
The reference program's roundings to bfloat16 on the way count: a program that leaves them out, or rounds other values in their place, can miss the bound.
Values may be sent and summed in bfloat16 or wider, within the bound.
A program may use at most 256 MiB of HBM per device.

```python
import math
import jax
import jax.numpy as jnp
from jax import lax

D = 256
HEADS = 8
INNER = 512
FF = 1024
L = 512
ITEMS = 200704
MB = 2
SEQ_DEV = 1
STEP = 10
DP_COUNT = 4
ROW_COUNT = 8
HIST = 32
ROWS_DEV = 6272
CAP = 98


def draw_plan(key):
    devices = HIST // SEQ_DEV
    requests = 2 * MB * SEQ_DEV * L
    early_rows = (CAP + 2 * MB * SEQ_DEV - 1) // (2 * MB * SEQ_DEV)
    key_rows, key_full, key_lengths, key_devices = jax.random.split(key, 4)
    item_row = jax.random.permutation(key_rows, ITEMS).astype(jnp.int32)
    row_item = jnp.argsort(item_row).astype(jnp.int32)
    span_all = (DP_COUNT - 1) * (ROW_COUNT - 1)
    owners = jnp.arange(devices, dtype=jnp.int32)
    climb_up = span_all + 2 * (owners // ROW_COUNT) * (ROW_COUNT - 1) + 2 * (owners % ROW_COUNT) * (DP_COUNT - 1)
    quota_of = jnp.clip(CAP * climb_up * climb_up // (25 * span_all * span_all), 1, CAP)
    order_of = jax.random.permutation(key_full, devices).astype(jnp.int32)
    chosen = jnp.argmax(jnp.where(quota_of == CAP, order_of, -1)).astype(jnp.int32)
    hist_owner = jnp.arange(HIST, dtype=jnp.int32) // SEQ_DEV
    base_len = L * (span_all + 2 * (hist_owner // ROW_COUNT) * (ROW_COUNT - 1) + 2 * (hist_owner % ROW_COUNT) * (DP_COUNT - 1)) // (5 * span_all)
    shrink = jax.random.randint(key_lengths, (MB, HIST), 0, L // 8 + 1).astype(jnp.int32)
    shrink = shrink.at[0, HIST - 1].set(0)
    lengths = jnp.clip(base_len[None, :] - shrink, max(early_rows, 1), L).astype(jnp.int32)
    pool_size = devices * CAP
    entry_of = jnp.arange(pool_size, dtype=jnp.int32)
    entry_owner = entry_of // CAP
    entry_class = jnp.where(entry_owner == chosen, 0, jnp.where(entry_of % CAP < quota_of[entry_owner], 1, 2))
    overflow_key = 2 * 1048576 + (5 * span_all - climb_up[entry_owner]) * CAP + entry_of % CAP
    slot_all = jnp.arange(requests, dtype=jnp.int32)
    slot_class = jnp.where(slot_all % L < early_rows, 0, 1)

    def one_device(device_key):
        key_entry, key_slot, key_local = jax.random.split(device_key, 3)
        entry_rank = jax.random.permutation(key_entry, pool_size).astype(jnp.int32)
        entry_key = jnp.where(entry_class == 2, overflow_key, entry_class * 1048576 + entry_rank)
        picked = jnp.argsort(entry_key)[:requests]
        slot_rank = jax.random.permutation(key_slot, requests).astype(jnp.int32)
        slot_order = jnp.argsort(slot_class * requests + slot_rank)
        owner_slot = jnp.zeros((requests,), jnp.int32).at[slot_order].set(entry_owner[picked])
        local_row = jax.random.randint(key_local, (requests,), 0, ROWS_DEV).astype(jnp.int32)
        return row_item[owner_slot * ROWS_DEV + local_row]
    items_all = jax.vmap(one_device)(jax.random.split(key_devices, devices))
    items_all = items_all.reshape(devices, 2, MB, SEQ_DEV, L)
    item_ids = jnp.transpose(items_all[:, 0], (1, 0, 2, 3)).reshape(MB, HIST, L)
    targets = jnp.transpose(items_all[:, 1], (1, 0, 2, 3)).reshape(MB, HIST, L)
    return (item_row, item_ids.astype(jnp.int32), targets.astype(jnp.int32), lengths)


def draw_item_ids(key, part):
    return draw_plan(key)[1]


def draw_targets(key, part):
    return draw_plan(key)[2]


def draw_lengths(key, part):
    return draw_plan(key)[3]


def draw_item_row(key, part):
    return draw_plan(key)[0]


def block_scale(rng, dims, cuts, least, largest):
    gain, own = 1.0, jax.random.fold_in(rng, 6)
    for axis_at, parts in cuts:
        steps = jnp.exp(jax.random.uniform(jax.random.fold_in(own, axis_at), (parts,), jnp.float32, least / len(cuts), largest / len(cuts)))
        gain = gain * jnp.repeat(steps, dims[axis_at] // parts).reshape([-1 if axis == axis_at else 1 for axis in range(len(dims))])
    return gain


def bell_draw(key, shape, spread, limit, cuts=(), kind=jnp.bfloat16):
    gain = block_scale(key, shape, cuts, -0.22, 0.18) if cuts else 1.0
    values = jax.random.normal(key, shape, jnp.float32) * spread * gain
    return jnp.minimum(jnp.maximum(values, -limit), limit).astype(kind)


def setup_inputs(seed: int = 0) -> dict:
    key_list = jax.random.split(jax.random.key(seed), 27)
    item_ids = draw_item_ids(jax.random.fold_in(key_list[26], 71), 0)
    targets = draw_targets(jax.random.fold_in(key_list[26], 71), 0)
    lengths = draw_lengths(jax.random.fold_in(key_list[26], 71), 0)
    correction = jnp.clip(-9.0 + 3.0 * jax.random.uniform(key_list[3], (MB, HIST, L), jnp.float32) ** block_scale(key_list[3], (MB, HIST, L), ((1, 32),), -0.2, 0.2), -9.0, -6.0)
    item_row = draw_item_row(jax.random.fold_in(key_list[26], 71), 0)
    item_table = bell_draw(key_list[5], (ITEMS, D), 0.1, 0.6, ((0, 32),), jnp.float32)
    qkv_weight = bell_draw(key_list[6], (D, 3 * INNER), D ** -0.5, 0.375, (), jnp.float32)
    out_weight = bell_draw(key_list[7], (INNER, D), (INNER // 16) ** -0.5, 1.0, (), jnp.float32)
    up_weight = bell_draw(key_list[8], (D, FF), D ** -0.5, 0.375, (), jnp.float32)
    down_weight = bell_draw(key_list[9], (FF, D), FF ** -0.5, 0.1875, (), jnp.float32)
    positions = bell_draw(key_list[10], (L, D), 0.1, 0.6, (), jnp.float32)
    gains = jnp.clip(1.0 + 0.1 * jax.random.normal(key_list[11], (3, D), jnp.float32), 0.5, 1.5)
    item_table_first = bell_draw(key_list[12], (ITEMS, D), (0.11 * (2 * D * MB * HIST * L) ** -0.5), 0.00015258789, ((0, 32),), jnp.float32)
    qkv_weight_first = bell_draw(key_list[13], (D, 3 * INNER), (0.11 * (2 * (4 * D * INNER + 2 * D * FF + L * D)) ** -0.5), 0.0004272461, (), jnp.float32)
    out_weight_first = bell_draw(key_list[14], (INNER, D), (0.11 * (2 * (4 * D * INNER + 2 * D * FF + L * D)) ** -0.5), 0.0004272461, (), jnp.float32)
    up_weight_first = bell_draw(key_list[15], (D, FF), (0.11 * (2 * (4 * D * INNER + 2 * D * FF + L * D)) ** -0.5), 0.0004272461, (), jnp.float32)
    down_weight_first = bell_draw(key_list[16], (FF, D), (0.11 * (2 * (4 * D * INNER + 2 * D * FF + L * D)) ** -0.5), 0.0004272461, (), jnp.float32)
    positions_first = bell_draw(key_list[17], (L, D), (0.11 * (2 * D * D * L) ** -0.5), 7.62939453125e-05, (), jnp.float32)
    gains_first = bell_draw(key_list[18], (3, D), (0.44 * (2 * (4 * D * INNER + 2 * D * FF + L * D)) ** -0.5), 0.0017089844, (), jnp.float32)
    item_table_second = jnp.clip(jnp.exp(math.log(2.3841859042583735e-10) - 1.3862944 * jax.random.uniform(key_list[19], (ITEMS, D), jnp.float32) ** block_scale(key_list[19], (ITEMS, D), ((0, 32),), -0.2, 0.2)), 5.960464760645934e-11, 2.3841859042583735e-10)
    qkv_weight_second = jnp.clip(jnp.exp(jax.random.uniform(key_list[20], (D, 3 * INNER), jnp.float32, math.log(4.2385525644839106e-10), math.log(1.6954210257935642e-09))), 4.2385525644839106e-10, 1.6954210257935642e-09)
    out_weight_second = jnp.clip(jnp.exp(jax.random.uniform(key_list[21], (INNER, D), jnp.float32, math.log(4.2385525644839106e-10), math.log(1.6954210257935642e-09))), 4.2385525644839106e-10, 1.6954210257935642e-09)
    up_weight_second = jnp.clip(jnp.exp(jax.random.uniform(key_list[22], (D, FF), jnp.float32, math.log(4.2385525644839106e-10), math.log(1.6954210257935642e-09))), 4.2385525644839106e-10, 1.6954210257935642e-09)
    down_weight_second = jnp.clip(jnp.exp(jax.random.uniform(key_list[23], (FF, D), jnp.float32, math.log(4.2385525644839106e-10), math.log(1.6954210257935642e-09))), 4.2385525644839106e-10, 1.6954210257935642e-09)
    positions_second = jnp.clip(jnp.exp(jax.random.uniform(key_list[24], (L, D), jnp.float32, math.log(1.4901161901614834e-11), math.log(5.960464760645934e-11))), 1.4901161901614834e-11, 5.960464760645934e-11)
    gains_second = jnp.clip(jnp.exp(jax.random.uniform(key_list[25], (3, D), jnp.float32, math.log(6.781684103174257e-09), math.log(2.7126736412697028e-08))), 6.781684103174257e-09, 2.7126736412697028e-08)
    return {"item_ids": item_ids, "targets": targets, "lengths": lengths, "correction": correction, "item_row": item_row, "item_table": item_table, "qkv_weight": qkv_weight, "out_weight": out_weight, "up_weight": up_weight, "down_weight": down_weight, "positions": positions, "gains": gains, "item_table_first": item_table_first, "qkv_weight_first": qkv_weight_first, "out_weight_first": out_weight_first, "up_weight_first": up_weight_first, "down_weight_first": down_weight_first, "positions_first": positions_first, "gains_first": gains_first, "item_table_second": item_table_second, "qkv_weight_second": qkv_weight_second, "out_weight_second": out_weight_second, "up_weight_second": up_weight_second, "down_weight_second": down_weight_second, "positions_second": positions_second, "gains_second": gains_second}


NORM_EPS = 1e-06
MASKED = -1e+30
BETA_ONE = 0.9
BETA_TWO = 0.999
ADAM_EPS = 1e-08
DECAY = 0.01
RATE = 0.1
GAIN_RATE = 1.0
CLIP = 1.0
HIGHEST = lax.Precision.HIGHEST

@jax.custom_vjp
def low(v):
    return lax.optimization_barrier(v.astype(jnp.bfloat16)).astype(jnp.float32)

@jax.custom_vjp
def low_back(v):
    return v

def low_keep(v):
    return (low(v), None)

def low_pass(kept, grad):
    return (grad,)

def back_keep(v):
    return (v, None)

def back_low(kept, grad):
    return (low(grad),)
low.defvjp(low_keep, low_pass)
low_back.defvjp(back_keep, back_low)

def rms_norm(values, gain_row):
    return values * lax.rsqrt(lax.optimization_barrier(jnp.mean(values * values, axis=-1, keepdims=True)) + NORM_EPS) * gain_row

def matmul(first_op, second_op):
    return jnp.dot(first_op, second_op, precision=HIGHEST)

def attention(joined, lengths_here):
    groups, length = (joined.shape[0], joined.shape[1])
    pieces = joined.reshape(groups, length, 3, HEADS, -1)
    queries, key_rows, value_rows = (pieces[:, :, 0], pieces[:, :, 1], pieces[:, :, 2])
    scaling = queries.shape[-1] ** (-0.5)
    scores = low_back(jnp.einsum('gqhe,gkhe->ghqk', queries, key_rows, precision=HIGHEST) * scaling)
    position = jnp.arange(length, dtype=jnp.int32)
    allowed = (position[None, :] <= position[:, None])[None, None] & (position[None, None, None, :] < lengths_here[:, None, None, None])
    scores = jnp.where(allowed, scores, MASKED)
    highest = lax.optimization_barrier(jnp.max(scores, axis=-1, keepdims=True))
    weights = jnp.exp(scores - highest)
    probabilities = low(weights / lax.optimization_barrier(jnp.sum(weights, axis=-1, keepdims=True)))
    attended = jnp.einsum('ghqk,gkhe->gqhe', probabilities, value_rows, precision=HIGHEST)
    return attended.reshape(groups * length, -1)

def group_loss(lowered, item_row, group_pieces):
    table_low, qkv_low, out_low, up_low, down_low, positions, gains = lowered
    ids_here, targets_here, lengths_here, correction_here = group_pieces
    groups = ids_here.shape[0]
    width = table_low.shape[1]
    embedded = math.sqrt(width) * table_low[item_row[ids_here]] + positions[None]
    embedded = embedded.reshape(groups * L, width)
    hidden_one = low(rms_norm(embedded, gains[0]))
    joined = low_back(low(matmul(hidden_one, qkv_low)))
    attended = low_back(low(attention(joined.reshape(groups, L, -1), lengths_here)))
    middle = embedded + low_back(matmul(attended, out_low))
    hidden_two = low(rms_norm(middle, gains[1]))
    upward = low_back(matmul(hidden_two, up_low))
    output = middle + low_back(matmul(low(jax.nn.gelu(upward)), down_low))
    query_low = low(rms_norm(output, gains[2]))
    candidates = table_low[item_row[targets_here]].reshape(groups * L, width)
    valid_pos = (jnp.arange(L, dtype=jnp.int32)[None, :] < lengths_here[:, None]).reshape(-1)
    cand_bias = jnp.where(valid_pos, low(-correction_here.reshape(-1)), MASKED)
    block_rows = min(512, groups * L)
    blocks = groups * L // block_rows
    column = jnp.arange(groups * L, dtype=jnp.int32)

    def block_loss(block_pieces):
        query_block, valid_block, start_row = block_pieces
        logits = low_back(jnp.dot(query_block, candidates.T, precision=HIGHEST)) + cand_bias[None]
        highest = lax.optimization_barrier(jnp.max(logits, axis=1, keepdims=True))
        log_total = highest[:, 0] + jnp.log(lax.optimization_barrier(jnp.sum(jnp.exp(logits - highest), axis=1)))
        target_hit = column[None, :] == (start_row + jnp.arange(block_rows, dtype=jnp.int32))[:, None]
        own_logit = lax.optimization_barrier(jnp.sum(jnp.where(target_hit, logits, 0.0), axis=1))
        return jnp.sum(jnp.where(valid_block, log_total - own_logit, 0.0))
    losses = lax.map(jax.checkpoint(block_loss), (query_low.reshape(blocks, block_rows, width), valid_pos.reshape(blocks, block_rows), jnp.arange(blocks, dtype=jnp.int32) * block_rows))
    return jnp.sum(losses)

def adam_step(weight, gradient, first, second, rate, decay):
    first_new = BETA_ONE * first + (1.0 - BETA_ONE) * gradient
    second_new = BETA_TWO * second + (1.0 - BETA_TWO) * gradient * gradient
    stepped = first_new / (1.0 - BETA_ONE ** STEP) / (jnp.sqrt(second_new / (1.0 - BETA_TWO ** STEP)) + ADAM_EPS)
    return (weight - rate * (stepped + decay * weight), first_new, second_new)

def reference(item_ids, targets, lengths, correction, item_row, item_table, qkv_weight, out_weight, up_weight, down_weight, positions, gains, item_table_first, qkv_weight_first, out_weight_first, up_weight_first, down_weight_first, positions_first, gains_first, item_table_second, qkv_weight_second, out_weight_second, up_weight_second, down_weight_second, positions_second, gains_second):
    group_hist = ROW_COUNT * SEQ_DEV
    count_groups = MB * DP_COUNT
    pieces = (item_ids.reshape(count_groups, group_hist, L), targets.reshape(count_groups, group_hist, L), lengths.reshape(count_groups, group_hist), correction.reshape(count_groups, group_hist, L))
    weights = (item_table, qkv_weight, out_weight, up_weight, down_weight, positions, gains)

    def forward(params):
        lowered = (low(params[0]), low(params[1]), low(params[2]), low(params[3]), low(params[4]), params[5], params[6])

        def one_group(running, group_pieces):
            return (running + group_loss(lowered, item_row, group_pieces), None)
        total, unused = lax.scan(jax.checkpoint(one_group), jnp.zeros((), jnp.float32), pieces)
        return total
    loss_sum, pull_back = jax.vjp(forward, weights)
    gradients = pull_back(jnp.ones((), jnp.float32))[0]
    valid_count = jnp.sum((jnp.arange(L, dtype=jnp.int32)[None, None, :] < lengths[:, :, None]).astype(jnp.float32))
    square_total = jnp.zeros((), jnp.float32)
    for gradient in gradients:
        square_total = square_total + jnp.sum(gradient * gradient)
    grad_norm = jnp.sqrt(square_total)
    factor = CLIP / jnp.maximum(grad_norm, CLIP)
    firsts = (item_table_first, qkv_weight_first, out_weight_first, up_weight_first, down_weight_first, positions_first, gains_first)
    seconds = (item_table_second, qkv_weight_second, out_weight_second, up_weight_second, down_weight_second, positions_second, gains_second)
    rates = (RATE, RATE, RATE, RATE, RATE, RATE, GAIN_RATE)
    decays = (DECAY, DECAY, DECAY, DECAY, DECAY, DECAY, 0.0)
    updated = [adam_step(weights[which_one], factor * gradients[which_one], firsts[which_one], seconds[which_one], rates[which_one], decays[which_one]) for which_one in range(7)]
    return (updated[0][0], updated[1][0], updated[2][0], updated[3][0], updated[4][0], updated[5][0], updated[6][0], updated[0][1], updated[1][1], updated[2][1], updated[3][1], updated[4][1], updated[5][1], updated[6][1], updated[0][2], updated[1][2], updated[2][2], updated[3][2], updated[4][2], updated[5][2], updated[6][2], loss_sum, valid_count, grad_norm)
```

```python
import functools
import math

import jax
import jax.numpy as jnp
from jax import lax
from jax.experimental import pallas as pl
from jax.experimental.pallas import tpu as pltpu
from jax.sharding import PartitionSpec as P

MESH = pl.DeviceIdType.MESH
VMEM = pl.BlockSpec(memory_space=pltpu.VMEM)
HEADS = 8
STEP = 10


NORM_EPS = 1e-06
MASKED = -1e30
BETA_ONE = 0.9
BETA_TWO = 0.999
ADAM_EPS = 1e-08
DECAY = 0.01
RATE = 0.1
GAIN_RATE = 1.0
CLIP = 1.0


def rounded(values):
    return values.astype(jnp.bfloat16)


def matmul(first_op, second_op):
    return jnp.dot(first_op, second_op, preferred_element_type=jnp.float32)


def inner_rows(first_op, second_op):
    return lax.dot_general(
        first_op, second_op, (((0,), (0,)), ((), ())), preferred_element_type=jnp.float32
    )


def inner_cols(first_op, second_op):
    return lax.dot_general(
        first_op, second_op, (((1,), (1,)), ((), ())), preferred_element_type=jnp.float32
    )


def rms_norm(values, gain_row):
    return (
        values * lax.rsqrt(jnp.mean(values * values, axis=-1, keepdims=True) + NORM_EPS) * gain_row
    )


def gelu_tanh(values):
    return jax.nn.gelu(values)


def split_heads(joined, histories, head_count):
    pieces = joined.reshape(histories, joined.shape[0] // histories, 3, head_count, -1)
    return (pieces[:, :, 0], pieces[:, :, 1], pieces[:, :, 2])


def masked_scores(queries, key_rows, lengths_here):
    length = queries.shape[1]
    scaling = queries.shape[-1] ** (-0.5)
    scores = (
        jnp.einsum("sqhe,skhe->shqk", queries, key_rows, preferred_element_type=jnp.float32)
        * scaling
    )
    position = jnp.arange(length, dtype=jnp.int32)
    allowed = (position[None, :] <= position[:, None])[None, None] & (
        position[None, None, None, :] < lengths_here[:, None, None, None]
    )
    return jnp.where(allowed, scores, MASKED)


def attention_forward(joined, lengths_here, head_count):
    queries, key_rows, value_rows = split_heads(joined, lengths_here.shape[0], head_count)
    scores = masked_scores(queries, key_rows, lengths_here)
    highest = jnp.max(scores, axis=-1, keepdims=True)
    log_total = highest + jnp.log(jnp.sum(jnp.exp(scores - highest), axis=-1, keepdims=True))
    probabilities = rounded(jnp.exp(scores - log_total))
    attended = jnp.einsum(
        "shqk,skhe->sqhe", probabilities, value_rows, preferred_element_type=jnp.float32
    )
    return (attended.reshape(joined.shape[0], -1), log_total)


def attention_backward(joined, log_total, lengths_here, grad_attended, head_count):
    queries, key_rows, value_rows = split_heads(joined, lengths_here.shape[0], head_count)
    probabilities = jnp.exp(masked_scores(queries, key_rows, lengths_here) - log_total)
    grad_heads = grad_attended.reshape(queries.shape)
    grad_probs = jnp.einsum(
        "sqhe,skhe->shqk", grad_heads, value_rows, preferred_element_type=jnp.float32
    )
    grad_values = jnp.einsum(
        "shqk,sqhe->skhe", rounded(probabilities), grad_heads, preferred_element_type=jnp.float32
    )
    row_inner = jnp.sum(probabilities * grad_probs, axis=-1, keepdims=True)
    grad_scores = rounded(probabilities * (grad_probs - row_inner))
    scaling = queries.shape[-1] ** (-0.5)
    grad_queries = (
        jnp.einsum("shqk,skhe->sqhe", grad_scores, key_rows, preferred_element_type=jnp.float32)
        * scaling
    )
    grad_keys = (
        jnp.einsum("shqk,sqhe->skhe", grad_scores, queries, preferred_element_type=jnp.float32)
        * scaling
    )
    stacked = jnp.stack([grad_queries, grad_keys, grad_values], axis=2)
    return stacked.reshape(joined.shape[0], -1)


def layer_forward(embedded, lengths_here, matrices, gains, head_count):
    qkv_low, out_low, up_low, down_low = matrices
    normed_one, back_one = jax.vjp(rms_norm, embedded, gains[0])
    hidden_one = rounded(normed_one)
    joined = rounded(matmul(hidden_one, qkv_low))
    attended, log_total = attention_forward(joined, lengths_here, head_count)
    attended_low = rounded(attended)
    middle = embedded + matmul(attended_low, out_low)
    normed_two, back_two = jax.vjp(rms_norm, middle, gains[1])
    hidden_two = rounded(normed_two)
    upward = matmul(hidden_two, up_low)
    active, back_active = jax.vjp(gelu_tanh, upward)
    active_low = rounded(active)
    output = middle + matmul(active_low, down_low)
    return (
        output,
        (
            back_one,
            hidden_one,
            joined,
            log_total,
            attended_low,
            back_two,
            hidden_two,
            back_active,
            active_low,
        ),
    )


def layer_backward(grad_output, saved_state, lengths_here, matrices, head_count):
    (
        back_one,
        hidden_one,
        joined,
        log_total,
        attended_low,
        back_two,
        hidden_two,
        back_active,
        active_low,
    ) = saved_state
    qkv_low, out_low, up_low, down_low = matrices
    grad_branch = rounded(grad_output)
    grad_down = inner_rows(active_low, grad_branch)
    grad_upward = rounded(back_active(inner_cols(grad_branch, down_low))[0])
    grad_up = inner_rows(hidden_two, grad_upward)
    grad_middle, gain_two = back_two(inner_cols(grad_upward, up_low))
    grad_middle = grad_middle + grad_output
    grad_attn = rounded(grad_middle)
    grad_out = inner_rows(attended_low, grad_attn)
    grad_attended = rounded(inner_cols(grad_attn, out_low))
    grad_joined = rounded(
        attention_backward(joined, log_total, lengths_here, grad_attended, head_count)
    )
    grad_qkv = inner_rows(hidden_one, grad_joined)
    grad_embedded, gain_one = back_one(inner_cols(grad_joined, qkv_low))
    return (
        grad_embedded + grad_middle,
        (grad_qkv, grad_out, grad_up, grad_down),
        (gain_one, gain_two),
    )


def candidate_loss(query_low, candidates, cand_bias, valid_here, offset):
    tokens, width = query_low.shape
    block_rows = min(512, tokens)
    blocks = tokens // block_rows
    column = jnp.arange(candidates.shape[0], dtype=jnp.int32)
    bias_wide = cand_bias.astype(jnp.float32)

    def one_block(running, block_pieces):
        query_block, valid_block, start_row = block_pieces
        logits = inner_cols(query_block, candidates) + bias_wide[None]
        highest = jnp.max(logits, axis=1, keepdims=True)
        log_total = highest + jnp.log(jnp.sum(jnp.exp(logits - highest), axis=1, keepdims=True))
        target_hit = (
            column[None, :]
            == (offset + start_row + jnp.arange(block_rows, dtype=jnp.int32))[:, None]
        )
        own_logit = jnp.sum(jnp.where(target_hit, logits, 0.0), axis=1)
        grad_logits = rounded(
            (jnp.exp(logits - log_total) - target_hit.astype(jnp.float32)) * valid_block[:, None]
        )
        return (
            running + jnp.sum(valid_block * (log_total[:, 0] - own_logit)),
            (grad_logits, log_total[:, 0]),
        )

    loss_part, block_out = lax.scan(
        one_block,
        jnp.zeros((), jnp.float32),
        (
            query_low.reshape(blocks, block_rows, width),
            valid_here.reshape(blocks, block_rows),
            jnp.arange(blocks, dtype=jnp.int32) * block_rows,
        ),
    )
    return (loss_part, block_out[0].reshape(tokens, -1), block_out[1].reshape(tokens))


def send_requests(asked_rows):
    moved = lax.all_to_all(asked_rows, ("dp", "rows"), split_axis=0, concat_axis=0, tiled=True)
    return moved


def send_replies(found_rows):
    moved = lax.all_to_all(found_rows, ("dp", "rows"), split_axis=0, concat_axis=0, tiled=True)
    return moved


def send_grads(row_terms):
    moved = lax.all_to_all(row_terms, ("dp", "rows"), split_axis=0, concat_axis=0, tiled=True)
    return moved


def adam_step(weight, gradient, first, second, rate, decay):
    first_new = BETA_ONE * first + (1.0 - BETA_ONE) * gradient
    second_new = BETA_TWO * second + (1.0 - BETA_TWO) * gradient * gradient
    stepped = (
        first_new
        / (1.0 - BETA_ONE**STEP)
        / (jnp.sqrt(second_new / (1.0 - BETA_TWO**STEP)) + ADAM_EPS)
    )
    return (weight - rate * (stepped + decay * weight), first_new, second_new)


def reduce_rows(total_rows, devices):
    unit = 16 * devices
    return -(-total_rows // unit) * unit


def tail_kernel(dp_count, row_count, padded, capacity, qkv, out, up, down, pos, outgoing, incoming, gathered, square,
                acc, low, recv0, recv1, recv2, send_a, recv_a, send_r, recv_r):
    devices = dp_count * row_count
    dp = lax.axis_index("dp")
    row = lax.axis_index("rows")
    me = dp * row_count + row
    bits = row_count.bit_length() - 1
    barrier = pltpu.get_barrier_semaphore()

    def place(k):
        other = lax.rem(me + k, devices)
        return other, (other // row_count, lax.rem(other, row_count))

    def greet(k, carry):
        other, where = place(k)
        pl.semaphore_signal(barrier, inc=1, device_id=where, device_id_type=MESH)
        return carry

    lax.fori_loop(1, devices, greet, 0)
    width = 256
    at = 0
    for ref in (qkv, up):
        for c in range(ref.shape[1] // width):
            acc[pl.ds(at, ref.shape[0]), :] = ref[:, pl.ds(c * width, width)]
            at += ref.shape[0]
    for ref in (out, down, pos):
        acc[pl.ds(at, ref.shape[0]), :] = ref[...]
        at += ref.shape[0]
    if at < padded:
        acc[pl.ds(at, padded - at), :] = jnp.zeros((padded - at, width), jnp.float32)
    pl.semaphore_wait(barrier, devices - 1)

    def a2a_send(k):
        other, where = place(k)
        return pltpu.make_async_remote_copy(
            outgoing.at[other], incoming.at[me], send_a.at[k], recv_a.at[me], device_id=where, device_id_type=MESH)

    def a2a_recv(k):
        other, where = place(k)
        return pltpu.make_async_remote_copy(
            outgoing.at[other], incoming.at[other], send_a.at[k], recv_a.at[other], device_id=where, device_id_type=MESH)

    def partner(bit):
        step = 1 << bit
        mine = lax.rem(row // step, 2)
        return mine, (dp, row + step - 2 * step * mine)

    half = padded // 2
    units = padded // (16 * devices)
    part_rows = [((units + 1) // 2) * 16 * (devices // 2), (units // 2) * 16 * (devices // 2)]
    orders = [list(range(1, bits)), list(range(bits - 1, 0, -1))]
    al = lambda v: pl.multiple_of(v, 16)

    mine, where = partner(0)
    low[pl.ds(al((1 - mine) * half), half), :] = acc[pl.ds(al((1 - mine) * half), half), :].astype(jnp.bfloat16)
    first = pltpu.make_async_remote_copy(low.at[pl.ds(al((1 - mine) * half), half)], recv0, send_r.at[0], recv_r.at[0],
                                         device_id=where, device_id_type=MESH)
    first.start()
    lax.fori_loop(1, devices, lambda k, c: (a2a_send(k).start(), c)[1], 0)
    incoming[me] = outgoing[me]
    first.wait_recv()
    base = mine * half
    pending = [first]
    starts = [base, base + part_rows[0]]
    sizes = list(part_rows)
    offs = [0, sizes[0]]
    live = [p for p in range(2) if part_rows[p] > 0]
    acc[pl.ds(al(base), half), :] = acc[pl.ds(al(base), half), :] + recv0[...].astype(jnp.float32)
    sem = 1
    scratch_at = 0
    history = []
    for step in range(bits - 1):
        copies = []
        for p in live:
            bit = orders[p][step]
            mine, where = partner(bit)
            size = sizes[p] // 2
            keep = starts[p] + mine * size
            give = starts[p] + (1 - mine) * size
            low[pl.ds(al(give), size), :] = acc[pl.ds(al(give), size), :].astype(jnp.bfloat16)
            landing = recv1.at[pl.ds(scratch_at, size)]
            copy = pltpu.make_async_remote_copy(low.at[pl.ds(al(give), size)], landing, send_r.at[sem], recv_r.at[sem],
                                                device_id=where, device_id_type=MESH)
            copy.start()
            copies.append((p, copy, keep, size, scratch_at, where))
            sem += 1
            scratch_at += size
        for p, copy, keep, size, off, where in copies:
            copy.wait_recv()
            acc[pl.ds(al(keep), size), :] = acc[pl.ds(al(keep), size), :] + recv1[pl.ds(off, size), :].astype(jnp.float32)
            history.append((p, keep, size, where))
            starts[p], sizes[p] = keep, size
            pending.append(copy)
    copies = []
    off = 0
    final = {}
    for p in live:
        size = sizes[p] // dp_count
        for k in range(1, dp_count):
            other = lax.rem(dp + k, dp_count)
            give = starts[p] + other * size
            low[pl.ds(al(give), size), :] = acc[pl.ds(al(give), size), :].astype(jnp.bfloat16)
            copy = pltpu.make_async_remote_copy(low.at[pl.ds(al(give), size)], recv2.at[pl.ds(off, size)], send_r.at[sem], recv_r.at[sem],
                                                device_id=(other, row), device_id_type=MESH)
            copy.start()
            copies.append((p, copy, off, size))
            sem += 1
            off += size
        final[p] = (starts[p] + dp * size, size)
    for p, copy, off, size in copies:
        copy.wait_recv()
        at, size = final[p]
        acc[pl.ds(al(at), size), :] = acc[pl.ds(al(at), size), :] + recv2[pl.ds(off, size), :].astype(jnp.float32)
        pending.append(copy)
    total = jnp.zeros((1, width), jnp.float32)
    for p in live:
        at, size = final[p]
        mine_low = acc[pl.ds(al(at), size), :]
        total = total + jnp.sum(mine_low * mine_low, axis=0, keepdims=True)
        gathered[pl.ds(al(at), size), :] = mine_low.astype(jnp.bfloat16)
    square[...] = jnp.broadcast_to(total, square.shape)

    copies = []
    for p in live:
        at, size = final[p]
        for k in range(1, dp_count):
            other = lax.rem(dp + k, dp_count)
            copy = pltpu.make_async_remote_copy(gathered.at[pl.ds(al(at), size)], gathered.at[pl.ds(al(at), size)], send_r.at[sem], recv_r.at[sem],
                                                device_id=(other, row), device_id_type=MESH)
            copy.start()
            copies.append((p, copy, k, sem))
            sem += 1
    for p, copy, k, s in copies:
        at, size = final[p]
        source = lax.rem(dp + dp_count - k, dp_count)
        land = starts[p] + source * size
        pltpu.make_async_remote_copy(gathered.at[pl.ds(al(at), size)], gathered.at[pl.ds(al(land), size)], send_r.at[s], recv_r.at[s],
                                     device_id=(source, row), device_id_type=MESH).wait_recv()
        pending.append(copy)
    for step in range(bits - 2, -1, -1):
        copies = []
        for p in live:
            bit = orders[p][step]
            mine, where = partner(bit)
            size = sizes[p]
            at = starts[p]
            copy = pltpu.make_async_remote_copy(gathered.at[pl.ds(al(at), size)], gathered.at[pl.ds(al(at), size)], send_r.at[sem], recv_r.at[sem],
                                                device_id=where, device_id_type=MESH)
            copy.start()
            copies.append((p, copy, sem, mine, size, where))
            sem += 1
        for p, copy, s, mine, size, where in copies:
            bottom = starts[p] - mine * size
            land = bottom + (1 - mine) * size
            pltpu.make_async_remote_copy(gathered.at[pl.ds(al(land), size)], gathered.at[pl.ds(al(land), size)], send_r.at[s], recv_r.at[s],
                                         device_id=where, device_id_type=MESH).wait_recv()
            starts[p], sizes[p] = bottom, 2 * size
            pending.append(copy)
    mine, where = partner(0)
    last = pltpu.make_async_remote_copy(gathered.at[pl.ds(al(mine * half), half)], gathered.at[pl.ds(al(mine * half), half)], send_r.at[sem], recv_r.at[sem],
                                        device_id=where, device_id_type=MESH)
    last.start()
    pltpu.make_async_remote_copy(gathered.at[pl.ds(al((1 - mine) * half), half)], gathered.at[pl.ds(al((1 - mine) * half), half)], send_r.at[sem], recv_r.at[sem],
                                 device_id=where, device_id_type=MESH).wait_recv()
    sem += 1
    pending.append(last)
    lax.fori_loop(1, devices, lambda k, c: (a2a_recv(k).wait_recv(), c)[1], 0)
    for copy in pending:
        copy.wait_send()
    lax.fori_loop(1, devices, lambda k, c: (a2a_send(k).wait_send(), c)[1], 0)


def tail_exchange(dp_count, row_count, qkv, out, up, down, pos, outgoing):
    devices = dp_count * row_count
    capacity = outgoing.shape[1]
    width = out.shape[1]
    rows = sum(a.size for a in (qkv, out, up, down, pos)) // width
    padded = reduce_rows(rows, devices)
    bits = row_count.bit_length() - 1
    sems = 2 + 4 * bits + 4 * dp_count + 8
    return pl.pallas_call(
        functools.partial(tail_kernel, dp_count, row_count, padded, capacity),
        out_shape=(jax.ShapeDtypeStruct(outgoing.shape, jnp.bfloat16), jax.ShapeDtypeStruct((padded, width), jnp.bfloat16),
                   jax.ShapeDtypeStruct((8, width), jnp.float32)),
        in_specs=[VMEM] * 6, out_specs=(VMEM,) * 3,
        scratch_shapes=[
            pltpu.VMEM((padded, width), jnp.float32),
            pltpu.VMEM((padded, width), jnp.bfloat16),
            pltpu.VMEM((padded // 2, width), jnp.bfloat16),
            pltpu.VMEM((padded // 2, width), jnp.bfloat16),
            pltpu.VMEM((padded // row_count, width), jnp.bfloat16),
            pltpu.SemaphoreType.DMA((devices,)), pltpu.SemaphoreType.DMA((devices,)),
            pltpu.SemaphoreType.DMA((sems,)), pltpu.SemaphoreType.DMA((sems,)),
        ],
        name="tail_exchange",
        compiler_params=pltpu.CompilerParams(collective_id=3, has_side_effects=True, vmem_limit_bytes=56 * 2**20),
    )(qkv, out, up, down, pos, outgoing)


def small_kernel(dp_count, row_count, part, summed, by_row, by_dp, send_sem, recv_sem):
    dp = lax.axis_index("dp")
    row = lax.axis_index("rows")
    barrier = pltpu.get_barrier_semaphore()
    row_places = [lax.rem(row + k, row_count) for k in range(1, row_count)]
    dp_places = [lax.rem(dp + k, dp_count) for k in range(1, dp_count)]
    for other in row_places:
        pl.semaphore_signal(barrier, inc=1, device_id=(dp, other), device_id_type=MESH)
    for other in dp_places:
        pl.semaphore_signal(barrier, inc=1, device_id=(other, row), device_id_type=MESH)
    pl.semaphore_wait(barrier, row_count + dp_count - 2)

    def spread(source, landing, mine, others, where, base):
        sends = []
        for k, other in enumerate(others):
            copy = pltpu.make_async_remote_copy(
                source, landing.at[mine], send_sem.at[base + k], recv_sem.at[base + mine],
                device_id=where(other), device_id_type=MESH,
            )
            copy.start()
            sends.append(copy)
        landing[mine] = source[...]
        for other in others:
            pltpu.make_async_remote_copy(
                source, landing.at[other], send_sem.at[base], recv_sem.at[base + other],
                device_id=where(other), device_id_type=MESH,
            ).wait_recv()
        for copy in sends:
            copy.wait_send()

    spread(part, by_row, row, row_places, lambda other: (dp, other), 0)
    summed[...] = jnp.sum(by_row[...], axis=0)
    spread(summed, by_dp, dp, dp_places, lambda other: (other, row), row_count)
    summed[...] = jnp.sum(by_dp[...], axis=0)


def small_sum(dp_count, row_count, part):
    return pl.pallas_call(
        functools.partial(small_kernel, dp_count, row_count),
        out_shape=jax.ShapeDtypeStruct(part.shape, part.dtype),
        in_specs=[VMEM],
        out_specs=VMEM,
        scratch_shapes=[
            pltpu.VMEM((row_count,) + part.shape, part.dtype),
            pltpu.VMEM((dp_count,) + part.shape, part.dtype),
            pltpu.SemaphoreType.DMA((row_count + dp_count,)),
            pltpu.SemaphoreType.DMA((row_count + dp_count,)),
        ],
        name="small_sum",
        compiler_params=pltpu.CompilerParams(collective_id=4, has_side_effects=True),
    )(part)


def local(
    item_ids,
    targets,
    lengths,
    correction,
    item_row,
    item_table,
    qkv_weight,
    out_weight,
    up_weight,
    down_weight,
    positions,
    gains,
    item_table_first,
    qkv_weight_first,
    out_weight_first,
    up_weight_first,
    down_weight_first,
    positions_first,
    gains_first,
    item_table_second,
    qkv_weight_second,
    out_weight_second,
    up_weight_second,
    down_weight_second,
    positions_second,
    gains_second,
):
    micro, histories, length = item_ids.shape
    rows_here, width = item_table.shape
    devices = lax.axis_size("dp") * lax.axis_size("rows")
    tokens = histories * length
    requests = 2 * micro * tokens
    capacity = 3 * (requests + devices) // (2 * devices) + 1
    capacity = -(-capacity // 16) * 16
    dp_count, row_count = lax.axis_size("dp"), lax.axis_size("rows")
    position = jnp.arange(length, dtype=jnp.int32)
    valid_pos = (position[None, None, :] < lengths[:, :, None]).reshape(micro, tokens)
    wanted = jnp.stack([item_ids, targets]).reshape(requests)
    live_request = jnp.concatenate([valid_pos.reshape(-1), valid_pos.reshape(-1)])
    table_rows = item_row[wanted]
    owner_of = table_rows // rows_here
    choose = (
        (owner_of[:, None] == jnp.arange(devices, dtype=jnp.int32)[None, :]) & live_request[:, None]
    ).astype(jnp.int32)
    earlier = jnp.sum((jnp.cumsum(choose, axis=0) - choose) * choose, axis=1)
    slot_of = jnp.where(live_request, owner_of * capacity + earlier, devices * capacity)
    asked_rows = (
        jnp.zeros((devices * capacity,), jnp.int32)
        .at[slot_of]
        .set(table_rows % rows_here, mode="drop")
    )
    received = send_requests(asked_rows.reshape(devices, capacity))
    replies = send_replies(rounded(item_table)[received]).reshape(devices * capacity, width)
    fetched = jnp.where(
        live_request[:, None],
        replies[jnp.minimum(slot_of, devices * capacity - 1)],
        jnp.zeros((), jnp.bfloat16),
    )
    fetched = fetched.reshape(2, micro, tokens, width)
    matrices = (rounded(qkv_weight), rounded(out_weight), rounded(up_weight), rounded(down_weight))
    scaling = math.sqrt(width)
    offset = lax.axis_index("rows") * tokens
    running = [
        jnp.zeros_like(qkv_weight),
        jnp.zeros_like(out_weight),
        jnp.zeros_like(up_weight),
        jnp.zeros_like(down_weight),
    ]
    grad_positions = jnp.zeros_like(positions)
    grad_gains = jnp.zeros_like(gains)
    loss_local = jnp.zeros((), jnp.float32)
    embed_grads = []
    target_grads = []
    for micro_index in range(micro):
        lengths_here = lengths[micro_index]
        valid_here = valid_pos[micro_index].astype(jnp.float32)
        embedded = scaling * fetched[0, micro_index].astype(jnp.float32) + jnp.tile(
            positions, (histories, 1)
        )
        output, saved_state = layer_forward(embedded, lengths_here, matrices, gains, HEADS)
        normed_three, back_three = jax.vjp(rms_norm, output, gains[2])
        query_low = rounded(normed_three)
        bias_low = jnp.where(
            valid_pos[micro_index],
            rounded(-correction[micro_index].reshape(-1)),
            jnp.asarray(MASKED, jnp.bfloat16),
        )
        candidates, cand_bias = (
            lax.all_gather(fetched[1, micro_index], "rows", axis=0, tiled=True),
            lax.all_gather(bias_low, "rows", axis=0, tiled=True),
        )
        loss_part, grad_logits, log_total = candidate_loss(
            query_low, candidates, cand_bias, valid_here, offset
        )
        loss_local = loss_local + loss_part
        grad_output, gain_three = back_three(matmul(grad_logits, candidates))
        target_grads.append(
            lax.psum_scatter(
                inner_rows(grad_logits, query_low).astype(jnp.bfloat16),
                "rows",
                scatter_dimension=0,
                tiled=True,
            ).astype(jnp.float32)
        )
        grad_embedded, grad_layer, gain_pair = layer_backward(
            grad_output, saved_state, lengths_here, matrices, HEADS
        )
        for which_one in range(4):
            running[which_one] = running[which_one] + grad_layer[which_one]
        grad_positions = grad_positions + jnp.sum(
            grad_embedded.reshape(histories, length, width), axis=0
        )
        grad_gains = grad_gains + jnp.stack([gain_pair[0], gain_pair[1], gain_three])
        embed_grads.append(scaling * grad_embedded)
    target_part = jnp.stack(target_grads)
    row_grads = jnp.concatenate([jnp.stack(embed_grads), target_part]).reshape(requests, width)
    outgoing = (
        jnp.zeros((devices * capacity, width), jnp.bfloat16)
        .at[slot_of]
        .set(rounded(row_grads), mode="drop")
    )
    incoming, gathered, square = tail_exchange(
        dp_count,
        row_count,
        running[0],
        running[1],
        running[2],
        running[3],
        grad_positions,
        outgoing.reshape(devices, capacity, width),
    )
    table_grad = (
        jnp.zeros((rows_here, width), jnp.float32)
        .at[received.reshape(-1)]
        .add(incoming.reshape(-1, width).astype(jnp.float32))
    )
    own_square = jnp.sum(table_grad * table_grad) + jnp.sum(square[0])
    scalars = jnp.stack([loss_local, jnp.sum(valid_pos.astype(jnp.float32)), own_square])
    part = jnp.concatenate(
        [grad_gains.reshape(-1), jnp.pad(scalars, (0, 1024 - grad_gains.size - 3))]
    ).reshape(8, 128)
    small = small_sum(dp_count, row_count, part).reshape(-1)
    sum_gains = small[: grad_gains.size].reshape(grad_gains.shape)
    sum_loss, sum_count, square_total = (small[grad_gains.size + k] for k in range(3))
    gathered = gathered.astype(jnp.float32)
    place = 0
    blocks = []
    for like in (qkv_weight, up_weight):
        count = like.shape[1] // width
        piece = gathered[place : place + count * like.shape[0]]
        blocks.append(
            jnp.concatenate(
                [piece[c * like.shape[0] : (c + 1) * like.shape[0]] for c in range(count)], axis=1
            )
        )
        place += count * like.shape[0]
    for like in (out_weight, down_weight, positions):
        blocks.append(gathered[place : place + like.shape[0]])
        place += like.shape[0]
    gradients = (table_grad, blocks[0], blocks[2], blocks[1], blocks[3], blocks[4], sum_gains)
    grad_norm = jnp.sqrt(square_total + jnp.sum(sum_gains * sum_gains))
    factor = CLIP / jnp.maximum(grad_norm, CLIP)
    weights = (item_table, qkv_weight, out_weight, up_weight, down_weight, positions, gains)
    firsts = (
        item_table_first,
        qkv_weight_first,
        out_weight_first,
        up_weight_first,
        down_weight_first,
        positions_first,
        gains_first,
    )
    seconds = (
        item_table_second,
        qkv_weight_second,
        out_weight_second,
        up_weight_second,
        down_weight_second,
        positions_second,
        gains_second,
    )
    rates = (RATE, RATE, RATE, RATE, RATE, RATE, GAIN_RATE)
    decays = (DECAY, DECAY, DECAY, DECAY, DECAY, DECAY, 0.0)
    updated = [
        adam_step(
            weights[which_one],
            factor * gradients[which_one],
            firsts[which_one],
            seconds[which_one],
            rates[which_one],
            decays[which_one],
        )
        for which_one in range(7)
    ]
    return (
        updated[0][0],
        updated[1][0],
        updated[2][0],
        updated[3][0],
        updated[4][0],
        updated[5][0],
        updated[6][0],
        updated[0][1],
        updated[1][1],
        updated[2][1],
        updated[3][1],
        updated[4][1],
        updated[5][1],
        updated[6][1],
        updated[0][2],
        updated[1][2],
        updated[2][2],
        updated[3][2],
        updated[4][2],
        updated[5][2],
        updated[6][2],
        sum_loss,
        sum_count,
        grad_norm,
    )


def solution(mesh):
    placed = (
        P(None, ("dp", "rows"), None),
        P(None, ("dp", "rows"), None),
        P(None, ("dp", "rows")),
        P(None, ("dp", "rows"), None),
        P(),
        P(("dp", "rows"), None),
        P(),
        P(),
        P(),
        P(),
        P(),
        P(),
        P(("dp", "rows"), None),
        P(),
        P(),
        P(),
        P(),
        P(),
        P(),
        P(("dp", "rows"), None),
        P(),
        P(),
        P(),
        P(),
        P(),
        P(),
    )
    return jax.shard_map(
        local,
        mesh=mesh,
        in_specs=placed,
        out_specs=(
            P(("dp", "rows"), None),
            P(),
            P(),
            P(),
            P(),
            P(),
            P(),
            P(("dp", "rows"), None),
            P(),
            P(),
            P(),
            P(),
            P(),
            P(),
            P(("dp", "rows"), None),
            P(),
            P(),
            P(),
            P(),
            P(),
            P(),
            P(),
            P(),
            P(),
        ),
        check_vma=False,
    )
```

```python
import functools
import math

import jax
import jax.numpy as jnp
from jax import lax
from jax.experimental import pallas as pl
from jax.experimental.pallas import tpu as pltpu
from jax.sharding import PartitionSpec as P

MESH = pl.DeviceIdType.MESH
VMEM = pl.BlockSpec(memory_space=pltpu.VMEM)
HEADS = 8
STEP = 10


NORM_EPS = 1e-06
MASKED = -1e30
BETA_ONE = 0.9
BETA_TWO = 0.999
ADAM_EPS = 1e-08
DECAY = 0.01
RATE = 0.1
GAIN_RATE = 1.0
CLIP = 1.0


def rounded(values):
    return values.astype(jnp.bfloat16)


def matmul(first_op, second_op):
    return jnp.dot(first_op, second_op, preferred_element_type=jnp.float32)


def inner_rows(first_op, second_op):
    return lax.dot_general(
        first_op, second_op, (((0,), (0,)), ((), ())), preferred_element_type=jnp.float32
    )


def inner_cols(first_op, second_op):
    return lax.dot_general(
        first_op, second_op, (((1,), (1,)), ((), ())), preferred_element_type=jnp.float32
    )


def rms_norm(values, gain_row):
    return (
        values * lax.rsqrt(jnp.mean(values * values, axis=-1, keepdims=True) + NORM_EPS) * gain_row
    )


def gelu_tanh(values):
    return jax.nn.gelu(values)


def split_heads(joined, histories, head_count):
    pieces = joined.reshape(histories, joined.shape[0] // histories, 3, head_count, -1)
    return (pieces[:, :, 0], pieces[:, :, 1], pieces[:, :, 2])


def masked_scores(queries, key_rows, lengths_here):
    length = queries.shape[1]
    scaling = queries.shape[-1] ** (-0.5)
    scores = (
        jnp.einsum("sqhe,skhe->shqk", queries, key_rows, preferred_element_type=jnp.float32)
        * scaling
    )
    position = jnp.arange(length, dtype=jnp.int32)
    allowed = (position[None, :] <= position[:, None])[None, None] & (
        position[None, None, None, :] < lengths_here[:, None, None, None]
    )
    return jnp.where(allowed, scores, MASKED)


def attention_forward(joined, lengths_here, head_count):
    queries, key_rows, value_rows = split_heads(joined, lengths_here.shape[0], head_count)
    scores = masked_scores(queries, key_rows, lengths_here)
    highest = jnp.max(scores, axis=-1, keepdims=True)
    log_total = highest + jnp.log(jnp.sum(jnp.exp(scores - highest), axis=-1, keepdims=True))
    probabilities = rounded(jnp.exp(scores - log_total))
    attended = jnp.einsum(
        "shqk,skhe->sqhe", probabilities, value_rows, preferred_element_type=jnp.float32
    )
    return (attended.reshape(joined.shape[0], -1), log_total)


def attention_backward(joined, log_total, lengths_here, grad_attended, head_count):
    queries, key_rows, value_rows = split_heads(joined, lengths_here.shape[0], head_count)
    probabilities = jnp.exp(masked_scores(queries, key_rows, lengths_here) - log_total)
    grad_heads = grad_attended.reshape(queries.shape)
    grad_probs = jnp.einsum(
        "sqhe,skhe->shqk", grad_heads, value_rows, preferred_element_type=jnp.float32
    )
    grad_values = jnp.einsum(
        "shqk,sqhe->skhe", rounded(probabilities), grad_heads, preferred_element_type=jnp.float32
    )
    row_inner = jnp.sum(probabilities * grad_probs, axis=-1, keepdims=True)
    grad_scores = rounded(probabilities * (grad_probs - row_inner))
    scaling = queries.shape[-1] ** (-0.5)
    grad_queries = (
        jnp.einsum("shqk,skhe->sqhe", grad_scores, key_rows, preferred_element_type=jnp.float32)
        * scaling
    )
    grad_keys = (
        jnp.einsum("shqk,sqhe->skhe", grad_scores, queries, preferred_element_type=jnp.float32)
        * scaling
    )
    stacked = jnp.stack([grad_queries, grad_keys, grad_values], axis=2)
    return stacked.reshape(joined.shape[0], -1)


def layer_forward(embedded, lengths_here, matrices, gains, head_count):
    qkv_low, out_low, up_low, down_low = matrices
    normed_one, back_one = jax.vjp(rms_norm, embedded, gains[0])
    hidden_one = rounded(normed_one)
    joined = rounded(matmul(hidden_one, qkv_low))
    attended, log_total = attention_forward(joined, lengths_here, head_count)
    attended_low = rounded(attended)
    middle = embedded + matmul(attended_low, out_low)
    normed_two, back_two = jax.vjp(rms_norm, middle, gains[1])
    hidden_two = rounded(normed_two)
    upward = matmul(hidden_two, up_low)
    active, back_active = jax.vjp(gelu_tanh, upward)
    active_low = rounded(active)
    output = middle + matmul(active_low, down_low)
    return (
        output,
        (
            back_one,
            hidden_one,
            joined,
            log_total,
            attended_low,
            back_two,
            hidden_two,
            back_active,
            active_low,
        ),
    )


def layer_backward(grad_output, saved_state, lengths_here, matrices, head_count):
    (
        back_one,
        hidden_one,
        joined,
        log_total,
        attended_low,
        back_two,
        hidden_two,
        back_active,
        active_low,
    ) = saved_state
    qkv_low, out_low, up_low, down_low = matrices
    grad_branch = rounded(grad_output)
    grad_down = inner_rows(active_low, grad_branch)
    grad_upward = rounded(back_active(inner_cols(grad_branch, down_low))[0])
    grad_up = inner_rows(hidden_two, grad_upward)
    grad_middle, gain_two = back_two(inner_cols(grad_upward, up_low))
    grad_middle = grad_middle + grad_output
    grad_attn = rounded(grad_middle)
    grad_out = inner_rows(attended_low, grad_attn)
    grad_attended = rounded(inner_cols(grad_attn, out_low))
    grad_joined = rounded(
        attention_backward(joined, log_total, lengths_here, grad_attended, head_count)
    )
    grad_qkv = inner_rows(hidden_one, grad_joined)
    grad_embedded, gain_one = back_one(inner_cols(grad_joined, qkv_low))
    return (
        grad_embedded + grad_middle,
        (grad_qkv, grad_out, grad_up, grad_down),
        (gain_one, gain_two),
    )


def candidate_loss(query_low, candidates, cand_bias, valid_here, offset):
    tokens, width = query_low.shape
    block_rows = min(512, tokens)
    blocks = tokens // block_rows
    column = jnp.arange(candidates.shape[0], dtype=jnp.int32)
    bias_wide = cand_bias.astype(jnp.float32)

    def one_block(running, block_pieces):
        query_block, valid_block, start_row = block_pieces
        logits = inner_cols(query_block, candidates) + bias_wide[None]
        highest = jnp.max(logits, axis=1, keepdims=True)
        log_total = highest + jnp.log(jnp.sum(jnp.exp(logits - highest), axis=1, keepdims=True))
        target_hit = (
            column[None, :]
            == (offset + start_row + jnp.arange(block_rows, dtype=jnp.int32))[:, None]
        )
        own_logit = jnp.sum(jnp.where(target_hit, logits, 0.0), axis=1)
        grad_logits = rounded(
            (jnp.exp(logits - log_total) - target_hit.astype(jnp.float32)) * valid_block[:, None]
        )
        return (
            running + jnp.sum(valid_block * (log_total[:, 0] - own_logit)),
            (grad_logits, log_total[:, 0]),
        )

    loss_part, block_out = lax.scan(
        one_block,
        jnp.zeros((), jnp.float32),
        (
            query_low.reshape(blocks, block_rows, width),
            valid_here.reshape(blocks, block_rows),
            jnp.arange(blocks, dtype=jnp.int32) * block_rows,
        ),
    )
    return (loss_part, block_out[0].reshape(tokens, -1), block_out[1].reshape(tokens))


def adam_step(weight, gradient, first, second, rate, decay):
    first_new = BETA_ONE * first + (1.0 - BETA_ONE) * gradient
    second_new = BETA_TWO * second + (1.0 - BETA_TWO) * gradient * gradient
    stepped = (
        first_new
        / (1.0 - BETA_ONE**STEP)
        / (jnp.sqrt(second_new / (1.0 - BETA_TWO**STEP)) + ADAM_EPS)
    )
    return (weight - rate * (stepped + decay * weight), first_new, second_new)


def reduce_rows(total_rows, devices):
    unit = 16 * devices
    return -(-total_rows // unit) * unit


def tail_kernel(dp_count, row_count, padded, capacity, qkv, out, up, down, pos, row_grads, slots, incoming, gathered, square,
                outgoing, acc, low, recv0, recv1, recv2, send_a, recv_a, send_r, recv_r):
    devices = dp_count * row_count
    dp = lax.axis_index("dp")
    row = lax.axis_index("rows")
    me = dp * row_count + row
    bits = row_count.bit_length() - 1
    barrier = pltpu.get_barrier_semaphore()

    def place(k):
        other = lax.rem(me + k, devices)
        return other, (other // row_count, lax.rem(other, row_count))

    def greet(k, carry):
        other, where = place(k)
        pl.semaphore_signal(barrier, inc=1, device_id=where, device_id_type=MESH)
        return carry

    lax.fori_loop(1, devices, greet, 0)
    width = 256
    at = 0
    for ref in (qkv, up):
        for c in range(ref.shape[1] // width):
            acc[pl.ds(at, ref.shape[0]), :] = ref[:, pl.ds(c * width, width)]
            at += ref.shape[0]
    for ref in (out, down, pos):
        acc[pl.ds(at, ref.shape[0]), :] = ref[...]
        at += ref.shape[0]
    if at < padded:
        acc[pl.ds(at, padded - at), :] = jnp.zeros((padded - at, width), jnp.float32)
    pl.semaphore_wait(barrier, devices - 1)

    def a2a_send(k):
        other, where = place(k)
        return pltpu.make_async_remote_copy(
            outgoing.at[other], incoming.at[me], send_a.at[k], recv_a.at[me], device_id=where, device_id_type=MESH)

    def a2a_recv(k):
        other, where = place(k)
        return pltpu.make_async_remote_copy(
            outgoing.at[other], incoming.at[other], send_a.at[k], recv_a.at[other], device_id=where, device_id_type=MESH)

    def partner(bit):
        step = 1 << bit
        mine = lax.rem(row // step, 2)
        return mine, (dp, row + step - 2 * step * mine)

    half = padded // 2
    units = padded // (16 * devices)
    part_rows = [((units + 1) // 2) * 16 * (devices // 2), (units // 2) * 16 * (devices // 2)]
    orders = [list(range(1, bits)), list(range(bits - 1, 0, -1))]
    al = lambda v: pl.multiple_of(v, 16)

    mine, where = partner(0)
    low[pl.ds(al((1 - mine) * half), half), :] = acc[pl.ds(al((1 - mine) * half), half), :].astype(jnp.bfloat16)
    first = pltpu.make_async_remote_copy(low.at[pl.ds(al((1 - mine) * half), half)], recv0, send_r.at[0], recv_r.at[0],
                                         device_id=where, device_id_type=MESH)
    first.start()
    slot_row = jnp.concatenate([slots[c : c + 1, :] for c in range(slots.shape[0])], axis=1)
    slot_index = lax.broadcasted_iota(jnp.int32, (capacity, slot_row.shape[1]), 0).astype(jnp.float32)

    def arrange(other):
        pick = one_hot(slot_index == slot_row - (other * capacity).astype(jnp.float32))
        return jnp.dot(pick, row_grads[...], preferred_element_type=jnp.float32).astype(jnp.bfloat16)

    def send_rows(k, carry):
        other, where = place(k)
        outgoing[other] = arrange(other)
        a2a_send(k).start()
        return carry

    lax.fori_loop(1, devices, send_rows, 0)
    incoming[me] = arrange(me)
    first.wait_recv()
    base = mine * half
    pending = [first]
    starts = [base, base + part_rows[0]]
    sizes = list(part_rows)
    offs = [0, sizes[0]]
    live = [p for p in range(2) if part_rows[p] > 0]
    acc[pl.ds(al(base), half), :] = acc[pl.ds(al(base), half), :] + recv0[...].astype(jnp.float32)
    sem = 1
    scratch_at = 0
    history = []
    for step in range(bits - 1):
        copies = []
        for p in live:
            bit = orders[p][step]
            mine, where = partner(bit)
            size = sizes[p] // 2
            keep = starts[p] + mine * size
            give = starts[p] + (1 - mine) * size
            low[pl.ds(al(give), size), :] = acc[pl.ds(al(give), size), :].astype(jnp.bfloat16)
            landing = recv1.at[pl.ds(scratch_at, size)]
            copy = pltpu.make_async_remote_copy(low.at[pl.ds(al(give), size)], landing, send_r.at[sem], recv_r.at[sem],
                                                device_id=where, device_id_type=MESH)
            copy.start()
            copies.append((p, copy, keep, size, scratch_at, where))
            sem += 1
            scratch_at += size
        for p, copy, keep, size, off, where in copies:
            copy.wait_recv()
            acc[pl.ds(al(keep), size), :] = acc[pl.ds(al(keep), size), :] + recv1[pl.ds(off, size), :].astype(jnp.float32)
            history.append((p, keep, size, where))
            starts[p], sizes[p] = keep, size
            pending.append(copy)
    copies = []
    off = 0
    final = {}
    for p in live:
        size = sizes[p] // dp_count
        for k in range(1, dp_count):
            other = lax.rem(dp + k, dp_count)
            give = starts[p] + other * size
            low[pl.ds(al(give), size), :] = acc[pl.ds(al(give), size), :].astype(jnp.bfloat16)
            copy = pltpu.make_async_remote_copy(low.at[pl.ds(al(give), size)], recv2.at[pl.ds(off, size)], send_r.at[sem], recv_r.at[sem],
                                                device_id=(other, row), device_id_type=MESH)
            copy.start()
            copies.append((p, copy, off, size))
            sem += 1
            off += size
        final[p] = (starts[p] + dp * size, size)
    for p, copy, off, size in copies:
        copy.wait_recv()
        at, size = final[p]
        acc[pl.ds(al(at), size), :] = acc[pl.ds(al(at), size), :] + recv2[pl.ds(off, size), :].astype(jnp.float32)
        pending.append(copy)
    total = jnp.zeros((1, width), jnp.float32)
    for p in live:
        at, size = final[p]
        mine_low = acc[pl.ds(al(at), size), :]
        total = total + jnp.sum(mine_low * mine_low, axis=0, keepdims=True)
        gathered[pl.ds(al(at), size), :] = mine_low.astype(jnp.bfloat16)
    square[...] = jnp.broadcast_to(total, square.shape)

    copies = []
    for p in live:
        at, size = final[p]
        for k in range(1, dp_count):
            other = lax.rem(dp + k, dp_count)
            copy = pltpu.make_async_remote_copy(gathered.at[pl.ds(al(at), size)], gathered.at[pl.ds(al(at), size)], send_r.at[sem], recv_r.at[sem],
                                                device_id=(other, row), device_id_type=MESH)
            copy.start()
            copies.append((p, copy, k, sem))
            sem += 1
    for p, copy, k, s in copies:
        at, size = final[p]
        source = lax.rem(dp + dp_count - k, dp_count)
        land = starts[p] + source * size
        pltpu.make_async_remote_copy(gathered.at[pl.ds(al(at), size)], gathered.at[pl.ds(al(land), size)], send_r.at[s], recv_r.at[s],
                                     device_id=(source, row), device_id_type=MESH).wait_recv()
        pending.append(copy)
    for step in range(bits - 2, -1, -1):
        copies = []
        for p in live:
            bit = orders[p][step]
            mine, where = partner(bit)
            size = sizes[p]
            at = starts[p]
            copy = pltpu.make_async_remote_copy(gathered.at[pl.ds(al(at), size)], gathered.at[pl.ds(al(at), size)], send_r.at[sem], recv_r.at[sem],
                                                device_id=where, device_id_type=MESH)
            copy.start()
            copies.append((p, copy, sem, mine, size, where))
            sem += 1
        for p, copy, s, mine, size, where in copies:
            bottom = starts[p] - mine * size
            land = bottom + (1 - mine) * size
            pltpu.make_async_remote_copy(gathered.at[pl.ds(al(land), size)], gathered.at[pl.ds(al(land), size)], send_r.at[s], recv_r.at[s],
                                         device_id=where, device_id_type=MESH).wait_recv()
            starts[p], sizes[p] = bottom, 2 * size
            pending.append(copy)
    mine, where = partner(0)
    last = pltpu.make_async_remote_copy(gathered.at[pl.ds(al(mine * half), half)], gathered.at[pl.ds(al(mine * half), half)], send_r.at[sem], recv_r.at[sem],
                                        device_id=where, device_id_type=MESH)
    last.start()
    pltpu.make_async_remote_copy(gathered.at[pl.ds(al((1 - mine) * half), half)], gathered.at[pl.ds(al((1 - mine) * half), half)], send_r.at[sem], recv_r.at[sem],
                                 device_id=where, device_id_type=MESH).wait_recv()
    sem += 1
    pending.append(last)
    lax.fori_loop(1, devices, lambda k, c: (a2a_recv(k).wait_recv(), c)[1], 0)
    for copy in pending:
        copy.wait_send()
    lax.fori_loop(1, devices, lambda k, c: (a2a_send(k).wait_send(), c)[1], 0)


def tail_exchange(dp_count, row_count, capacity, qkv, out, up, down, pos, row_grads, slots):
    devices = dp_count * row_count
    width = out.shape[1]
    rows = sum(a.size for a in (qkv, out, up, down, pos)) // width
    padded = reduce_rows(rows, devices)
    bits = row_count.bit_length() - 1
    sems = 2 + 4 * bits + 4 * dp_count + 8
    return pl.pallas_call(
        functools.partial(tail_kernel, dp_count, row_count, padded, capacity),
        out_shape=(jax.ShapeDtypeStruct((devices, capacity, width), jnp.bfloat16), jax.ShapeDtypeStruct((padded, width), jnp.bfloat16),
                   jax.ShapeDtypeStruct((8, width), jnp.float32)),
        in_specs=[VMEM] * 7, out_specs=(VMEM,) * 3,
        scratch_shapes=[
            pltpu.VMEM((devices, capacity, width), jnp.bfloat16),
            pltpu.VMEM((padded, width), jnp.float32),
            pltpu.VMEM((padded, width), jnp.bfloat16),
            pltpu.VMEM((padded // 2, width), jnp.bfloat16),
            pltpu.VMEM((padded // 2, width), jnp.bfloat16),
            pltpu.VMEM((padded // row_count, width), jnp.bfloat16),
            pltpu.SemaphoreType.DMA((devices,)), pltpu.SemaphoreType.DMA((devices,)),
            pltpu.SemaphoreType.DMA((sems,)), pltpu.SemaphoreType.DMA((sems,)),
        ],
        name="tail_exchange",
        compiler_params=pltpu.CompilerParams(collective_id=3, has_side_effects=True, vmem_limit_bytes=56 * 2**20),
    )(qkv, out, up, down, pos, row_grads, slots)


def other_device(k, dp_count, row_count):
    devices = dp_count * row_count
    me = lax.axis_index("dp") * row_count + lax.axis_index("rows")
    other = lax.rem(me + k, devices)
    return other, (other // row_count, lax.rem(other, row_count))


def one_hot(flags):
    return jnp.where(flags, 1.0, 0.0).astype(jnp.bfloat16)


def lookup_kernel(dp_count, row_count, capacity, used, wanted, item_row, table_hbm, fetched, slots, received,
                  table, pieces, slot_col, asked, ask, got, stage, ready, landed, asked_here,
                  table_sem, local_sem, send_q, recv_q, send_a, recv_a):
    devices = dp_count * row_count
    me = lax.axis_index("dp") * row_count + lax.axis_index("rows")
    rows_here = table.shape[0]
    events = wanted.shape[0]
    chunk = 256
    barrier = pltpu.get_barrier_semaphore()
    load_table = pltpu.make_async_copy(table_hbm, table, table_sem)
    load_table.start()

    def greet(k, carry):
        other, where = other_device(k, dp_count, row_count)
        pl.semaphore_signal(barrier, inc=1, device_id=where, device_id_type=MESH)
        return carry

    lax.fori_loop(1, devices, greet, 0)

    whole_rows = item_row.shape[0]
    lanes = item_row.shape[1]
    pieces[pl.ds(whole_rows, pieces.shape[0] - whole_rows), :] = jnp.zeros(
        (pieces.shape[0] - whole_rows, 3 * lanes), jnp.bfloat16
    )
    part = 224
    def cut(c, carry):
        at = pl.multiple_of(c * part, 16)
        values = item_row[pl.ds(at, part), :]
        for digit in range(3):
            piece = jnp.bitwise_and(jnp.right_shift(values, 8 * digit), 255)
            pieces[pl.ds(at, part), digit * lanes : (digit + 1) * lanes] = piece.astype(jnp.float32).astype(jnp.bfloat16)
        return carry
    lax.fori_loop(0, whole_rows // part, cut, 0)

    lane = lax.broadcasted_iota(jnp.int32, (chunk, lanes), 1)
    lane_f = lane.astype(jnp.float32)
    wide = lax.broadcasted_iota(jnp.int32, (chunk, pieces.shape[0]), 1)
    below = one_hot(
        lax.broadcasted_iota(jnp.int32, (chunk, chunk), 1) < lax.broadcasted_iota(jnp.int32, (chunk, chunk), 0)
    )
    diagonal = lax.broadcasted_iota(jnp.int32, (chunk, chunk), 1) == lax.broadcasted_iota(jnp.int32, (chunk, chunk), 0)
    asked[...] = jnp.zeros_like(asked)

    def route(c, counts):
        at = pl.multiple_of(c * chunk, chunk)
        ids = wanted[pl.ds(at, chunk), :]
        high = jnp.right_shift(ids, 7)
        low = jnp.bitwise_and(ids, 127)
        found = jnp.dot(one_hot(wide == high), pieces[...], preferred_element_type=jnp.float32)
        value = found[:, :lanes] + 256.0 * found[:, lanes : 2 * lanes] + 65536.0 * found[:, 2 * lanes :]
        row = jnp.sum(jnp.where(lane == low, value, 0.0), axis=1, keepdims=True)
        owner = jnp.floor((row + 0.5) * (1.0 / rows_here))
        local = row - owner * rows_here
        live = ids >= 0
        owned = jnp.logical_and(lane_f == owner, live)
        owned_low = one_hot(owned)
        before = jnp.dot(below, owned_low, preferred_element_type=jnp.float32) + counts
        rank = jnp.sum(jnp.where(owned, before, 0.0), axis=1, keepdims=True)
        slot = jnp.where(live, owner * capacity + rank, -1.0)
        slot_col[pl.ds(at, chunk), :] = slot
        slots[pl.ds(c, 1), :] = jnp.sum(jnp.where(diagonal, slot, 0.0), axis=0, keepdims=True)
        local_high = jnp.floor(local * (1.0 / 128))
        local_low = local - 128.0 * local_high
        at_rank = lane_f == rank
        both = jnp.concatenate(
            [jnp.where(at_rank, local_high, 0.0), jnp.where(at_rank, local_low, 0.0)], axis=1
        ).astype(jnp.bfloat16)
        asked[...] += lax.dot_general(owned_low, both, (((0,), (0,)), ((), ())), preferred_element_type=jnp.float32)
        return counts + jnp.sum(jnp.where(owned, 1.0, 0.0), axis=0, keepdims=True)

    lax.fori_loop(0, events // chunk, route, jnp.zeros((1, lanes), jnp.float32))
    rows_asked = (128.0 * asked[:, :lanes] + asked[:, lanes:]).astype(jnp.int32)
    for d in range(devices):
        ask[d] = rows_asked[d : d + 1, :]
    pl.semaphore_wait(barrier, devices - 1)

    def query(k, at_other):
        other, where = other_device(k, dp_count, row_count)
        return pltpu.make_async_remote_copy(
            ask.at[other], got.at[other if at_other else me], send_q.at[k], recv_q.at[other if at_other else me],
            device_id=where, device_id_type=MESH,
        )

    def answer(k, at_other):
        other, where = other_device(k, dp_count, row_count)
        place = pl.multiple_of((other if at_other else me) * capacity, 16)
        return pltpu.make_async_remote_copy(
            ready.at[k], landed.at[pl.ds(place, capacity)], send_a.at[k], recv_a.at[other if at_other else me],
            device_id=where, device_id_type=MESH,
        )

    lax.fori_loop(1, devices, lambda k, c: (query(k, False).start(), c)[1], 0)
    got[me] = ask[me]
    stage[...] = jnp.zeros_like(stage)
    load_table.wait()
    lax.fori_loop(1, devices, lambda k, c: (query(k, True).wait_recv(), c)[1], 0)
    received[...] = jnp.clip(got[...], 0, rows_here - 1)
    to_scalars = pltpu.make_async_copy(received, asked_here, local_sem)
    to_scalars.start()
    to_scalars.wait()

    def gather(source):
        def some(c, carry):
            at = pl.multiple_of(c * 8, 8)
            for j in range(8):
                row = asked_here[source, 0, at + j]
                stage[pl.ds(at + j, 1), :] = table[pl.ds(row, 1), :]
            return carry
        lax.fori_loop(0, used // 8, some, 0)
        return stage[...].astype(jnp.bfloat16)

    def reply(k, carry):
        other, where = other_device(k, dp_count, row_count)
        ready[k] = gather(other)
        answer(k, False).start()
        return carry

    lax.fori_loop(1, devices, reply, 0)
    landed[pl.ds(pl.multiple_of(me * capacity, 16), capacity), :] = gather(me)
    lax.fori_loop(1, devices, lambda k, c: (answer(k, True).wait_recv(), c)[1], 0)

    slot_lane = lax.broadcasted_iota(jnp.int32, (chunk, devices * capacity), 1).astype(jnp.float32)

    def settle(c, carry):
        at = pl.multiple_of(c * chunk, chunk)
        pick = one_hot(slot_lane == slot_col[pl.ds(at, chunk), :])
        fetched[pl.ds(at, chunk), :] = jnp.dot(pick, landed[...], preferred_element_type=jnp.float32).astype(jnp.bfloat16)
        return carry

    lax.fori_loop(0, events // chunk, settle, 0)
    lax.fori_loop(1, devices, lambda k, c: (query(k, False).wait_send(), c)[1], 0)
    lax.fori_loop(1, devices, lambda k, c: (answer(k, False).wait_send(), c)[1], 0)


def lookup(dp_count, row_count, capacity, used, wanted, item_row, item_table):
    devices = dp_count * row_count
    events = wanted.shape[0]
    lanes = 128
    width = item_table.shape[1]
    blocks = item_row.shape[0] // lanes
    return pl.pallas_call(
        functools.partial(lookup_kernel, dp_count, row_count, capacity, used),
        out_shape=(
            jax.ShapeDtypeStruct((events, width), jnp.bfloat16),
            jax.ShapeDtypeStruct((events // 256, 256), jnp.float32),
            jax.ShapeDtypeStruct((devices, 1, lanes), jnp.int32),
        ),
        in_specs=[VMEM, VMEM, pl.BlockSpec(memory_space=pl.ANY)],
        out_specs=(VMEM,) * 3,
        scratch_shapes=[
            pltpu.VMEM(item_table.shape, jnp.float32),
            pltpu.VMEM((-(-blocks // lanes) * lanes, 3 * lanes), jnp.bfloat16),
            pltpu.VMEM((events, 1), jnp.float32),
            pltpu.VMEM((lanes, 2 * lanes), jnp.float32),
            pltpu.VMEM((devices, 1, lanes), jnp.int32),
            pltpu.VMEM((devices, 1, lanes), jnp.int32),
            pltpu.VMEM((capacity, width), jnp.float32),
            pltpu.VMEM((devices, capacity, width), jnp.bfloat16),
            pltpu.VMEM((devices * capacity, width), jnp.bfloat16),
            pltpu.SMEM((devices, 1, lanes), jnp.int32),
            pltpu.SemaphoreType.DMA,
            pltpu.SemaphoreType.DMA,
            pltpu.SemaphoreType.DMA((devices,)),
            pltpu.SemaphoreType.DMA((devices,)),
            pltpu.SemaphoreType.DMA((devices,)),
            pltpu.SemaphoreType.DMA((devices,)),
        ],
        name="lookup",
        compiler_params=pltpu.CompilerParams(collective_id=2, has_side_effects=True, vmem_limit_bytes=56 * 2**20),
    )(wanted, item_row.reshape(-1, lanes), item_table)


def table_kernel(received, incoming, grads, square):
    tile, width = grads.shape
    step = pl.program_id(0)
    rows = lax.broadcasted_iota(jnp.int32, (tile, received.shape[1]), 0) + step * tile
    grad = jnp.dot(one_hot(rows == received[...]), incoming[...], preferred_element_type=jnp.float32)
    grads[...] = grad

    @pl.when(step == 0)
    def start():
        square[...] = jnp.zeros_like(square)

    square[...] += jnp.broadcast_to(jnp.sum(grad * grad, axis=0, keepdims=True), square.shape)


def table_gradient(rows_here, received, incoming):
    width = incoming.shape[1]
    tile = 224
    return pl.pallas_call(
        table_kernel,
        grid=(rows_here // tile,),
        out_shape=(
            jax.ShapeDtypeStruct((rows_here, width), jnp.float32),
            jax.ShapeDtypeStruct((8, width), jnp.float32),
        ),
        in_specs=[
            pl.BlockSpec(received.shape, lambda i: (0, 0)),
            pl.BlockSpec(incoming.shape, lambda i: (0, 0)),
        ],
        out_specs=(
            pl.BlockSpec((tile, width), lambda i: (i, 0)),
            pl.BlockSpec((8, width), lambda i: (0, 0)),
        ),
        name="table_gradient",
        compiler_params=pltpu.CompilerParams(vmem_limit_bytes=40 * 2**20),
    )(received, incoming)


def small_kernel(dp_count, row_count, part, summed, by_row, by_dp, send_sem, recv_sem):
    dp = lax.axis_index("dp")
    row = lax.axis_index("rows")
    barrier = pltpu.get_barrier_semaphore()
    row_places = [lax.rem(row + k, row_count) for k in range(1, row_count)]
    dp_places = [lax.rem(dp + k, dp_count) for k in range(1, dp_count)]
    for other in row_places:
        pl.semaphore_signal(barrier, inc=1, device_id=(dp, other), device_id_type=MESH)
    for other in dp_places:
        pl.semaphore_signal(barrier, inc=1, device_id=(other, row), device_id_type=MESH)
    pl.semaphore_wait(barrier, row_count + dp_count - 2)

    def spread(source, landing, mine, others, where, base):
        sends = []
        for k, other in enumerate(others):
            copy = pltpu.make_async_remote_copy(
                source, landing.at[mine], send_sem.at[base + k], recv_sem.at[base + mine],
                device_id=where(other), device_id_type=MESH,
            )
            copy.start()
            sends.append(copy)
        landing[mine] = source[...]
        for other in others:
            pltpu.make_async_remote_copy(
                source, landing.at[other], send_sem.at[base], recv_sem.at[base + other],
                device_id=where(other), device_id_type=MESH,
            ).wait_recv()
        for copy in sends:
            copy.wait_send()

    spread(part, by_row, row, row_places, lambda other: (dp, other), 0)
    summed[...] = jnp.sum(by_row[...], axis=0)
    spread(summed, by_dp, dp, dp_places, lambda other: (other, row), row_count)
    summed[...] = jnp.sum(by_dp[...], axis=0)


def small_sum(dp_count, row_count, part):
    return pl.pallas_call(
        functools.partial(small_kernel, dp_count, row_count),
        out_shape=jax.ShapeDtypeStruct(part.shape, part.dtype),
        in_specs=[VMEM],
        out_specs=VMEM,
        scratch_shapes=[
            pltpu.VMEM((row_count,) + part.shape, part.dtype),
            pltpu.VMEM((dp_count,) + part.shape, part.dtype),
            pltpu.SemaphoreType.DMA((row_count + dp_count,)),
            pltpu.SemaphoreType.DMA((row_count + dp_count,)),
        ],
        name="small_sum",
        compiler_params=pltpu.CompilerParams(collective_id=4, has_side_effects=True),
    )(part)


def local(
    item_ids,
    targets,
    lengths,
    correction,
    item_row,
    item_table,
    qkv_weight,
    out_weight,
    up_weight,
    down_weight,
    positions,
    gains,
    item_table_first,
    qkv_weight_first,
    out_weight_first,
    up_weight_first,
    down_weight_first,
    positions_first,
    gains_first,
    item_table_second,
    qkv_weight_second,
    out_weight_second,
    up_weight_second,
    down_weight_second,
    positions_second,
    gains_second,
):
    micro, histories, length = item_ids.shape
    rows_here, width = item_table.shape
    devices = lax.axis_size("dp") * lax.axis_size("rows")
    tokens = histories * length
    requests = 2 * micro * tokens
    capacity = 3 * (requests + devices) // (2 * devices) + 1
    used = -(-capacity // 8) * 8
    capacity = -(-capacity // 16) * 16
    dp_count, row_count = lax.axis_size("dp"), lax.axis_size("rows")
    position = jnp.arange(length, dtype=jnp.int32)
    valid_pos = (position[None, None, :] < lengths[:, :, None]).reshape(micro, tokens)
    wanted = jnp.where(
        valid_pos.reshape(1, -1), jnp.stack([item_ids, targets]).reshape(2, micro * tokens), -1
    ).reshape(requests, 1)
    fetched, slots, received = lookup(
        dp_count, row_count, capacity, used, wanted, item_row, item_table
    )
    received = received[:, 0, :capacity].reshape(1, devices * capacity)
    fetched = fetched.reshape(2, micro, tokens, width)
    matrices = (rounded(qkv_weight), rounded(out_weight), rounded(up_weight), rounded(down_weight))
    scaling = math.sqrt(width)
    offset = lax.axis_index("rows") * tokens
    running = [
        jnp.zeros_like(qkv_weight),
        jnp.zeros_like(out_weight),
        jnp.zeros_like(up_weight),
        jnp.zeros_like(down_weight),
    ]
    grad_positions = jnp.zeros_like(positions)
    grad_gains = jnp.zeros_like(gains)
    loss_local = jnp.zeros((), jnp.float32)
    embed_grads = []
    target_grads = []
    for micro_index in range(micro):
        lengths_here = lengths[micro_index]
        valid_here = valid_pos[micro_index].astype(jnp.float32)
        embedded = scaling * fetched[0, micro_index].astype(jnp.float32) + jnp.tile(
            positions, (histories, 1)
        )
        output, saved_state = layer_forward(embedded, lengths_here, matrices, gains, HEADS)
        normed_three, back_three = jax.vjp(rms_norm, output, gains[2])
        query_low = rounded(normed_three)
        bias_low = jnp.where(
            valid_pos[micro_index],
            rounded(-correction[micro_index].reshape(-1)),
            jnp.asarray(MASKED, jnp.bfloat16),
        )
        candidates, cand_bias = (
            lax.all_gather(fetched[1, micro_index], "rows", axis=0, tiled=True),
            lax.all_gather(bias_low, "rows", axis=0, tiled=True),
        )
        loss_part, grad_logits, log_total = candidate_loss(
            query_low, candidates, cand_bias, valid_here, offset
        )
        loss_local = loss_local + loss_part
        grad_output, gain_three = back_three(matmul(grad_logits, candidates))
        target_grads.append(
            lax.psum_scatter(
                inner_rows(grad_logits, query_low).astype(jnp.bfloat16),
                "rows",
                scatter_dimension=0,
                tiled=True,
            ).astype(jnp.float32)
        )
        grad_embedded, grad_layer, gain_pair = layer_backward(
            grad_output, saved_state, lengths_here, matrices, HEADS
        )
        for which_one in range(4):
            running[which_one] = running[which_one] + grad_layer[which_one]
        grad_positions = grad_positions + jnp.sum(
            grad_embedded.reshape(histories, length, width), axis=0
        )
        grad_gains = grad_gains + jnp.stack([gain_pair[0], gain_pair[1], gain_three])
        embed_grads.append(scaling * grad_embedded)
    target_part = jnp.stack(target_grads)
    row_grads = jnp.concatenate([jnp.stack(embed_grads), target_part]).reshape(requests, width)
    incoming, gathered, square = tail_exchange(
        dp_count,
        row_count,
        capacity,
        running[0],
        running[1],
        running[2],
        running[3],
        grad_positions,
        rounded(row_grads),
        slots,
    )
    table_grad, table_square = table_gradient(
        rows_here, received, incoming.reshape(devices * capacity, width)
    )
    own_square = jnp.sum(table_square[0] + square[0])
    scalars = jnp.stack([loss_local, jnp.sum(valid_pos.astype(jnp.float32)), own_square])
    part = jnp.concatenate(
        [grad_gains.reshape(-1), jnp.pad(scalars, (0, 1024 - grad_gains.size - 3))]
    ).reshape(8, 128)
    small = small_sum(dp_count, row_count, part).reshape(-1)
    sum_gains = small[: grad_gains.size].reshape(grad_gains.shape)
    sum_loss, sum_count, square_total = (small[grad_gains.size + k] for k in range(3))
    gathered = gathered.astype(jnp.float32)
    place = 0
    blocks = []
    for like in (qkv_weight, up_weight):
        count = like.shape[1] // width
        piece = gathered[place : place + count * like.shape[0]]
        blocks.append(
            jnp.concatenate(
                [piece[c * like.shape[0] : (c + 1) * like.shape[0]] for c in range(count)], axis=1
            )
        )
        place += count * like.shape[0]
    for like in (out_weight, down_weight, positions):
        blocks.append(gathered[place : place + like.shape[0]])
        place += like.shape[0]
    gradients = (table_grad, blocks[0], blocks[2], blocks[1], blocks[3], blocks[4], sum_gains)
    grad_norm = jnp.sqrt(square_total + jnp.sum(sum_gains * sum_gains))
    factor = CLIP / jnp.maximum(grad_norm, CLIP)
    weights = (item_table, qkv_weight, out_weight, up_weight, down_weight, positions, gains)
    firsts = (
        item_table_first,
        qkv_weight_first,
        out_weight_first,
        up_weight_first,
        down_weight_first,
        positions_first,
        gains_first,
    )
    seconds = (
        item_table_second,
        qkv_weight_second,
        out_weight_second,
        up_weight_second,
        down_weight_second,
        positions_second,
        gains_second,
    )
    rates = (RATE, RATE, RATE, RATE, RATE, RATE, GAIN_RATE)
    decays = (DECAY, DECAY, DECAY, DECAY, DECAY, DECAY, 0.0)
    updated = [
        adam_step(
            weights[which_one],
            factor * gradients[which_one],
            firsts[which_one],
            seconds[which_one],
            rates[which_one],
            decays[which_one],
        )
        for which_one in range(7)
    ]
    return (
        updated[0][0],
        updated[1][0],
        updated[2][0],
        updated[3][0],
        updated[4][0],
        updated[5][0],
        updated[6][0],
        updated[0][1],
        updated[1][1],
        updated[2][1],
        updated[3][1],
        updated[4][1],
        updated[5][1],
        updated[6][1],
        updated[0][2],
        updated[1][2],
        updated[2][2],
        updated[3][2],
        updated[4][2],
        updated[5][2],
        updated[6][2],
        sum_loss,
        sum_count,
        grad_norm,
    )


def solution(mesh):
    placed = (
        P(None, ("dp", "rows"), None),
        P(None, ("dp", "rows"), None),
        P(None, ("dp", "rows")),
        P(None, ("dp", "rows"), None),
        P(),
        P(("dp", "rows"), None),
        P(),
        P(),
        P(),
        P(),
        P(),
        P(),
        P(("dp", "rows"), None),
        P(),
        P(),
        P(),
        P(),
        P(),
        P(),
        P(("dp", "rows"), None),
        P(),
        P(),
        P(),
        P(),
        P(),
        P(),
    )
    return jax.shard_map(
        local,
        mesh=mesh,
        in_specs=placed,
        out_specs=(
            P(("dp", "rows"), None),
            P(),
            P(),
            P(),
            P(),
            P(),
            P(),
            P(("dp", "rows"), None),
            P(),
            P(),
            P(),
            P(),
            P(),
            P(),
            P(("dp", "rows"), None),
            P(),
            P(),
            P(),
            P(),
            P(),
            P(),
            P(),
            P(),
            P(),
        ),
        check_vma=False,
    )
```

```python
import functools
import math

import jax
import jax.numpy as jnp
from jax import lax
from jax.experimental import pallas as pl
from jax.experimental.pallas import tpu as pltpu
from jax.sharding import PartitionSpec as P

MESH = pl.DeviceIdType.MESH
VMEM = pl.BlockSpec(memory_space=pltpu.VMEM)
HEADS = 8
STEP = 10


NORM_EPS = 1e-06
MASKED = -1e30
BETA_ONE = 0.9
BETA_TWO = 0.999
ADAM_EPS = 1e-08
DECAY = 0.01
RATE = 0.1
GAIN_RATE = 1.0
CLIP = 1.0


def rounded(values):
    return values.astype(jnp.bfloat16)


def matmul(first_op, second_op):
    return jnp.dot(first_op, second_op, preferred_element_type=jnp.float32)


def inner_rows(first_op, second_op):
    return lax.dot_general(
        first_op, second_op, (((0,), (0,)), ((), ())), preferred_element_type=jnp.float32
    )


def inner_cols(first_op, second_op):
    return lax.dot_general(
        first_op, second_op, (((1,), (1,)), ((), ())), preferred_element_type=jnp.float32
    )


def rms_norm(values, gain_row):
    return (
        values * lax.rsqrt(jnp.mean(values * values, axis=-1, keepdims=True) + NORM_EPS) * gain_row
    )


def gelu_tanh(values):
    return jax.nn.gelu(values)


def split_heads(joined, histories, head_count):
    pieces = joined.reshape(histories, joined.shape[0] // histories, 3, head_count, -1)
    return (pieces[:, :, 0], pieces[:, :, 1], pieces[:, :, 2])


def masked_scores(queries, key_rows, lengths_here):
    length = queries.shape[1]
    scaling = queries.shape[-1] ** (-0.5)
    scores = (
        jnp.einsum("sqhe,skhe->shqk", queries, key_rows, preferred_element_type=jnp.float32)
        * scaling
    )
    position = jnp.arange(length, dtype=jnp.int32)
    allowed = (position[None, :] <= position[:, None])[None, None] & (
        position[None, None, None, :] < lengths_here[:, None, None, None]
    )
    return jnp.where(allowed, scores, MASKED)


def attention_forward(joined, lengths_here, head_count):
    queries, key_rows, value_rows = split_heads(joined, lengths_here.shape[0], head_count)
    scores = masked_scores(queries, key_rows, lengths_here)
    highest = jnp.max(scores, axis=-1, keepdims=True)
    log_total = highest + jnp.log(jnp.sum(jnp.exp(scores - highest), axis=-1, keepdims=True))
    probabilities = rounded(jnp.exp(scores - log_total))
    attended = jnp.einsum(
        "shqk,skhe->sqhe", probabilities, value_rows, preferred_element_type=jnp.float32
    )
    return (attended.reshape(joined.shape[0], -1), log_total)


def attention_backward(joined, log_total, lengths_here, grad_attended, head_count):
    queries, key_rows, value_rows = split_heads(joined, lengths_here.shape[0], head_count)
    probabilities = jnp.exp(masked_scores(queries, key_rows, lengths_here) - log_total)
    grad_heads = grad_attended.reshape(queries.shape)
    grad_probs = jnp.einsum(
        "sqhe,skhe->shqk", grad_heads, value_rows, preferred_element_type=jnp.float32
    )
    grad_values = jnp.einsum(
        "shqk,sqhe->skhe", rounded(probabilities), grad_heads, preferred_element_type=jnp.float32
    )
    row_inner = jnp.sum(probabilities * grad_probs, axis=-1, keepdims=True)
    grad_scores = rounded(probabilities * (grad_probs - row_inner))
    scaling = queries.shape[-1] ** (-0.5)
    grad_queries = (
        jnp.einsum("shqk,skhe->sqhe", grad_scores, key_rows, preferred_element_type=jnp.float32)
        * scaling
    )
    grad_keys = (
        jnp.einsum("shqk,sqhe->skhe", grad_scores, queries, preferred_element_type=jnp.float32)
        * scaling
    )
    stacked = jnp.stack([grad_queries, grad_keys, grad_values], axis=2)
    return stacked.reshape(joined.shape[0], -1)


def layer_forward(embedded, lengths_here, matrices, gains, head_count):
    qkv_low, out_low, up_low, down_low = matrices
    normed_one, back_one = jax.vjp(rms_norm, embedded, gains[0])
    hidden_one = rounded(normed_one)
    joined = rounded(matmul(hidden_one, qkv_low))
    attended, log_total = attention_forward(joined, lengths_here, head_count)
    attended_low = rounded(attended)
    middle = embedded + matmul(attended_low, out_low)
    normed_two, back_two = jax.vjp(rms_norm, middle, gains[1])
    hidden_two = rounded(normed_two)
    upward = matmul(hidden_two, up_low)
    active, back_active = jax.vjp(gelu_tanh, upward)
    active_low = rounded(active)
    output = middle + matmul(active_low, down_low)
    return (
        output,
        (
            back_one,
            hidden_one,
            joined,
            log_total,
            attended_low,
            back_two,
            hidden_two,
            back_active,
            active_low,
        ),
    )


def layer_backward(grad_output, saved_state, lengths_here, matrices, head_count):
    (
        back_one,
        hidden_one,
        joined,
        log_total,
        attended_low,
        back_two,
        hidden_two,
        back_active,
        active_low,
    ) = saved_state
    qkv_low, out_low, up_low, down_low = matrices
    grad_branch = rounded(grad_output)
    grad_down = inner_rows(active_low, grad_branch)
    grad_upward = rounded(back_active(inner_cols(grad_branch, down_low))[0])
    grad_up = inner_rows(hidden_two, grad_upward)
    grad_middle, gain_two = back_two(inner_cols(grad_upward, up_low))
    grad_middle = grad_middle + grad_output
    grad_attn = rounded(grad_middle)
    grad_out = inner_rows(attended_low, grad_attn)
    grad_attended = rounded(inner_cols(grad_attn, out_low))
    grad_joined = rounded(
        attention_backward(joined, log_total, lengths_here, grad_attended, head_count)
    )
    grad_qkv = inner_rows(hidden_one, grad_joined)
    grad_embedded, gain_one = back_one(inner_cols(grad_joined, qkv_low))
    return (
        grad_embedded + grad_middle,
        (grad_qkv, grad_out, grad_up, grad_down),
        (gain_one, gain_two),
    )


def candidate_loss(query_low, candidates, cand_bias, valid_here, offset):
    tokens, width = query_low.shape
    block_rows = min(512, tokens)
    blocks = tokens // block_rows
    column = jnp.arange(candidates.shape[0], dtype=jnp.int32)
    bias_wide = cand_bias.astype(jnp.float32)

    def one_block(running, block_pieces):
        query_block, valid_block, start_row = block_pieces
        logits = inner_cols(query_block, candidates) + bias_wide[None]
        highest = jnp.max(logits, axis=1, keepdims=True)
        log_total = highest + jnp.log(jnp.sum(jnp.exp(logits - highest), axis=1, keepdims=True))
        target_hit = (
            column[None, :]
            == (offset + start_row + jnp.arange(block_rows, dtype=jnp.int32))[:, None]
        )
        own_logit = jnp.sum(jnp.where(target_hit, logits, 0.0), axis=1)
        grad_logits = rounded(
            (jnp.exp(logits - log_total) - target_hit.astype(jnp.float32)) * valid_block[:, None]
        )
        return (
            running + jnp.sum(valid_block * (log_total[:, 0] - own_logit)),
            (grad_logits, log_total[:, 0]),
        )

    loss_part, block_out = lax.scan(
        one_block,
        jnp.zeros((), jnp.float32),
        (
            query_low.reshape(blocks, block_rows, width),
            valid_here.reshape(blocks, block_rows),
            jnp.arange(blocks, dtype=jnp.int32) * block_rows,
        ),
    )
    return (loss_part, block_out[0].reshape(tokens, -1), block_out[1].reshape(tokens))


def adam_step(weight, gradient, first, second, rate, decay):
    first_new = BETA_ONE * first + (1.0 - BETA_ONE) * gradient
    second_new = BETA_TWO * second + (1.0 - BETA_TWO) * gradient * gradient
    stepped = (
        first_new
        / (1.0 - BETA_ONE**STEP)
        / (jnp.sqrt(second_new / (1.0 - BETA_TWO**STEP)) + ADAM_EPS)
    )
    return (weight - rate * (stepped + decay * weight), first_new, second_new)


def reduce_rows(total_rows, devices):
    unit = 16 * devices
    return -(-total_rows // unit) * unit


def tail_kernel(dp_count, row_count, padded, capacity, qkv, out, up, down, pos, row_grads, slots, incoming, gathered, square,
                outgoing, acc, low, recv0, recv1, recv2, send_a, recv_a, send_r, recv_r):
    devices = dp_count * row_count
    dp = lax.axis_index("dp")
    row = lax.axis_index("rows")
    me = dp * row_count + row
    bits = row_count.bit_length() - 1
    barrier = pltpu.get_barrier_semaphore()

    def place(k):
        other = lax.rem(me + k, devices)
        return other, (other // row_count, lax.rem(other, row_count))

    def greet(k, carry):
        other, where = place(k)
        pl.semaphore_signal(barrier, inc=1, device_id=where, device_id_type=MESH)
        return carry

    lax.fori_loop(1, devices, greet, 0)
    width = 256
    at = 0
    for ref in (qkv, up):
        for c in range(ref.shape[1] // width):
            acc[pl.ds(at, ref.shape[0]), :] = ref[:, pl.ds(c * width, width)]
            at += ref.shape[0]
    for ref in (out, down, pos):
        acc[pl.ds(at, ref.shape[0]), :] = ref[...]
        at += ref.shape[0]
    if at < padded:
        acc[pl.ds(at, padded - at), :] = jnp.zeros((padded - at, width), jnp.float32)
    pl.semaphore_wait(barrier, devices - 1)

    def a2a_send(k):
        other, where = place(k)
        return pltpu.make_async_remote_copy(
            outgoing.at[other], incoming.at[me], send_a.at[k], recv_a.at[me], device_id=where, device_id_type=MESH)

    def a2a_recv(k):
        other, where = place(k)
        return pltpu.make_async_remote_copy(
            outgoing.at[other], incoming.at[other], send_a.at[k], recv_a.at[other], device_id=where, device_id_type=MESH)

    def partner(bit):
        step = 1 << bit
        mine = lax.rem(row // step, 2)
        return mine, (dp, row + step - 2 * step * mine)

    half = padded // 2
    units = padded // (16 * devices)
    part_rows = [((units + 1) // 2) * 16 * (devices // 2), (units // 2) * 16 * (devices // 2)]
    orders = [list(range(1, bits)), list(range(bits - 1, 0, -1))]
    al = lambda v: pl.multiple_of(v, 16)

    mine, where = partner(0)
    low[pl.ds(al((1 - mine) * half), half), :] = acc[pl.ds(al((1 - mine) * half), half), :].astype(jnp.bfloat16)
    first = pltpu.make_async_remote_copy(low.at[pl.ds(al((1 - mine) * half), half)], recv0, send_r.at[0], recv_r.at[0],
                                         device_id=where, device_id_type=MESH)
    first.start()
    slot_row = jnp.concatenate([slots[c : c + 1, :] for c in range(slots.shape[0])], axis=1)
    slot_index = lax.broadcasted_iota(jnp.int32, (capacity, slot_row.shape[1]), 0).astype(jnp.float32)

    def arrange(other):
        pick = one_hot(slot_index == slot_row - (other * capacity).astype(jnp.float32))
        return jnp.dot(pick, row_grads[...], preferred_element_type=jnp.float32).astype(jnp.bfloat16)

    def send_rows(k, carry):
        other, where = place(k)
        outgoing[other] = arrange(other)
        a2a_send(k).start()
        return carry

    lax.fori_loop(1, devices, send_rows, 0)
    incoming[me] = arrange(me)
    first.wait_recv()
    base = mine * half
    pending = [first]
    starts = [base, base + part_rows[0]]
    sizes = list(part_rows)
    offs = [0, sizes[0]]
    live = [p for p in range(2) if part_rows[p] > 0]
    acc[pl.ds(al(base), half), :] = acc[pl.ds(al(base), half), :] + recv0[...].astype(jnp.float32)
    sem = 1
    scratch_at = 0
    history = []
    for step in range(bits - 1):
        copies = []
        for p in live:
            bit = orders[p][step]
            mine, where = partner(bit)
            size = sizes[p] // 2
            keep = starts[p] + mine * size
            give = starts[p] + (1 - mine) * size
            low[pl.ds(al(give), size), :] = acc[pl.ds(al(give), size), :].astype(jnp.bfloat16)
            landing = recv1.at[pl.ds(scratch_at, size)]
            copy = pltpu.make_async_remote_copy(low.at[pl.ds(al(give), size)], landing, send_r.at[sem], recv_r.at[sem],
                                                device_id=where, device_id_type=MESH)
            copy.start()
            copies.append((p, copy, keep, size, scratch_at, where))
            sem += 1
            scratch_at += size
        for p, copy, keep, size, off, where in copies:
            copy.wait_recv()
            acc[pl.ds(al(keep), size), :] = acc[pl.ds(al(keep), size), :] + recv1[pl.ds(off, size), :].astype(jnp.float32)
            history.append((p, keep, size, where))
            starts[p], sizes[p] = keep, size
            pending.append(copy)
    copies = []
    off = 0
    final = {}
    for p in live:
        size = sizes[p] // dp_count
        for k in range(1, dp_count):
            other = lax.rem(dp + k, dp_count)
            give = starts[p] + other * size
            low[pl.ds(al(give), size), :] = acc[pl.ds(al(give), size), :].astype(jnp.bfloat16)
            copy = pltpu.make_async_remote_copy(low.at[pl.ds(al(give), size)], recv2.at[pl.ds(off, size)], send_r.at[sem], recv_r.at[sem],
                                                device_id=(other, row), device_id_type=MESH)
            copy.start()
            copies.append((p, copy, off, size))
            sem += 1
            off += size
        final[p] = (starts[p] + dp * size, size)
    for p, copy, off, size in copies:
        copy.wait_recv()
        at, size = final[p]
        acc[pl.ds(al(at), size), :] = acc[pl.ds(al(at), size), :] + recv2[pl.ds(off, size), :].astype(jnp.float32)
        pending.append(copy)
    total = jnp.zeros((1, width), jnp.float32)
    for p in live:
        at, size = final[p]
        mine_low = acc[pl.ds(al(at), size), :]
        total = total + jnp.sum(mine_low * mine_low, axis=0, keepdims=True)
        gathered[pl.ds(al(at), size), :] = mine_low.astype(jnp.bfloat16)
    square[...] = jnp.broadcast_to(total, square.shape)

    copies = []
    for p in live:
        at, size = final[p]
        for k in range(1, dp_count):
            other = lax.rem(dp + k, dp_count)
            copy = pltpu.make_async_remote_copy(gathered.at[pl.ds(al(at), size)], gathered.at[pl.ds(al(at), size)], send_r.at[sem], recv_r.at[sem],
                                                device_id=(other, row), device_id_type=MESH)
            copy.start()
            copies.append((p, copy, k, sem))
            sem += 1
    for p, copy, k, s in copies:
        at, size = final[p]
        source = lax.rem(dp + dp_count - k, dp_count)
        land = starts[p] + source * size
        pltpu.make_async_remote_copy(gathered.at[pl.ds(al(at), size)], gathered.at[pl.ds(al(land), size)], send_r.at[s], recv_r.at[s],
                                     device_id=(source, row), device_id_type=MESH).wait_recv()
        pending.append(copy)
    for step in range(bits - 2, -1, -1):
        copies = []
        for p in live:
            bit = orders[p][step]
            mine, where = partner(bit)
            size = sizes[p]
            at = starts[p]
            copy = pltpu.make_async_remote_copy(gathered.at[pl.ds(al(at), size)], gathered.at[pl.ds(al(at), size)], send_r.at[sem], recv_r.at[sem],
                                                device_id=where, device_id_type=MESH)
            copy.start()
            copies.append((p, copy, sem, mine, size, where))
            sem += 1
        for p, copy, s, mine, size, where in copies:
            bottom = starts[p] - mine * size
            land = bottom + (1 - mine) * size
            pltpu.make_async_remote_copy(gathered.at[pl.ds(al(land), size)], gathered.at[pl.ds(al(land), size)], send_r.at[s], recv_r.at[s],
                                         device_id=where, device_id_type=MESH).wait_recv()
            starts[p], sizes[p] = bottom, 2 * size
            pending.append(copy)
    mine, where = partner(0)
    last = pltpu.make_async_remote_copy(gathered.at[pl.ds(al(mine * half), half)], gathered.at[pl.ds(al(mine * half), half)], send_r.at[sem], recv_r.at[sem],
                                        device_id=where, device_id_type=MESH)
    last.start()
    pltpu.make_async_remote_copy(gathered.at[pl.ds(al((1 - mine) * half), half)], gathered.at[pl.ds(al((1 - mine) * half), half)], send_r.at[sem], recv_r.at[sem],
                                 device_id=where, device_id_type=MESH).wait_recv()
    sem += 1
    pending.append(last)
    lax.fori_loop(1, devices, lambda k, c: (a2a_recv(k).wait_recv(), c)[1], 0)
    for copy in pending:
        copy.wait_send()
    lax.fori_loop(1, devices, lambda k, c: (a2a_send(k).wait_send(), c)[1], 0)


def tail_exchange(dp_count, row_count, capacity, qkv, out, up, down, pos, row_grads, slots):
    devices = dp_count * row_count
    width = out.shape[1]
    rows = sum(a.size for a in (qkv, out, up, down, pos)) // width
    padded = reduce_rows(rows, devices)
    bits = row_count.bit_length() - 1
    sems = 2 + 4 * bits + 4 * dp_count + 8
    return pl.pallas_call(
        functools.partial(tail_kernel, dp_count, row_count, padded, capacity),
        out_shape=(jax.ShapeDtypeStruct((devices, capacity, width), jnp.bfloat16), jax.ShapeDtypeStruct((padded, width), jnp.bfloat16),
                   jax.ShapeDtypeStruct((8, width), jnp.float32)),
        in_specs=[VMEM] * 7, out_specs=(VMEM,) * 3,
        scratch_shapes=[
            pltpu.VMEM((devices, capacity, width), jnp.bfloat16),
            pltpu.VMEM((padded, width), jnp.float32),
            pltpu.VMEM((padded, width), jnp.bfloat16),
            pltpu.VMEM((padded // 2, width), jnp.bfloat16),
            pltpu.VMEM((padded // 2, width), jnp.bfloat16),
            pltpu.VMEM((padded // row_count, width), jnp.bfloat16),
            pltpu.SemaphoreType.DMA((devices,)), pltpu.SemaphoreType.DMA((devices,)),
            pltpu.SemaphoreType.DMA((sems,)), pltpu.SemaphoreType.DMA((sems,)),
        ],
        name="tail_exchange",
        compiler_params=pltpu.CompilerParams(collective_id=3, has_side_effects=True, vmem_limit_bytes=56 * 2**20),
    )(qkv, out, up, down, pos, row_grads, slots)


def other_device(k, dp_count, row_count):
    devices = dp_count * row_count
    me = lax.axis_index("dp") * row_count + lax.axis_index("rows")
    other = lax.rem(me + k, devices)
    return other, (other // row_count, lax.rem(other, row_count))


def one_hot(flags):
    return jnp.where(flags, 1.0, 0.0).astype(jnp.bfloat16)


def lookup_kernel(dp_count, row_count, capacity, used, wanted, item_row, table_hbm, fetched, slots, received,
                  table, pieces, slot_col, asked, ask, got, stage, ready, landed, asked_here,
                  table_sem, local_sem, send_q, recv_q, send_a, recv_a):
    devices = dp_count * row_count
    me = lax.axis_index("dp") * row_count + lax.axis_index("rows")
    rows_here = table.shape[0]
    events = wanted.shape[0]
    chunk = 256
    barrier = pltpu.get_barrier_semaphore()
    load_table = pltpu.make_async_copy(table_hbm, table, table_sem)
    load_table.start()

    def greet(k, carry):
        other, where = other_device(k, dp_count, row_count)
        pl.semaphore_signal(barrier, inc=1, device_id=where, device_id_type=MESH)
        return carry

    lax.fori_loop(1, devices, greet, 0)

    whole_rows = item_row.shape[0]
    lanes = item_row.shape[1]
    pieces[pl.ds(whole_rows, pieces.shape[0] - whole_rows), :] = jnp.zeros(
        (pieces.shape[0] - whole_rows, 3 * lanes), jnp.bfloat16
    )
    part = 224
    def cut(c, carry):
        at = pl.multiple_of(c * part, 16)
        values = item_row[pl.ds(at, part), :]
        for digit in range(3):
            piece = jnp.bitwise_and(jnp.right_shift(values, 8 * digit), 255)
            pieces[pl.ds(at, part), digit * lanes : (digit + 1) * lanes] = piece.astype(jnp.float32).astype(jnp.bfloat16)
        return carry
    lax.fori_loop(0, whole_rows // part, cut, 0)

    lane = lax.broadcasted_iota(jnp.int32, (chunk, lanes), 1)
    lane_f = lane.astype(jnp.float32)
    wide = lax.broadcasted_iota(jnp.int32, (chunk, pieces.shape[0]), 1)
    below = one_hot(
        lax.broadcasted_iota(jnp.int32, (chunk, chunk), 1) < lax.broadcasted_iota(jnp.int32, (chunk, chunk), 0)
    )
    diagonal = lax.broadcasted_iota(jnp.int32, (chunk, chunk), 1) == lax.broadcasted_iota(jnp.int32, (chunk, chunk), 0)
    asked[...] = jnp.zeros_like(asked)

    def route(c, counts):
        at = pl.multiple_of(c * chunk, chunk)
        ids = wanted[pl.ds(at, chunk), :]
        high = jnp.right_shift(ids, 7)
        low = jnp.bitwise_and(ids, 127)
        found = jnp.dot(one_hot(wide == high), pieces[...], preferred_element_type=jnp.float32)
        value = found[:, :lanes] + 256.0 * found[:, lanes : 2 * lanes] + 65536.0 * found[:, 2 * lanes :]
        row = jnp.sum(jnp.where(lane == low, value, 0.0), axis=1, keepdims=True)
        owner = jnp.floor((row + 0.5) * (1.0 / rows_here))
        local = row - owner * rows_here
        live = ids >= 0
        owned = jnp.logical_and(lane_f == owner, live)
        owned_low = one_hot(owned)
        before = jnp.dot(below, owned_low, preferred_element_type=jnp.float32) + counts
        rank = jnp.sum(jnp.where(owned, before, 0.0), axis=1, keepdims=True)
        slot = jnp.where(live, owner * capacity + rank, -1.0)
        slot_col[pl.ds(at, chunk), :] = slot
        slots[pl.ds(c, 1), :] = jnp.sum(jnp.where(diagonal, slot, 0.0), axis=0, keepdims=True)
        local_high = jnp.floor(local * (1.0 / 128))
        local_low = local - 128.0 * local_high
        at_rank = lane_f == rank
        both = jnp.concatenate(
            [jnp.where(at_rank, local_high, 0.0), jnp.where(at_rank, local_low, 0.0)], axis=1
        ).astype(jnp.bfloat16)
        asked[...] += lax.dot_general(owned_low, both, (((0,), (0,)), ((), ())), preferred_element_type=jnp.float32)
        return counts + jnp.sum(jnp.where(owned, 1.0, 0.0), axis=0, keepdims=True)

    lax.fori_loop(0, events // chunk, route, jnp.zeros((1, lanes), jnp.float32))
    rows_asked = (128.0 * asked[:, :lanes] + asked[:, lanes:]).astype(jnp.int32)
    for d in range(devices):
        ask[d] = rows_asked[d : d + 1, :]
    pl.semaphore_wait(barrier, devices - 1)

    def query(k, at_other):
        other, where = other_device(k, dp_count, row_count)
        return pltpu.make_async_remote_copy(
            ask.at[other], got.at[other if at_other else me], send_q.at[k], recv_q.at[other if at_other else me],
            device_id=where, device_id_type=MESH,
        )

    def answer(k, at_other):
        other, where = other_device(k, dp_count, row_count)
        place = pl.multiple_of((other if at_other else me) * capacity, 16)
        return pltpu.make_async_remote_copy(
            ready.at[k], landed.at[pl.ds(place, capacity)], send_a.at[k], recv_a.at[other if at_other else me],
            device_id=where, device_id_type=MESH,
        )

    lax.fori_loop(1, devices, lambda k, c: (query(k, False).start(), c)[1], 0)
    got[me] = ask[me]
    stage[...] = jnp.zeros_like(stage)
    load_table.wait()
    lax.fori_loop(1, devices, lambda k, c: (query(k, True).wait_recv(), c)[1], 0)
    received[...] = jnp.clip(got[...], 0, rows_here - 1)
    to_scalars = pltpu.make_async_copy(received, asked_here, local_sem)
    to_scalars.start()
    to_scalars.wait()

    def gather(source):
        def some(c, carry):
            at = pl.multiple_of(c * 8, 8)
            for j in range(8):
                row = asked_here[source, 0, at + j]
                stage[pl.ds(at + j, 1), :] = table[pl.ds(row, 1), :]
            return carry
        lax.fori_loop(0, used // 8, some, 0)
        return stage[...].astype(jnp.bfloat16)

    def reply(k, carry):
        other, where = other_device(k, dp_count, row_count)
        ready[k] = gather(other)
        answer(k, False).start()
        return carry

    lax.fori_loop(1, devices, reply, 0)
    landed[pl.ds(pl.multiple_of(me * capacity, 16), capacity), :] = gather(me)
    lax.fori_loop(1, devices, lambda k, c: (answer(k, True).wait_recv(), c)[1], 0)

    slot_lane = lax.broadcasted_iota(jnp.int32, (chunk, devices * capacity), 1).astype(jnp.float32)

    def settle(c, carry):
        at = pl.multiple_of(c * chunk, chunk)
        pick = one_hot(slot_lane == slot_col[pl.ds(at, chunk), :])
        fetched[pl.ds(at, chunk), :] = jnp.dot(pick, landed[...], preferred_element_type=jnp.float32).astype(jnp.bfloat16)
        return carry

    lax.fori_loop(0, events // chunk, settle, 0)
    lax.fori_loop(1, devices, lambda k, c: (query(k, False).wait_send(), c)[1], 0)
    lax.fori_loop(1, devices, lambda k, c: (answer(k, False).wait_send(), c)[1], 0)


def lookup(dp_count, row_count, capacity, used, wanted, item_row, item_table):
    devices = dp_count * row_count
    events = wanted.shape[0]
    lanes = 128
    width = item_table.shape[1]
    blocks = item_row.shape[0] // lanes
    return pl.pallas_call(
        functools.partial(lookup_kernel, dp_count, row_count, capacity, used),
        out_shape=(
            jax.ShapeDtypeStruct((events, width), jnp.bfloat16),
            jax.ShapeDtypeStruct((events // 256, 256), jnp.float32),
            jax.ShapeDtypeStruct((devices, 1, lanes), jnp.int32),
        ),
        in_specs=[VMEM, VMEM, pl.BlockSpec(memory_space=pl.ANY)],
        out_specs=(VMEM,) * 3,
        scratch_shapes=[
            pltpu.VMEM(item_table.shape, jnp.float32),
            pltpu.VMEM((-(-blocks // lanes) * lanes, 3 * lanes), jnp.bfloat16),
            pltpu.VMEM((events, 1), jnp.float32),
            pltpu.VMEM((lanes, 2 * lanes), jnp.float32),
            pltpu.VMEM((devices, 1, lanes), jnp.int32),
            pltpu.VMEM((devices, 1, lanes), jnp.int32),
            pltpu.VMEM((capacity, width), jnp.float32),
            pltpu.VMEM((devices, capacity, width), jnp.bfloat16),
            pltpu.VMEM((devices * capacity, width), jnp.bfloat16),
            pltpu.SMEM((devices, 1, lanes), jnp.int32),
            pltpu.SemaphoreType.DMA,
            pltpu.SemaphoreType.DMA,
            pltpu.SemaphoreType.DMA((devices,)),
            pltpu.SemaphoreType.DMA((devices,)),
            pltpu.SemaphoreType.DMA((devices,)),
            pltpu.SemaphoreType.DMA((devices,)),
        ],
        name="lookup",
        compiler_params=pltpu.CompilerParams(collective_id=2, has_side_effects=True, vmem_limit_bytes=56 * 2**20),
    )(wanted, item_row.reshape(-1, lanes), item_table)


def table_kernel(received, incoming, grads, square):
    tile, width = grads.shape
    step = pl.program_id(0)
    rows = lax.broadcasted_iota(jnp.int32, (tile, received.shape[1]), 0) + step * tile
    grad = jnp.dot(one_hot(rows == received[...]), incoming[...], preferred_element_type=jnp.float32)
    grads[...] = grad

    @pl.when(step == 0)
    def start():
        square[...] = jnp.zeros_like(square)

    square[...] += jnp.broadcast_to(jnp.sum(grad * grad, axis=0, keepdims=True), square.shape)


def table_gradient(rows_here, received, incoming):
    width = incoming.shape[1]
    tile = 224
    return pl.pallas_call(
        table_kernel,
        grid=(rows_here // tile,),
        out_shape=(
            jax.ShapeDtypeStruct((rows_here, width), jnp.float32),
            jax.ShapeDtypeStruct((8, width), jnp.float32),
        ),
        in_specs=[
            pl.BlockSpec(received.shape, lambda i: (0, 0)),
            pl.BlockSpec(incoming.shape, lambda i: (0, 0)),
        ],
        out_specs=(
            pl.BlockSpec((tile, width), lambda i: (i, 0)),
            pl.BlockSpec((8, width), lambda i: (0, 0)),
        ),
        name="table_gradient",
        compiler_params=pltpu.CompilerParams(vmem_limit_bytes=40 * 2**20),
    )(received, incoming)


def dot_nn(first_op, second_op):
    return jnp.dot(first_op, second_op, preferred_element_type=jnp.float32)


def dot_nt(first_op, second_op):
    return lax.dot_general(
        first_op, second_op, (((1,), (1,)), ((), ())), preferred_element_type=jnp.float32
    )


def dot_tn(first_op, second_op):
    return lax.dot_general(
        first_op, second_op, (((0,), (0,)), ((), ())), preferred_element_type=jnp.float32
    )


def inverse_rms(values):
    return lax.rsqrt(jnp.mean(values * values, axis=-1, keepdims=True) + NORM_EPS)


def rms_back(values, gain_row, grad):
    scale = inverse_rms(values)
    grad_scaled = grad * gain_row
    inner = jnp.mean(values * grad_scaled, axis=-1, keepdims=True)
    gain_part = jnp.sum(grad * values * scale, axis=0, keepdims=True)
    return scale * grad_scaled - values * (scale * scale * scale * inner), gain_part


def subsets(bits):
    found = [()]
    for bit in bits:
        found = found + [one + (bit,) for one in found]
    return found


def flip(index, bits):
    for bit in bits:
        step = 1 << bit
        index = index + step - 2 * step * lax.rem(index // step, 2)
    return index


def layer_kernel(row_count, lengths, items, targets, correction, qkv_hbm, out_hbm, up_hbm, down_hbm, positions, gains,
                 grad_qkv, grad_out, grad_up, grad_down, grad_positions, row_grads, small,
                 qkv_low, out_low, up_low, down_low, embedded, hidden_one, joined, probs_top, probs_low, attended,
                 middle, hidden_two, slope, active, output, query, cand, bias, cand_grads, landing, logits,
                 grad_logits, highest, scores, grad_scores, grad_middle_low, grad_attended, part_k, part_v,
                 load_sem, send_b, recv_b, send_g, recv_g, send_s, recv_s):
    micro = 2
    tokens = positions.shape[0]
    half = tokens // 2
    width = positions.shape[1]
    inner = out_low.shape[0]
    bits = row_count.bit_length() - 1
    dp = lax.axis_index("dp")
    row = lax.axis_index("rows")
    bf = jnp.bfloat16
    barrier = pltpu.get_barrier_semaphore()
    for k in range(1, row_count):
        pl.semaphore_signal(
            barrier, inc=1, device_id=(dp, lax.rem(row + k, row_count)), device_id_type=MESH
        )
    ff = up_low.shape[1]
    loads = [
        (qkv_hbm, 0, 0, 3 * inner, qkv_low),
        (up_hbm, 0, 3 * inner, ff, up_low),
    ]
    at = 3 * inner + ff
    for source, low in ((out_hbm, out_low), (down_hbm, down_low)):
        for k in range(source.shape[0] // width):
            loads.append((source, k * width, at, width, low))
            at += width
    copies = []
    for k, (source, first, at, count, low) in enumerate(loads):
        copy = pltpu.make_async_copy(
            source.at[pl.ds(first, width)], logits.at[:, pl.ds(at, count)], load_sem.at[k]
        )
        copy.start()
        copies.append(copy)

    column = lax.broadcasted_iota(jnp.int32, (1, tokens), 1)
    for m in range(micro):
        own_bias = jnp.where(
            column < lengths[m], (-correction[m : m + 1, :]).astype(bf).astype(jnp.float32), MASKED
        )
        bias[row, m : m + 1, :] = own_bias.astype(bf).astype(jnp.float32)
        cand[m, pl.ds(pl.multiple_of(row * tokens, tokens), tokens), :] = targets[m * tokens : (m + 1) * tokens, :]
    pl.semaphore_wait(barrier, row_count - 1)

    pending = []
    for k in range(1, row_count):
        copy = pltpu.make_async_remote_copy(
            bias.at[row], bias.at[row], send_b.at[k], recv_b.at[row],
            device_id=(dp, lax.rem(row + k, row_count)), device_id_type=MESH,
        )
        copy.start()
        pending.append(copy)

    orders = [list(range(1, bits)) + [0], list(range(bits - 1, 0, -1)) + [0]]
    block_of = lambda ref, m, owner: ref.at[m, pl.ds(pl.multiple_of(owner * tokens, tokens), tokens)]
    gather_steps = []
    count = 0
    for step in range(bits):
        here = []
        for m in range(micro):
            for mask in subsets(orders[m][:step]):
                here.append((m, orders[m][step], mask, count))
                count += 1
        gather_steps.append(here)

    def gather_start(step):
        for m, bit, mask, sem in gather_steps[step]:
            mine = flip(row, mask)
            copy = pltpu.make_async_remote_copy(
                block_of(cand, m, mine), block_of(cand, m, mine), send_g.at[sem], recv_g.at[sem],
                device_id=(dp, flip(row, (bit,))), device_id_type=MESH,
            )
            copy.start()
            pending.append(copy)

    def gather_wait(step):
        for m, bit, mask, sem in gather_steps[step]:
            theirs = flip(flip(row, (bit,)), mask)
            pltpu.make_async_remote_copy(
                block_of(cand, m, theirs), block_of(cand, m, theirs), send_g.at[sem], recv_g.at[sem],
                device_id=(dp, flip(row, (bit,))), device_id_type=MESH,
            ).wait_recv()

    gather_start(0)

    scatter_orders = [[0] + list(range(1, bits)), [0] + list(range(bits - 1, 0, -1))]
    scatter_steps = []
    count = 0
    for m in range(micro):
        levels = []
        for step in range(bits):
            bit = scatter_orders[m][step]
            levels.append([(bit, mask, count + i) for i, mask in enumerate(subsets(scatter_orders[m][step + 1 :]))])
            count += len(levels[-1])
        scatter_steps.append(levels)

    def scatter_start(m, step):
        for bit, mask, sem in scatter_steps[m][step]:
            there = flip(row, (bit,))
            copy = pltpu.make_async_remote_copy(
                block_of(cand_grads, m, flip(there, mask)), landing.at[sem], send_s.at[sem], recv_s.at[sem],
                device_id=(dp, there), device_id_type=MESH,
            )
            copy.start()
            pending.append(copy)

    def scatter_wait(m, step):
        for bit, mask, sem in scatter_steps[m][step]:
            there = flip(row, (bit,))
            pltpu.make_async_remote_copy(
                block_of(cand_grads, m, flip(row, mask)), landing.at[sem], send_s.at[sem], recv_s.at[sem],
                device_id=(dp, there), device_id_type=MESH,
            ).wait_recv()
            base = flip(row, mask) * tokens
            last = step == bits - 1

            def add(c, carry):
                at = pl.multiple_of(base + c * 64, 64)
                near = pl.multiple_of(c * 64, 64)
                total = cand_grads[m, pl.ds(at, 64), :].astype(jnp.float32) + landing[sem, pl.ds(near, 64), :].astype(jnp.float32)
                if last:
                    row_grads[pl.ds(pl.multiple_of((micro + m) * tokens + c * 64, 64), 64), :] = total.astype(bf)
                else:
                    cand_grads[m, pl.ds(at, 64), :] = total.astype(bf)
                return carry

            lax.fori_loop(0, tokens // 64, add, 0)

    for copy, (source, first, at, count, low) in zip(copies, loads):
        copy.wait()
    for source, first, at, count, low in loads:
        low[pl.ds(first, width), :] = logits[:, pl.ds(at, count)].astype(bf)

    chunks = micro * 2
    gain_one, gain_two, gain_three = gains[0:1, :], gains[1:2, :], gains[2:3, :]
    scaling = math.sqrt(width)

    def project(c, carry):
        at = pl.multiple_of(c * half, half)
        near = pl.multiple_of(lax.rem(c, 2) * half, half)
        values = scaling * items[pl.ds(at, half), :].astype(jnp.float32) + positions[pl.ds(near, half), :]
        embedded[pl.ds(at, half), :] = values
        normed = (values * inverse_rms(values) * gain_one).astype(bf)
        hidden_one[pl.ds(at, half), :] = normed
        joined[pl.ds(at, half), :inner] = (dot_nn(normed, qkv_low[:, :inner]).astype(bf) * bf(0.125))
        joined[pl.ds(at, half), inner:] = dot_nn(normed, qkv_low[:, inner:]).astype(bf)
        return carry

    lax.fori_loop(0, chunks, project, 0)
    gather_wait(0)
    gather_start(1)

    lane = lax.broadcasted_iota(jnp.int32, (1, 128), 1)
    head_mask = [jnp.where(lane < 64, 1.0, 0.0).astype(bf), jnp.where(lane < 64, 0.0, 1.0).astype(bf)]
    pairs = inner // 128
    sub = 32

    def attend(m):
        masked_row = jnp.where(column < lengths[m], 0.0, MASKED)
        base = m * tokens

        def pair(hp, carry):
            lanes = [pl.ds(pl.multiple_of(k * inner + hp * 128, 128), 128) for k in range(3)]
            keys = joined[base : base + tokens, lanes[1]]
            values = joined[base : base + tokens, lanes[2]]
            for rb in range(2):
                first = base + rb * half
                span = (rb + 1) * half
                probs = probs_low if rb else probs_top
                queries = joined[first : first + half, lanes[0]]
                for h in range(2):
                    scores[h, :, :span] = dot_nt(queries * head_mask[h], keys[:span])
                for h in range(2):
                    for s in range(half // sub):
                        value = scores[h, s * sub : (s + 1) * sub, :span] + masked_row[:, :span]
                        allowed = (
                            lax.broadcasted_iota(jnp.int32, (sub, half), 1)
                            <= lax.broadcasted_iota(jnp.int32, (sub, half), 0) + s * sub
                        )
                        corner = jnp.where(allowed, value[:, rb * half :], MASKED)
                        value = jnp.concatenate([value[:, :half], corner], axis=1) if rb else corner
                        value = jnp.exp(value - jnp.max(value, axis=1, keepdims=True))
                        value = value * (1.0 / jnp.sum(value, axis=1, keepdims=True))
                        probs[m * 2 * pairs + hp * 2 + h, s * sub : (s + 1) * sub, :] = value.astype(bf)
                total = dot_nn(probs[m * 2 * pairs + hp * 2], values[:span] * head_mask[0]) + dot_nn(
                    probs[m * 2 * pairs + hp * 2 + 1], values[:span] * head_mask[1]
                )
                attended[first : first + half, pl.ds(pl.multiple_of(hp * 128, 128), 128)] = total.astype(bf)
            return carry

        lax.fori_loop(0, pairs, pair, 0)

    attend(0)
    gather_wait(1)
    for step in range(2, bits):
        gather_start(step)
        if step < bits - 1:
            gather_wait(step)
    attend(1)

    gelu_scale = math.sqrt(2.0 / math.pi)

    def feed(c, carry):
        at = pl.multiple_of(c * half, half)
        values = embedded[pl.ds(at, half), :] + dot_nn(attended[pl.ds(at, half), :], out_low[...])
        middle[pl.ds(at, half), :] = values
        normed = (values * inverse_rms(values) * gain_two).astype(bf)
        hidden_two[pl.ds(at, half), :] = normed
        logits[:, :ff] = dot_nn(normed, up_low[...])

        def bend(s, carry):
            for part in range(2):
                near = pl.multiple_of(s * 32 + part * 16, 16)
                there = pl.multiple_of(at + s * 32 + part * 16, 16)
                upward = logits[pl.ds(near, 16), :ff]
                square = upward * upward
                bent = jnp.tanh(gelu_scale * upward * (1.0 + 0.044715 * square))
                active[pl.ds(there, 16), :] = (0.5 * upward * (1.0 + bent)).astype(bf)
                slope[pl.ds(there, 16), :] = 0.5 * (1.0 + bent) + 0.5 * gelu_scale * upward * (1.0 - bent * bent) * (
                    1.0 + 3.0 * 0.044715 * square
                )
            return carry

        lax.fori_loop(0, half // 32, bend, 0)
        values = values + dot_nn(active[pl.ds(at, half), :], down_low[...])
        output[pl.ds(at, half), :] = values
        query[pl.ds(at, half), :] = (values * inverse_rms(values) * gain_three).astype(bf)
        return carry

    lax.fori_loop(0, chunks, feed, 0)
    gather_wait(bits - 1)
    for k in range(1, row_count):
        other = lax.rem(row + k, row_count)
        pltpu.make_async_remote_copy(
            bias.at[other], bias.at[other], send_b.at[k], recv_b.at[other],
            device_id=(dp, other), device_id_type=MESH,
        ).wait_recv()

    block = 512
    blocks = row_count * tokens // block
    fine = 16

    def loss_of(m):
        length = lengths[m]

        def one_half(rh, carry):
            first = pl.multiple_of(m * tokens + rh * half, half)
            queries = query[pl.ds(first, half), :]
            highest[...] = jnp.full_like(highest, -3.0e38)

            def score(j, carry):
                at = pl.multiple_of(j * block, block)
                value = dot_nt(queries, cand[m, pl.ds(at, block), :]) + bias[j, m : m + 1, :]
                logits[:, pl.ds(at, block)] = value
                top = jnp.maximum(
                    jnp.maximum(value[:, :128], value[:, 128:256]), jnp.maximum(value[:, 256:384], value[:, 384:])
                )
                highest[...] = jnp.maximum(highest[...], top)
                return carry

            lax.fori_loop(0, blocks, score, 0)

            def soften(s, carry):
                near = pl.multiple_of(s * fine, fine)
                place = rh * half + s * fine
                own_at = pl.multiple_of(row * tokens + (place // 128) * 128, 128)
                hit = lax.broadcasted_iota(jnp.int32, (fine, 128), 1) == lax.broadcasted_iota(
                    jnp.int32, (fine, 128), 0
                ) + lax.rem(place, 128)
                valid = jnp.where(
                    lax.broadcasted_iota(jnp.int32, (fine, 1), 0) + place < length, 1.0, 0.0
                )
                top = jnp.max(highest[pl.ds(near, fine), :], axis=1, keepdims=True)
                own_logit = jnp.sum(
                    jnp.where(hit, logits[pl.ds(near, fine), pl.ds(own_at, 128)], 0.0), axis=1, keepdims=True
                )
                total = jnp.zeros((fine, 128), jnp.float32)
                for j in range(blocks):
                    value = jnp.exp(logits[pl.ds(near, fine), j * block : (j + 1) * block] - top)
                    logits[pl.ds(near, fine), j * block : (j + 1) * block] = value
                    total = total + ((value[:, :128] + value[:, 128:256]) + (value[:, 256:384] + value[:, 384:]))
                total = jnp.sum(total, axis=1, keepdims=True)
                share = valid / total
                there = pl.multiple_of(place, fine)
                for j in range(blocks):
                    grad_logits[pl.ds(there, fine), j * block : (j + 1) * block] = (
                        logits[pl.ds(near, fine), j * block : (j + 1) * block] * share
                    ).astype(bf)
                own = logits[pl.ds(near, fine), pl.ds(own_at, 128)] * share - jnp.where(hit, valid, 0.0)
                grad_logits[pl.ds(there, fine), pl.ds(own_at, 128)] = own.astype(bf)
                return carry + valid * (top + jnp.log(total) - own_logit)

            loss = lax.fori_loop(0, half // fine, soften, jnp.zeros((fine, 1), jnp.float32))
            small[3:4, :] += jnp.broadcast_to(jnp.sum(loss, axis=0, keepdims=True), (1, width))
            grad_query = dot_nn(grad_logits[pl.ds(pl.multiple_of(rh * half, half), half), :], cand[m])
            grad, gain_part = rms_back(output[pl.ds(first, half), :], gain_three, grad_query)
            output[pl.ds(first, half), :] = grad
            small[2:3, :] += gain_part
            return carry

        lax.fori_loop(0, 2, one_half, 0)

        def to_targets(j, carry):
            at = pl.multiple_of(j * block, block)
            cand_grads[m, pl.ds(at, block), :] = dot_tn(
                grad_logits[:, pl.ds(at, block)], query[m * tokens : (m + 1) * tokens, :]
            ).astype(bf)
            return carry

        lax.fori_loop(0, blocks, to_targets, 0)
        scatter_start(m, 0)
        small[4:5, :] += jnp.broadcast_to(
            jnp.sum(jnp.where(column < length, 1.0, 0.0), axis=1, keepdims=True), (1, width)
        )

    small[...] = jnp.zeros_like(small)
    loss_of(0)
    loss_of(1)
    scatter_wait(0, 0)
    if bits > 1:
        scatter_start(0, 1)

    query[...] = output[...].astype(bf)
    for k in range(ff // width):
        grad_down[k * width : (k + 1) * width, :] = dot_tn(active[:, k * width : (k + 1) * width], query[...])
    scatter_wait(1, 0)
    if bits > 1:
        scatter_start(1, 1)

    def feed_back(c, carry):
        at = pl.multiple_of(c * half, half)
        branch = query[pl.ds(at, half), :]
        for k in range(ff // width):
            active[pl.ds(at, half), k * width : (k + 1) * width] = (
                dot_nt(branch, down_low[k * width : (k + 1) * width, :])
                * slope[pl.ds(at, half), k * width : (k + 1) * width]
            ).astype(bf)
        grad_hidden = dot_nt(active[pl.ds(at, half), :], up_low[...])
        grad, gain_part = rms_back(middle[pl.ds(at, half), :], gain_two, grad_hidden)
        small[1:2, :] += gain_part
        grad = grad + output[pl.ds(at, half), :]
        output[pl.ds(at, half), :] = grad
        grad_low = grad.astype(bf)
        grad_middle_low[pl.ds(at, half), :] = grad_low
        grad_attended[pl.ds(at, half), :] = dot_nt(grad_low, out_low[...]).astype(bf)
        return carry

    lax.fori_loop(0, chunks, feed_back, 0)
    grad_up[...] = dot_tn(hidden_two[...], active[...])
    grad_out[...] = dot_tn(attended[...], grad_middle_low[...])
    for step in range(1, bits - 1):
        for m in range(micro):
            scatter_wait(m, step)
            scatter_start(m, step + 1)

    def attend_back(m):
        base = m * tokens

        def pair(hp, carry):
            lanes = [pl.ds(pl.multiple_of(k * inner + hp * 128, 128), 128) for k in range(3)]
            here = pl.ds(pl.multiple_of(hp * 128, 128), 128)
            keys = joined[base : base + tokens, lanes[1]]
            values = joined[base : base + tokens, lanes[2]]
            for rb in (1, 0):
                first = base + rb * half
                span = (rb + 1) * half
                probs = probs_low if rb else probs_top
                queries = joined[first : first + half, lanes[0]]
                upper = grad_attended[first : first + half, here]
                for h in range(2):
                    scores[h, :, :span] = dot_nt(upper * head_mask[h], values[:span])
                for h in range(2):
                    for s in range(half // sub):
                        chance = probs[m * 2 * pairs + hp * 2 + h, s * sub : (s + 1) * sub, :].astype(jnp.float32)
                        grad = scores[h, s * sub : (s + 1) * sub, :span]
                        inner_sum = jnp.sum(chance * grad, axis=1, keepdims=True)
                        grad_scores[h, s * sub : (s + 1) * sub, :span] = (chance * (grad - inner_sum)).astype(bf)
                total_q = dot_nn(grad_scores[0, :, :span], keys[:span] * head_mask[0]) + dot_nn(
                    grad_scores[1, :, :span], keys[:span] * head_mask[1]
                )
                total_k = dot_tn(grad_scores[0, :, :span], queries * head_mask[0]) + dot_tn(
                    grad_scores[1, :, :span], queries * head_mask[1]
                )
                total_v = dot_tn(probs[m * 2 * pairs + hp * 2], upper * head_mask[0]) + dot_tn(
                    probs[m * 2 * pairs + hp * 2 + 1], upper * head_mask[1]
                )
                joined[first : first + half, lanes[0]] = (total_q * 0.125).astype(bf)
                if rb:
                    part_k[...] = total_k
                    part_v[...] = total_v
                else:
                    part_k[:half, :] += total_k
                    part_v[:half, :] += total_v
            joined[base : base + tokens, lanes[1]] = part_k[...].astype(bf)
            joined[base : base + tokens, lanes[2]] = part_v[...].astype(bf)
            return carry

        lax.fori_loop(0, pairs, pair, 0)

    attend_back(0)
    attend_back(1)

    def project_back(c, carry):
        at = pl.multiple_of(c * half, half)
        near = pl.multiple_of(lax.rem(c, 2) * half, half)
        grad_hidden = dot_nt(joined[pl.ds(at, half), :], qkv_low[...])
        grad, gain_part = rms_back(embedded[pl.ds(at, half), :], gain_one, grad_hidden)
        small[0:1, :] += gain_part
        grad = grad + output[pl.ds(at, half), :]
        grad_positions[pl.ds(near, half), :] += grad
        row_grads[pl.ds(at, half), :] = (scaling * grad).astype(bf)
        return carry

    grad_positions[...] = jnp.zeros_like(grad_positions)
    lax.fori_loop(0, chunks, project_back, 0)
    for k in range(3 * inner // 512):
        grad_qkv[:, k * 512 : (k + 1) * 512] = dot_tn(hidden_one[...], joined[:, k * 512 : (k + 1) * 512])
    for m in range(micro):
        if bits > 1:
            scatter_wait(m, bits - 1)
    for copy in pending:
        copy.wait_send()


def layer(row_count, lengths, items, targets, correction, matrices, positions, gains):
    qkv, out, up, down = matrices
    tokens, width = positions.shape
    half = tokens // 2
    inner, ff = out.shape[0], up.shape[1]
    events = 2 * tokens
    group = row_count * tokens
    bf, f32 = jnp.bfloat16, jnp.float32
    pairs = inner // 128
    bits = row_count.bit_length() - 1
    hops = 2 * (row_count - 1)
    sems = lambda count: pltpu.SemaphoreType.DMA((count,))
    hbm = pl.BlockSpec(memory_space=pl.ANY)
    return pl.pallas_call(
        functools.partial(layer_kernel, row_count),
        out_shape=(
            jax.ShapeDtypeStruct(qkv.shape, f32),
            jax.ShapeDtypeStruct(out.shape, f32),
            jax.ShapeDtypeStruct(up.shape, f32),
            jax.ShapeDtypeStruct(down.shape, f32),
            jax.ShapeDtypeStruct(positions.shape, f32),
            jax.ShapeDtypeStruct((2 * events, width), bf),
            jax.ShapeDtypeStruct((8, width), f32),
        ),
        in_specs=[pl.BlockSpec(memory_space=pltpu.SMEM), VMEM, VMEM, VMEM, hbm, hbm, hbm, hbm, VMEM, VMEM],
        out_specs=(VMEM,) * 7,
        scratch_shapes=[
            pltpu.VMEM(qkv.shape, bf),
            pltpu.VMEM(out.shape, bf),
            pltpu.VMEM(up.shape, bf),
            pltpu.VMEM(down.shape, bf),
            pltpu.VMEM((events, width), f32),
            pltpu.VMEM((events, width), bf),
            pltpu.VMEM((events, 3 * inner), bf),
            pltpu.VMEM((4 * pairs, half, half), bf),
            pltpu.VMEM((4 * pairs, half, tokens), bf),
            pltpu.VMEM((events, inner), bf),
            pltpu.VMEM((events, width), f32),
            pltpu.VMEM((events, width), bf),
            pltpu.VMEM((events, ff), f32),
            pltpu.VMEM((events, ff), bf),
            pltpu.VMEM((events, width), f32),
            pltpu.VMEM((events, width), bf),
            pltpu.VMEM((2, group, width), bf),
            pltpu.VMEM((row_count, 2, tokens), f32),
            pltpu.VMEM((2, group, width), bf),
            pltpu.VMEM((hops, tokens, width), bf),
            pltpu.VMEM((half, group), f32),
            pltpu.VMEM((tokens, group), bf),
            pltpu.VMEM((half, 128), f32),
            pltpu.VMEM((2, half, tokens), f32),
            pltpu.VMEM((2, half, tokens), bf),
            pltpu.VMEM((events, width), bf),
            pltpu.VMEM((events, inner), bf),
            pltpu.VMEM((tokens, 128), f32),
            pltpu.VMEM((tokens, 128), f32),
            sems(2 + (inner + ff) // width),
            sems(row_count),
            sems(row_count),
            sems(hops),
            sems(hops),
            sems(hops),
            sems(hops),
        ],
        name="layer",
        compiler_params=pltpu.CompilerParams(collective_id=5, has_side_effects=True, vmem_limit_bytes=60 * 2**20),
    )(lengths, items, targets, correction, qkv, out, up, down, positions, gains)


def small_kernel(dp_count, row_count, part, summed, by_row, by_dp, send_sem, recv_sem):
    dp = lax.axis_index("dp")
    row = lax.axis_index("rows")
    barrier = pltpu.get_barrier_semaphore()
    row_places = [lax.rem(row + k, row_count) for k in range(1, row_count)]
    dp_places = [lax.rem(dp + k, dp_count) for k in range(1, dp_count)]
    for other in row_places:
        pl.semaphore_signal(barrier, inc=1, device_id=(dp, other), device_id_type=MESH)
    for other in dp_places:
        pl.semaphore_signal(barrier, inc=1, device_id=(other, row), device_id_type=MESH)
    pl.semaphore_wait(barrier, row_count + dp_count - 2)

    def spread(source, landing, mine, others, where, base):
        sends = []
        for k, other in enumerate(others):
            copy = pltpu.make_async_remote_copy(
                source, landing.at[mine], send_sem.at[base + k], recv_sem.at[base + mine],
                device_id=where(other), device_id_type=MESH,
            )
            copy.start()
            sends.append(copy)
        landing[mine] = source[...]
        for other in others:
            pltpu.make_async_remote_copy(
                source, landing.at[other], send_sem.at[base], recv_sem.at[base + other],
                device_id=where(other), device_id_type=MESH,
            ).wait_recv()
        for copy in sends:
            copy.wait_send()

    spread(part, by_row, row, row_places, lambda other: (dp, other), 0)
    summed[...] = jnp.sum(by_row[...], axis=0)
    spread(summed, by_dp, dp, dp_places, lambda other: (other, row), row_count)
    summed[...] = jnp.sum(by_dp[...], axis=0)


def small_sum(dp_count, row_count, part):
    return pl.pallas_call(
        functools.partial(small_kernel, dp_count, row_count),
        out_shape=jax.ShapeDtypeStruct(part.shape, part.dtype),
        in_specs=[VMEM],
        out_specs=VMEM,
        scratch_shapes=[
            pltpu.VMEM((row_count,) + part.shape, part.dtype),
            pltpu.VMEM((dp_count,) + part.shape, part.dtype),
            pltpu.SemaphoreType.DMA((row_count + dp_count,)),
            pltpu.SemaphoreType.DMA((row_count + dp_count,)),
        ],
        name="small_sum",
        compiler_params=pltpu.CompilerParams(collective_id=4, has_side_effects=True),
    )(part)


def grouped_layer(fetched, valid_pos, lengths, correction, weights, positions, gains):
    qkv_weight, out_weight, up_weight, down_weight = weights
    micro, tokens = valid_pos.shape
    histories = lengths.shape[1]
    length, width = positions.shape
    matrices = (rounded(qkv_weight), rounded(out_weight), rounded(up_weight), rounded(down_weight))
    scaling = math.sqrt(width)
    offset = lax.axis_index("rows") * tokens
    running = [
        jnp.zeros_like(qkv_weight),
        jnp.zeros_like(out_weight),
        jnp.zeros_like(up_weight),
        jnp.zeros_like(down_weight),
    ]
    grad_positions = jnp.zeros_like(positions)
    grad_gains = jnp.zeros_like(gains)
    loss_local = jnp.zeros((), jnp.float32)
    embed_grads = []
    target_grads = []
    for micro_index in range(micro):
        lengths_here = lengths[micro_index]
        valid_here = valid_pos[micro_index].astype(jnp.float32)
        embedded = scaling * fetched[0, micro_index].astype(jnp.float32) + jnp.tile(
            positions, (histories, 1)
        )
        output, saved_state = layer_forward(embedded, lengths_here, matrices, gains, HEADS)
        normed_three, back_three = jax.vjp(rms_norm, output, gains[2])
        query_low = rounded(normed_three)
        bias_low = jnp.where(
            valid_pos[micro_index],
            rounded(-correction[micro_index].reshape(-1)),
            jnp.asarray(MASKED, jnp.bfloat16),
        )
        candidates, cand_bias = (
            lax.all_gather(fetched[1, micro_index], "rows", axis=0, tiled=True),
            lax.all_gather(bias_low, "rows", axis=0, tiled=True),
        )
        loss_part, grad_logits, log_total = candidate_loss(
            query_low, candidates, cand_bias, valid_here, offset
        )
        loss_local = loss_local + loss_part
        grad_output, gain_three = back_three(matmul(grad_logits, candidates))
        target_grads.append(
            lax.psum_scatter(
                inner_rows(grad_logits, query_low).astype(jnp.bfloat16),
                "rows",
                scatter_dimension=0,
                tiled=True,
            ).astype(jnp.float32)
        )
        grad_embedded, grad_layer, gain_pair = layer_backward(
            grad_output, saved_state, lengths_here, matrices, HEADS
        )
        for which_one in range(4):
            running[which_one] = running[which_one] + grad_layer[which_one]
        grad_positions = grad_positions + jnp.sum(
            grad_embedded.reshape(histories, length, width), axis=0
        )
        grad_gains = grad_gains + jnp.stack([gain_pair[0], gain_pair[1], gain_three])
        embed_grads.append(scaling * grad_embedded)
    target_part = jnp.stack(target_grads)
    row_grads = jnp.concatenate([jnp.stack(embed_grads), target_part]).reshape(-1, width)
    return running, grad_positions, rounded(row_grads), grad_gains, loss_local


def local(
    item_ids,
    targets,
    lengths,
    correction,
    item_row,
    item_table,
    qkv_weight,
    out_weight,
    up_weight,
    down_weight,
    positions,
    gains,
    item_table_first,
    qkv_weight_first,
    out_weight_first,
    up_weight_first,
    down_weight_first,
    positions_first,
    gains_first,
    item_table_second,
    qkv_weight_second,
    out_weight_second,
    up_weight_second,
    down_weight_second,
    positions_second,
    gains_second,
):
    micro, histories, length = item_ids.shape
    rows_here, width = item_table.shape
    devices = lax.axis_size("dp") * lax.axis_size("rows")
    tokens = histories * length
    requests = 2 * micro * tokens
    capacity = 3 * (requests + devices) // (2 * devices) + 1
    used = -(-capacity // 8) * 8
    capacity = -(-capacity // 16) * 16
    dp_count, row_count = lax.axis_size("dp"), lax.axis_size("rows")
    position = jnp.arange(length, dtype=jnp.int32)
    valid_pos = (position[None, None, :] < lengths[:, :, None]).reshape(micro, tokens)
    wanted = jnp.where(
        valid_pos.reshape(1, -1), jnp.stack([item_ids, targets]).reshape(2, micro * tokens), -1
    ).reshape(requests, 1)
    fetched, slots, received = lookup(
        dp_count, row_count, capacity, used, wanted, item_row, item_table
    )
    received = received[:, 0, :capacity].reshape(1, devices * capacity)
    fetched = fetched.reshape(2, micro, tokens, width)
    fits = histories == 1 and micro == 2 and row_count * tokens <= 4096
    if fits:
        outs = layer(
            row_count,
            lengths.reshape(micro),
            fetched[0].reshape(micro * tokens, width),
            fetched[1].reshape(micro * tokens, width),
            correction.reshape(micro, tokens),
            (qkv_weight, out_weight, up_weight, down_weight),
            positions,
            gains,
        )
        running = outs[:4]
        grad_positions, row_grads, small = outs[4:]
        grad_gains, loss_local, count_local = small[:3], small[3, 0], small[4, 0]
    else:
        running, grad_positions, row_grads, grad_gains, loss_local = grouped_layer(
            fetched,
            valid_pos,
            lengths,
            correction,
            (qkv_weight, out_weight, up_weight, down_weight),
            positions,
            gains,
        )
        count_local = jnp.sum(valid_pos.astype(jnp.float32))
    incoming, gathered, square = tail_exchange(
        dp_count,
        row_count,
        capacity,
        running[0],
        running[1],
        running[2],
        running[3],
        grad_positions,
        row_grads,
        slots,
    )
    table_grad, table_square = table_gradient(
        rows_here, received, incoming.reshape(devices * capacity, width)
    )
    own_square = jnp.sum(table_square[0] + square[0])
    scalars = jnp.stack([loss_local, count_local, own_square])
    part = jnp.concatenate(
        [grad_gains.reshape(-1), jnp.pad(scalars, (0, 1024 - grad_gains.size - 3))]
    ).reshape(8, 128)
    small = small_sum(dp_count, row_count, part).reshape(-1)
    sum_gains = small[: grad_gains.size].reshape(grad_gains.shape)
    sum_loss, sum_count, square_total = (small[grad_gains.size + k] for k in range(3))
    gathered = gathered.astype(jnp.float32)
    place = 0
    blocks = []
    for like in (qkv_weight, up_weight):
        count = like.shape[1] // width
        piece = gathered[place : place + count * like.shape[0]]
        blocks.append(
            jnp.concatenate(
                [piece[c * like.shape[0] : (c + 1) * like.shape[0]] for c in range(count)], axis=1
            )
        )
        place += count * like.shape[0]
    for like in (out_weight, down_weight, positions):
        blocks.append(gathered[place : place + like.shape[0]])
        place += like.shape[0]
    gradients = (table_grad, blocks[0], blocks[2], blocks[1], blocks[3], blocks[4], sum_gains)
    grad_norm = jnp.sqrt(square_total + jnp.sum(sum_gains * sum_gains))
    factor = CLIP / jnp.maximum(grad_norm, CLIP)
    weights = (item_table, qkv_weight, out_weight, up_weight, down_weight, positions, gains)
    firsts = (
        item_table_first,
        qkv_weight_first,
        out_weight_first,
        up_weight_first,
        down_weight_first,
        positions_first,
        gains_first,
    )
    seconds = (
        item_table_second,
        qkv_weight_second,
        out_weight_second,
        up_weight_second,
        down_weight_second,
        positions_second,
        gains_second,
    )
    rates = (RATE, RATE, RATE, RATE, RATE, RATE, GAIN_RATE)
    decays = (DECAY, DECAY, DECAY, DECAY, DECAY, DECAY, 0.0)
    updated = [
        adam_step(
            weights[which_one],
            factor * gradients[which_one],
            firsts[which_one],
            seconds[which_one],
            rates[which_one],
            decays[which_one],
        )
        for which_one in range(7)
    ]
    return (
        updated[0][0],
        updated[1][0],
        updated[2][0],
        updated[3][0],
        updated[4][0],
        updated[5][0],
        updated[6][0],
        updated[0][1],
        updated[1][1],
        updated[2][1],
        updated[3][1],
        updated[4][1],
        updated[5][1],
        updated[6][1],
        updated[0][2],
        updated[1][2],
        updated[2][2],
        updated[3][2],
        updated[4][2],
        updated[5][2],
        updated[6][2],
        sum_loss,
        sum_count,
        grad_norm,
    )


def solution(mesh):
    placed = (
        P(None, ("dp", "rows"), None),
        P(None, ("dp", "rows"), None),
        P(None, ("dp", "rows")),
        P(None, ("dp", "rows"), None),
        P(),
        P(("dp", "rows"), None),
        P(),
        P(),
        P(),
        P(),
        P(),
        P(),
        P(("dp", "rows"), None),
        P(),
        P(),
        P(),
        P(),
        P(),
        P(),
        P(("dp", "rows"), None),
        P(),
        P(),
        P(),
        P(),
        P(),
        P(),
    )
    return jax.shard_map(
        local,
        mesh=mesh,
        in_specs=placed,
        out_specs=(
            P(("dp", "rows"), None),
            P(),
            P(),
            P(),
            P(),
            P(),
            P(),
            P(("dp", "rows"), None),
            P(),
            P(),
            P(),
            P(),
            P(),
            P(),
            P(("dp", "rows"), None),
            P(),
            P(),
            P(),
            P(),
            P(),
            P(),
            P(),
            P(),
            P(),
        ),
        check_vma=False,
    )
```

```python
import functools
import math

import jax
import jax.numpy as jnp
from jax import lax
from jax.experimental import pallas as pl
from jax.experimental.pallas import tpu as pltpu
from jax.sharding import PartitionSpec as P

MESH = pl.DeviceIdType.MESH
VMEM = pl.BlockSpec(memory_space=pltpu.VMEM)
HEADS = 8
STEP = 10


NORM_EPS = 1e-06
MASKED = -1e30
BETA_ONE = 0.9
BETA_TWO = 0.999
ADAM_EPS = 1e-08
DECAY = 0.01
RATE = 0.1
GAIN_RATE = 1.0
CLIP = 1.0


def rounded(values):
    return values.astype(jnp.bfloat16)


def matmul(first_op, second_op):
    return jnp.dot(first_op, second_op, preferred_element_type=jnp.float32)


def inner_rows(first_op, second_op):
    return lax.dot_general(
        first_op, second_op, (((0,), (0,)), ((), ())), preferred_element_type=jnp.float32
    )


def inner_cols(first_op, second_op):
    return lax.dot_general(
        first_op, second_op, (((1,), (1,)), ((), ())), preferred_element_type=jnp.float32
    )


def rms_norm(values, gain_row):
    return (
        values * lax.rsqrt(jnp.mean(values * values, axis=-1, keepdims=True) + NORM_EPS) * gain_row
    )


def gelu_tanh(values):
    return jax.nn.gelu(values)


def split_heads(joined, histories, head_count):
    pieces = joined.reshape(histories, joined.shape[0] // histories, 3, head_count, -1)
    return (pieces[:, :, 0], pieces[:, :, 1], pieces[:, :, 2])


def masked_scores(queries, key_rows, lengths_here):
    length = queries.shape[1]
    scaling = queries.shape[-1] ** (-0.5)
    scores = (
        jnp.einsum("sqhe,skhe->shqk", queries, key_rows, preferred_element_type=jnp.float32)
        * scaling
    )
    position = jnp.arange(length, dtype=jnp.int32)
    allowed = (position[None, :] <= position[:, None])[None, None] & (
        position[None, None, None, :] < lengths_here[:, None, None, None]
    )
    return jnp.where(allowed, scores, MASKED)


def attention_forward(joined, lengths_here, head_count):
    queries, key_rows, value_rows = split_heads(joined, lengths_here.shape[0], head_count)
    scores = masked_scores(queries, key_rows, lengths_here)
    highest = jnp.max(scores, axis=-1, keepdims=True)
    log_total = highest + jnp.log(jnp.sum(jnp.exp(scores - highest), axis=-1, keepdims=True))
    probabilities = rounded(jnp.exp(scores - log_total))
    attended = jnp.einsum(
        "shqk,skhe->sqhe", probabilities, value_rows, preferred_element_type=jnp.float32
    )
    return (attended.reshape(joined.shape[0], -1), log_total)


def attention_backward(joined, log_total, lengths_here, grad_attended, head_count):
    queries, key_rows, value_rows = split_heads(joined, lengths_here.shape[0], head_count)
    probabilities = jnp.exp(masked_scores(queries, key_rows, lengths_here) - log_total)
    grad_heads = grad_attended.reshape(queries.shape)
    grad_probs = jnp.einsum(
        "sqhe,skhe->shqk", grad_heads, value_rows, preferred_element_type=jnp.float32
    )
    grad_values = jnp.einsum(
        "shqk,sqhe->skhe", rounded(probabilities), grad_heads, preferred_element_type=jnp.float32
    )
    row_inner = jnp.sum(probabilities * grad_probs, axis=-1, keepdims=True)
    grad_scores = rounded(probabilities * (grad_probs - row_inner))
    scaling = queries.shape[-1] ** (-0.5)
    grad_queries = (
        jnp.einsum("shqk,skhe->sqhe", grad_scores, key_rows, preferred_element_type=jnp.float32)
        * scaling
    )
    grad_keys = (
        jnp.einsum("shqk,sqhe->skhe", grad_scores, queries, preferred_element_type=jnp.float32)
        * scaling
    )
    stacked = jnp.stack([grad_queries, grad_keys, grad_values], axis=2)
    return stacked.reshape(joined.shape[0], -1)


def layer_forward(embedded, lengths_here, matrices, gains, head_count):
    qkv_low, out_low, up_low, down_low = matrices
    normed_one, back_one = jax.vjp(rms_norm, embedded, gains[0])
    hidden_one = rounded(normed_one)
    joined = rounded(matmul(hidden_one, qkv_low))
    attended, log_total = attention_forward(joined, lengths_here, head_count)
    attended_low = rounded(attended)
    middle = embedded + matmul(attended_low, out_low)
    normed_two, back_two = jax.vjp(rms_norm, middle, gains[1])
    hidden_two = rounded(normed_two)
    upward = matmul(hidden_two, up_low)
    active, back_active = jax.vjp(gelu_tanh, upward)
    active_low = rounded(active)
    output = middle + matmul(active_low, down_low)
    return (
        output,
        (
            back_one,
            hidden_one,
            joined,
            log_total,
            attended_low,
            back_two,
            hidden_two,
            back_active,
            active_low,
        ),
    )


def layer_backward(grad_output, saved_state, lengths_here, matrices, head_count):
    (
        back_one,
        hidden_one,
        joined,
        log_total,
        attended_low,
        back_two,
        hidden_two,
        back_active,
        active_low,
    ) = saved_state
    qkv_low, out_low, up_low, down_low = matrices
    grad_branch = rounded(grad_output)
    grad_down = inner_rows(active_low, grad_branch)
    grad_upward = rounded(back_active(inner_cols(grad_branch, down_low))[0])
    grad_up = inner_rows(hidden_two, grad_upward)
    grad_middle, gain_two = back_two(inner_cols(grad_upward, up_low))
    grad_middle = grad_middle + grad_output
    grad_attn = rounded(grad_middle)
    grad_out = inner_rows(attended_low, grad_attn)
    grad_attended = rounded(inner_cols(grad_attn, out_low))
    grad_joined = rounded(
        attention_backward(joined, log_total, lengths_here, grad_attended, head_count)
    )
    grad_qkv = inner_rows(hidden_one, grad_joined)
    grad_embedded, gain_one = back_one(inner_cols(grad_joined, qkv_low))
    return (
        grad_embedded + grad_middle,
        (grad_qkv, grad_out, grad_up, grad_down),
        (gain_one, gain_two),
    )


def candidate_loss(query_low, candidates, cand_bias, valid_here, offset):
    tokens, width = query_low.shape
    block_rows = min(512, tokens)
    blocks = tokens // block_rows
    column = jnp.arange(candidates.shape[0], dtype=jnp.int32)
    bias_wide = cand_bias.astype(jnp.float32)

    def one_block(running, block_pieces):
        query_block, valid_block, start_row = block_pieces
        logits = inner_cols(query_block, candidates) + bias_wide[None]
        highest = jnp.max(logits, axis=1, keepdims=True)
        log_total = highest + jnp.log(jnp.sum(jnp.exp(logits - highest), axis=1, keepdims=True))
        target_hit = (
            column[None, :]
            == (offset + start_row + jnp.arange(block_rows, dtype=jnp.int32))[:, None]
        )
        own_logit = jnp.sum(jnp.where(target_hit, logits, 0.0), axis=1)
        grad_logits = rounded(
            (jnp.exp(logits - log_total) - target_hit.astype(jnp.float32)) * valid_block[:, None]
        )
        return (
            running + jnp.sum(valid_block * (log_total[:, 0] - own_logit)),
            (grad_logits, log_total[:, 0]),
        )

    loss_part, block_out = lax.scan(
        one_block,
        jnp.zeros((), jnp.float32),
        (
            query_low.reshape(blocks, block_rows, width),
            valid_here.reshape(blocks, block_rows),
            jnp.arange(blocks, dtype=jnp.int32) * block_rows,
        ),
    )
    return (loss_part, block_out[0].reshape(tokens, -1), block_out[1].reshape(tokens))


def adam_step(weight, gradient, first, second, rate, decay):
    first_new = BETA_ONE * first + (1.0 - BETA_ONE) * gradient
    second_new = BETA_TWO * second + (1.0 - BETA_TWO) * gradient * gradient
    stepped = (
        first_new
        / (1.0 - BETA_ONE**STEP)
        / (jnp.sqrt(second_new / (1.0 - BETA_TWO**STEP)) + ADAM_EPS)
    )
    return (weight - rate * (stepped + decay * weight), first_new, second_new)


def reduce_rows(total_rows, devices):
    unit = 16 * devices
    return -(-total_rows // unit) * unit


def tail_kernel(dp_count, row_count, padded, capacity, qkv, out, up, down, pos, row_grads, slots, incoming, gathered, square,
                outgoing, acc, low, recv0, recv1, recv2, send_a, recv_a, send_r, recv_r):
    devices = dp_count * row_count
    dp = lax.axis_index("dp")
    row = lax.axis_index("rows")
    me = dp * row_count + row
    bits = row_count.bit_length() - 1
    barrier = pltpu.get_barrier_semaphore()

    def place(k):
        other = lax.rem(me + k, devices)
        return other, (other // row_count, lax.rem(other, row_count))

    def greet(k, carry):
        other, where = place(k)
        pl.semaphore_signal(barrier, inc=1, device_id=where, device_id_type=MESH)
        return carry

    lax.fori_loop(1, devices, greet, 0)
    width = 256
    at = 0
    for ref in (qkv, up):
        for c in range(ref.shape[1] // width):
            acc[pl.ds(at, ref.shape[0]), :] = ref[:, pl.ds(c * width, width)]
            at += ref.shape[0]
    for ref in (out, down, pos):
        acc[pl.ds(at, ref.shape[0]), :] = ref[...]
        at += ref.shape[0]
    if at < padded:
        acc[pl.ds(at, padded - at), :] = jnp.zeros((padded - at, width), jnp.float32)
    pl.semaphore_wait(barrier, devices - 1)

    def a2a_send(k):
        other, where = place(k)
        return pltpu.make_async_remote_copy(
            outgoing.at[other], incoming.at[k], send_a.at[k], recv_a.at[k], device_id=where, device_id_type=MESH)

    def a2a_recv(k):
        other, where = place(k)
        return pltpu.make_async_remote_copy(
            outgoing.at[other], incoming.at[k], send_a.at[k], recv_a.at[k], device_id=where, device_id_type=MESH)

    def partner(bit):
        step = 1 << bit
        mine = lax.rem(row // step, 2)
        return mine, (dp, row + step - 2 * step * mine)

    half = padded // 2
    units = padded // (16 * devices)
    part_rows = [((units + 1) // 2) * 16 * (devices // 2), (units // 2) * 16 * (devices // 2)]
    orders = [list(range(1, bits)), list(range(bits - 1, 0, -1))]
    al = lambda v: pl.multiple_of(v, 16)

    mine, where = partner(0)
    low[pl.ds(al((1 - mine) * half), half), :] = acc[pl.ds(al((1 - mine) * half), half), :].astype(jnp.bfloat16)
    first = pltpu.make_async_remote_copy(low.at[pl.ds(al((1 - mine) * half), half)], recv0, send_r.at[0], recv_r.at[0],
                                         device_id=where, device_id_type=MESH)
    first.start()
    slot_row = jnp.concatenate([slots[c : c + 1, :] for c in range(slots.shape[0])], axis=1)
    slot_index = lax.broadcasted_iota(jnp.int32, (capacity, slot_row.shape[1]), 0).astype(jnp.float32)

    def arrange(other):
        pick = one_hot(slot_index == slot_row - (other * capacity).astype(jnp.float32))
        return jnp.dot(pick, row_grads[...], preferred_element_type=jnp.float32).astype(jnp.bfloat16)

    def send_rows(k, carry):
        other, where = place(k)
        outgoing[other] = arrange(other)
        a2a_send(k).start()
        return carry

    lax.fori_loop(1, devices, send_rows, 0)
    incoming[0] = arrange(me)
    first.wait_recv()
    base = mine * half
    pending = [first]
    starts = [base, base + part_rows[0]]
    sizes = list(part_rows)
    offs = [0, sizes[0]]
    live = [p for p in range(2) if part_rows[p] > 0]
    acc[pl.ds(al(base), half), :] = acc[pl.ds(al(base), half), :] + recv0[...].astype(jnp.float32)
    sem = 1
    scratch_at = 0
    history = []
    for step in range(bits - 1):
        copies = []
        for p in live:
            bit = orders[p][step]
            mine, where = partner(bit)
            size = sizes[p] // 2
            keep = starts[p] + mine * size
            give = starts[p] + (1 - mine) * size
            low[pl.ds(al(give), size), :] = acc[pl.ds(al(give), size), :].astype(jnp.bfloat16)
            landing = recv1.at[pl.ds(scratch_at, size)]
            copy = pltpu.make_async_remote_copy(low.at[pl.ds(al(give), size)], landing, send_r.at[sem], recv_r.at[sem],
                                                device_id=where, device_id_type=MESH)
            copy.start()
            copies.append((p, copy, keep, size, scratch_at, where))
            sem += 1
            scratch_at += size
        for p, copy, keep, size, off, where in copies:
            copy.wait_recv()
            acc[pl.ds(al(keep), size), :] = acc[pl.ds(al(keep), size), :] + recv1[pl.ds(off, size), :].astype(jnp.float32)
            history.append((p, keep, size, where))
            starts[p], sizes[p] = keep, size
            pending.append(copy)
    copies = []
    off = 0
    final = {}
    for p in live:
        size = sizes[p] // dp_count
        for k in range(1, dp_count):
            other = lax.rem(dp + k, dp_count)
            give = starts[p] + other * size
            low[pl.ds(al(give), size), :] = acc[pl.ds(al(give), size), :].astype(jnp.bfloat16)
            copy = pltpu.make_async_remote_copy(low.at[pl.ds(al(give), size)], recv2.at[pl.ds(off, size)], send_r.at[sem], recv_r.at[sem],
                                                device_id=(other, row), device_id_type=MESH)
            copy.start()
            copies.append((p, copy, off, size))
            sem += 1
            off += size
        final[p] = (starts[p] + dp * size, size)
    for p, copy, off, size in copies:
        copy.wait_recv()
        at, size = final[p]
        acc[pl.ds(al(at), size), :] = acc[pl.ds(al(at), size), :] + recv2[pl.ds(off, size), :].astype(jnp.float32)
        pending.append(copy)
    total = jnp.zeros((1, width), jnp.float32)
    for p in live:
        at, size = final[p]
        mine_low = acc[pl.ds(al(at), size), :]
        total = total + jnp.sum(mine_low * mine_low, axis=0, keepdims=True)
        gathered[pl.ds(al(at), size), :] = mine_low.astype(jnp.bfloat16)
    square[...] = jnp.broadcast_to(total, square.shape)

    copies = []
    for p in live:
        at, size = final[p]
        for k in range(1, dp_count):
            other = lax.rem(dp + k, dp_count)
            copy = pltpu.make_async_remote_copy(gathered.at[pl.ds(al(at), size)], gathered.at[pl.ds(al(at), size)], send_r.at[sem], recv_r.at[sem],
                                                device_id=(other, row), device_id_type=MESH)
            copy.start()
            copies.append((p, copy, k, sem))
            sem += 1
    for p, copy, k, s in copies:
        at, size = final[p]
        source = lax.rem(dp + dp_count - k, dp_count)
        land = starts[p] + source * size
        pltpu.make_async_remote_copy(gathered.at[pl.ds(al(at), size)], gathered.at[pl.ds(al(land), size)], send_r.at[s], recv_r.at[s],
                                     device_id=(source, row), device_id_type=MESH).wait_recv()
        pending.append(copy)
    for step in range(bits - 2, -1, -1):
        copies = []
        for p in live:
            bit = orders[p][step]
            mine, where = partner(bit)
            size = sizes[p]
            at = starts[p]
            copy = pltpu.make_async_remote_copy(gathered.at[pl.ds(al(at), size)], gathered.at[pl.ds(al(at), size)], send_r.at[sem], recv_r.at[sem],
                                                device_id=where, device_id_type=MESH)
            copy.start()
            copies.append((p, copy, sem, mine, size, where))
            sem += 1
        for p, copy, s, mine, size, where in copies:
            bottom = starts[p] - mine * size
            land = bottom + (1 - mine) * size
            pltpu.make_async_remote_copy(gathered.at[pl.ds(al(land), size)], gathered.at[pl.ds(al(land), size)], send_r.at[s], recv_r.at[s],
                                         device_id=where, device_id_type=MESH).wait_recv()
            starts[p], sizes[p] = bottom, 2 * size
            pending.append(copy)
    mine, where = partner(0)
    last = pltpu.make_async_remote_copy(gathered.at[pl.ds(al(mine * half), half)], gathered.at[pl.ds(al(mine * half), half)], send_r.at[sem], recv_r.at[sem],
                                        device_id=where, device_id_type=MESH)
    last.start()
    pltpu.make_async_remote_copy(gathered.at[pl.ds(al((1 - mine) * half), half)], gathered.at[pl.ds(al((1 - mine) * half), half)], send_r.at[sem], recv_r.at[sem],
                                 device_id=where, device_id_type=MESH).wait_recv()
    sem += 1
    pending.append(last)
    lax.fori_loop(1, devices, lambda k, c: (a2a_recv(k).wait_recv(), c)[1], 0)
    for copy in pending:
        copy.wait_send()
    lax.fori_loop(1, devices, lambda k, c: (a2a_send(k).wait_send(), c)[1], 0)


def tail_exchange(dp_count, row_count, capacity, qkv, out, up, down, pos, row_grads, slots):
    devices = dp_count * row_count
    width = out.shape[1]
    rows = sum(a.size for a in (qkv, out, up, down, pos)) // width
    padded = reduce_rows(rows, devices)
    bits = row_count.bit_length() - 1
    sems = 2 + 4 * bits + 4 * dp_count + 8
    return pl.pallas_call(
        functools.partial(tail_kernel, dp_count, row_count, padded, capacity),
        out_shape=(jax.ShapeDtypeStruct((devices, capacity, width), jnp.bfloat16), jax.ShapeDtypeStruct((padded, width), jnp.bfloat16),
                   jax.ShapeDtypeStruct((8, width), jnp.float32)),
        in_specs=[VMEM] * 7, out_specs=(VMEM,) * 3,
        scratch_shapes=[
            pltpu.VMEM((devices, capacity, width), jnp.bfloat16),
            pltpu.VMEM((padded, width), jnp.float32),
            pltpu.VMEM((padded, width), jnp.bfloat16),
            pltpu.VMEM((padded // 2, width), jnp.bfloat16),
            pltpu.VMEM((padded // 2, width), jnp.bfloat16),
            pltpu.VMEM((padded // row_count, width), jnp.bfloat16),
            pltpu.SemaphoreType.DMA((devices,)), pltpu.SemaphoreType.DMA((devices,)),
            pltpu.SemaphoreType.DMA((sems,)), pltpu.SemaphoreType.DMA((sems,)),
        ],
        name="tail_exchange",
        compiler_params=pltpu.CompilerParams(collective_id=3, has_side_effects=True, vmem_limit_bytes=56 * 2**20),
    )(qkv, out, up, down, pos, row_grads, slots)


def other_device(k, dp_count, row_count):
    devices = dp_count * row_count
    me = lax.axis_index("dp") * row_count + lax.axis_index("rows")
    other = lax.rem(me + k, devices)
    return other, (other // row_count, lax.rem(other, row_count))


def one_hot(flags):
    return jnp.where(flags, 1.0, 0.0).astype(jnp.bfloat16)


def lookup_kernel(dp_count, row_count, capacity, used, wanted, item_row, table_hbm, fetched, slots, received,
                  table, pieces, slot_col, asked, ask, got, stage, ready, landed, asked_here,
                  table_sem, local_sem, send_q, recv_q, send_a, recv_a):
    devices = dp_count * row_count
    me = lax.axis_index("dp") * row_count + lax.axis_index("rows")
    rows_here = table.shape[0]
    events = wanted.shape[0]
    chunk = 256
    barrier = pltpu.get_barrier_semaphore()
    load_table = pltpu.make_async_copy(table_hbm, table, table_sem)
    load_table.start()

    def greet(k, carry):
        other, where = other_device(k, dp_count, row_count)
        pl.semaphore_signal(barrier, inc=1, device_id=where, device_id_type=MESH)
        return carry

    lax.fori_loop(1, devices, greet, 0)

    whole_rows = item_row.shape[0]
    lanes = item_row.shape[1]
    pieces[pl.ds(whole_rows, pieces.shape[0] - whole_rows), :] = jnp.zeros(
        (pieces.shape[0] - whole_rows, 3 * lanes), jnp.bfloat16
    )
    part = 224
    def cut(c, carry):
        at = pl.multiple_of(c * part, 16)
        values = item_row[pl.ds(at, part), :]
        for digit in range(3):
            piece = jnp.bitwise_and(jnp.right_shift(values, 8 * digit), 255)
            pieces[pl.ds(at, part), digit * lanes : (digit + 1) * lanes] = piece.astype(jnp.float32).astype(jnp.bfloat16)
        return carry
    lax.fori_loop(0, whole_rows // part, cut, 0)

    lane = lax.broadcasted_iota(jnp.int32, (chunk, lanes), 1)
    lane_f = lane.astype(jnp.float32)
    wide = lax.broadcasted_iota(jnp.int32, (chunk, pieces.shape[0]), 1)
    below = one_hot(
        lax.broadcasted_iota(jnp.int32, (chunk, chunk), 1) < lax.broadcasted_iota(jnp.int32, (chunk, chunk), 0)
    )
    diagonal = lax.broadcasted_iota(jnp.int32, (chunk, chunk), 1) == lax.broadcasted_iota(jnp.int32, (chunk, chunk), 0)
    asked[...] = jnp.zeros_like(asked)

    def route(c, counts):
        at = pl.multiple_of(c * chunk, chunk)
        ids = wanted[pl.ds(at, chunk), :]
        high = jnp.right_shift(ids, 7)
        low = jnp.bitwise_and(ids, 127)
        found = jnp.dot(one_hot(wide == high), pieces[...], preferred_element_type=jnp.float32)
        value = found[:, :lanes] + 256.0 * found[:, lanes : 2 * lanes] + 65536.0 * found[:, 2 * lanes :]
        row = jnp.sum(jnp.where(lane == low, value, 0.0), axis=1, keepdims=True)
        owner = jnp.floor((row + 0.5) * (1.0 / rows_here))
        local = row - owner * rows_here
        live = ids >= 0
        owned = jnp.logical_and(lane_f == owner, live)
        owned_low = one_hot(owned)
        before = jnp.dot(below, owned_low, preferred_element_type=jnp.float32) + counts
        rank = jnp.sum(jnp.where(owned, before, 0.0), axis=1, keepdims=True)
        slot = jnp.where(live, owner * capacity + rank, -1.0)
        slot_col[pl.ds(at, chunk), :] = slot
        slots[pl.ds(c, 1), :] = jnp.sum(jnp.where(diagonal, slot, 0.0), axis=0, keepdims=True)
        local_high = jnp.floor(local * (1.0 / 128))
        local_low = local - 128.0 * local_high
        at_rank = lane_f == rank
        both = jnp.concatenate(
            [jnp.where(at_rank, local_high, 0.0), jnp.where(at_rank, local_low, 0.0)], axis=1
        ).astype(jnp.bfloat16)
        asked[...] += lax.dot_general(owned_low, both, (((0,), (0,)), ((), ())), preferred_element_type=jnp.float32)
        return counts + jnp.sum(jnp.where(owned, 1.0, 0.0), axis=0, keepdims=True)

    lax.fori_loop(0, events // chunk, route, jnp.zeros((1, lanes), jnp.float32))
    rows_asked = (128.0 * asked[:, :lanes] + asked[:, lanes:]).astype(jnp.int32)
    for d in range(devices):
        ask[d] = rows_asked[d : d + 1, :]
    pl.semaphore_wait(barrier, devices - 1)

    def query(k, at_other):
        other, where = other_device(k, dp_count, row_count)
        return pltpu.make_async_remote_copy(
            ask.at[other], got.at[other if at_other else me], send_q.at[k], recv_q.at[other if at_other else me],
            device_id=where, device_id_type=MESH,
        )

    def answer(k, at_other):
        other, where = other_device(k, dp_count, row_count)
        place = pl.multiple_of((other if at_other else me) * capacity, 16)
        return pltpu.make_async_remote_copy(
            ready.at[k], landed.at[pl.ds(place, capacity)], send_a.at[k], recv_a.at[other if at_other else me],
            device_id=where, device_id_type=MESH,
        )

    lax.fori_loop(1, devices, lambda k, c: (query(k, False).start(), c)[1], 0)
    got[me] = ask[me]
    stage[...] = jnp.zeros_like(stage)
    load_table.wait()
    lax.fori_loop(1, devices, lambda k, c: (query(k, True).wait_recv(), c)[1], 0)
    got[...] = jnp.clip(got[...], 0, rows_here - 1)
    to_scalars = pltpu.make_async_copy(got, asked_here, local_sem)
    to_scalars.start()

    def by_distance(k, carry):
        received[k] = got[lax.rem(me + devices - k, devices)]
        return carry

    lax.fori_loop(0, devices, by_distance, 0)
    to_scalars.wait()

    def gather(source):
        def some(c, carry):
            at = pl.multiple_of(c * 8, 8)
            for j in range(8):
                row = asked_here[source, 0, at + j]
                stage[pl.ds(at + j, 1), :] = table[pl.ds(row, 1), :]
            return carry
        lax.fori_loop(0, used // 8, some, 0)
        return stage[...].astype(jnp.bfloat16)

    def reply(k, carry):
        other, where = other_device(k, dp_count, row_count)
        ready[k] = gather(other)
        answer(k, False).start()
        return carry

    lax.fori_loop(1, devices, reply, 0)
    landed[pl.ds(pl.multiple_of(me * capacity, 16), capacity), :] = gather(me)
    lax.fori_loop(1, devices, lambda k, c: (answer(k, True).wait_recv(), c)[1], 0)

    slot_lane = lax.broadcasted_iota(jnp.int32, (chunk, devices * capacity), 1).astype(jnp.float32)

    def settle(c, carry):
        at = pl.multiple_of(c * chunk, chunk)
        pick = one_hot(slot_lane == slot_col[pl.ds(at, chunk), :])
        fetched[pl.ds(at, chunk), :] = jnp.dot(pick, landed[...], preferred_element_type=jnp.float32).astype(jnp.bfloat16)
        return carry

    lax.fori_loop(0, events // chunk, settle, 0)
    lax.fori_loop(1, devices, lambda k, c: (query(k, False).wait_send(), c)[1], 0)
    lax.fori_loop(1, devices, lambda k, c: (answer(k, False).wait_send(), c)[1], 0)


def lookup(dp_count, row_count, capacity, used, wanted, item_row, item_table):
    devices = dp_count * row_count
    events = wanted.shape[0]
    lanes = 128
    width = item_table.shape[1]
    blocks = item_row.shape[0] // lanes
    return pl.pallas_call(
        functools.partial(lookup_kernel, dp_count, row_count, capacity, used),
        out_shape=(
            jax.ShapeDtypeStruct((events, width), jnp.bfloat16),
            jax.ShapeDtypeStruct((events // 256, 256), jnp.float32),
            jax.ShapeDtypeStruct((devices, 1, lanes), jnp.int32),
        ),
        in_specs=[VMEM, VMEM, pl.BlockSpec(memory_space=pl.ANY)],
        out_specs=(VMEM,) * 3,
        scratch_shapes=[
            pltpu.VMEM(item_table.shape, jnp.float32),
            pltpu.VMEM((-(-blocks // lanes) * lanes, 3 * lanes), jnp.bfloat16),
            pltpu.VMEM((events, 1), jnp.float32),
            pltpu.VMEM((lanes, 2 * lanes), jnp.float32),
            pltpu.VMEM((devices, 1, lanes), jnp.int32),
            pltpu.VMEM((devices, 1, lanes), jnp.int32),
            pltpu.VMEM((capacity, width), jnp.float32),
            pltpu.VMEM((devices, capacity, width), jnp.bfloat16),
            pltpu.VMEM((devices * capacity, width), jnp.bfloat16),
            pltpu.SMEM((devices, 1, lanes), jnp.int32),
            pltpu.SemaphoreType.DMA,
            pltpu.SemaphoreType.DMA,
            pltpu.SemaphoreType.DMA((devices,)),
            pltpu.SemaphoreType.DMA((devices,)),
            pltpu.SemaphoreType.DMA((devices,)),
            pltpu.SemaphoreType.DMA((devices,)),
        ],
        name="lookup",
        compiler_params=pltpu.CompilerParams(collective_id=2, has_side_effects=True, vmem_limit_bytes=56 * 2**20),
    )(wanted, item_row.reshape(-1, lanes), item_table)


def table_kernel(received, incoming, grads, square):
    tile, width = grads.shape
    step = pl.program_id(0)
    rows = lax.broadcasted_iota(jnp.int32, (tile, received.shape[1]), 0) + step * tile
    grad = jnp.dot(one_hot(rows == received[...]), incoming[...], preferred_element_type=jnp.float32)
    grads[...] = grad

    @pl.when(step == 0)
    def start():
        square[...] = jnp.zeros_like(square)

    square[...] += jnp.broadcast_to(jnp.sum(grad * grad, axis=0, keepdims=True), square.shape)


def table_gradient(rows_here, received, incoming):
    width = incoming.shape[1]
    tile = 224
    return pl.pallas_call(
        table_kernel,
        grid=(rows_here // tile,),
        out_shape=(
            jax.ShapeDtypeStruct((rows_here, width), jnp.float32),
            jax.ShapeDtypeStruct((8, width), jnp.float32),
        ),
        in_specs=[
            pl.BlockSpec(received.shape, lambda i: (0, 0)),
            pl.BlockSpec(incoming.shape, lambda i: (0, 0)),
        ],
        out_specs=(
            pl.BlockSpec((tile, width), lambda i: (i, 0)),
            pl.BlockSpec((8, width), lambda i: (0, 0)),
        ),
        name="table_gradient",
        compiler_params=pltpu.CompilerParams(vmem_limit_bytes=40 * 2**20),
    )(received, incoming)


def dot_nn(first_op, second_op):
    return jnp.dot(first_op, second_op, preferred_element_type=jnp.float32)


def dot_nt(first_op, second_op):
    return lax.dot_general(
        first_op, second_op, (((1,), (1,)), ((), ())), preferred_element_type=jnp.float32
    )


def dot_tn(first_op, second_op):
    return lax.dot_general(
        first_op, second_op, (((0,), (0,)), ((), ())), preferred_element_type=jnp.float32
    )


def inverse_rms(values):
    return lax.rsqrt(jnp.mean(values * values, axis=-1, keepdims=True) + NORM_EPS)


def rms_back(values, gain_row, grad):
    scale = inverse_rms(values)
    grad_scaled = grad * gain_row
    inner = jnp.mean(values * grad_scaled, axis=-1, keepdims=True)
    gain_part = jnp.sum(grad * values * scale, axis=0, keepdims=True)
    return scale * grad_scaled - values * (scale * scale * scale * inner), gain_part


def subsets(bits):
    found = [()]
    for bit in bits:
        found = found + [one + (bit,) for one in found]
    return found


def flip(index, bits):
    for bit in bits:
        step = 1 << bit
        index = index + step - 2 * step * lax.rem(index // step, 2)
    return index


def layer_kernel(dp_count, row_count, capacity, rows_here, lengths, items, targets, correction, qkv_hbm, out_hbm,
                 up_hbm, down_hbm, positions, gains, slots, received,
                 table_grads, gathered, summed,
                 qkv_low, out_low, up_low, down_low, embedded, hidden_one, joined, probs_top, probs_low, attended,
                 middle, hidden_two, slope, active, output, query, cand, bias, cand_grads, landing, logits,
                 grad_logits, highest, row_grads, small, acc, got_sums, incoming, by_row, by_dp, row_small, part_k, part_v,
                 load_sem, send_b, recv_b, send_g, recv_g, send_s, recv_s, send_r, recv_r, send_a, recv_a,
                 send_n, recv_n, store_sem):
    devices = dp_count * row_count
    micro = 2
    tokens = positions.shape[0]
    half = tokens // 2
    width = positions.shape[1]
    inner = out_low.shape[0]
    bits = row_count.bit_length() - 1
    dp = lax.axis_index("dp")
    row = lax.axis_index("rows")
    bf = jnp.bfloat16
    barrier = pltpu.get_barrier_semaphore()

    def greet(k, carry):
        other, where = other_device(k, dp_count, row_count)
        pl.semaphore_signal(barrier, inc=1, device_id=where, device_id_type=MESH)
        return carry

    lax.fori_loop(1, devices, greet, 0)
    ff = up_low.shape[1]
    loads = [
        (qkv_hbm, 0, 0, 3 * inner, qkv_low),
        (up_hbm, 0, 3 * inner, ff, up_low),
    ]
    at = 3 * inner + ff
    for source, low in ((out_hbm, out_low), (down_hbm, down_low)):
        for k in range(source.shape[0] // width):
            loads.append((source, k * width, at, width, low))
            at += width
    copies = []
    for k, (source, first, at, count, low) in enumerate(loads):
        copy = pltpu.make_async_copy(
            source.at[pl.ds(first, width)], logits.at[:, pl.ds(at, count)], load_sem.at[k]
        )
        copy.start()
        copies.append(copy)

    column = lax.broadcasted_iota(jnp.int32, (1, tokens), 1)
    for m in range(micro):
        own_bias = jnp.where(
            column < lengths[m], (-correction[m : m + 1, :]).astype(bf).astype(jnp.float32), MASKED
        )
        bias[row, m : m + 1, :] = own_bias.astype(bf).astype(jnp.float32)
        cand[pl.ds(pl.multiple_of((m * row_count + row) * tokens, tokens), tokens), :] = targets[m * tokens : (m + 1) * tokens, :]
    pl.semaphore_wait(barrier, devices - 1)

    pending = []
    gathers = []
    for k in range(1, row_count):
        copy = pltpu.make_async_remote_copy(
            bias.at[row], bias.at[row], send_b.at[k], recv_b.at[row],
            device_id=(dp, lax.rem(row + k, row_count)), device_id_type=MESH,
        )
        copy.start()
        pending.append(copy)

    orders = [list(range(1, bits)) + [0], list(range(bits - 1, 0, -1)) + [0]]
    block_of = lambda ref, m, owner: ref.at[pl.ds(pl.multiple_of((m * row_count + owner) * tokens, tokens), tokens)]
    gather_steps = []
    count = 0
    for step in range(bits):
        here = []
        for m in range(micro):
            for mask in subsets(orders[m][:step]):
                here.append((m, orders[m][step], mask, count))
                count += 1
        gather_steps.append(here)

    def gather_start(step):
        for m, bit, mask, sem in gather_steps[step]:
            mine = flip(row, mask)
            copy = pltpu.make_async_remote_copy(
                block_of(cand, m, mine), block_of(cand, m, mine), send_g.at[sem], recv_g.at[sem],
                device_id=(dp, flip(row, (bit,))), device_id_type=MESH,
            )
            copy.start()
            gathers.append(copy)

    def gather_wait(step):
        for m, bit, mask, sem in gather_steps[step]:
            theirs = flip(flip(row, (bit,)), mask)
            pltpu.make_async_remote_copy(
                block_of(cand, m, theirs), block_of(cand, m, theirs), send_g.at[sem], recv_g.at[sem],
                device_id=(dp, flip(row, (bit,))), device_id_type=MESH,
            ).wait_recv()

    gather_start(0)

    scatter_orders = [[0] + list(range(1, bits)), [0] + list(range(bits - 1, 0, -1))]
    scatter_steps = []
    count = 0
    for m in range(micro):
        levels = []
        for step in range(bits):
            bit = scatter_orders[m][step]
            levels.append([(bit, mask, count + i) for i, mask in enumerate(subsets(scatter_orders[m][step + 1 :]))])
            count += len(levels[-1])
        scatter_steps.append(levels)

    def scatter_start(m, step):
        for bit, mask, sem in scatter_steps[m][step]:
            there = flip(row, (bit,))
            copy = pltpu.make_async_remote_copy(
                block_of(cand_grads, m, flip(there, mask)), landing.at[sem], send_s.at[sem], recv_s.at[sem],
                device_id=(dp, there), device_id_type=MESH,
            )
            copy.start()
            pending.append(copy)

    def scatter_wait(m, step):
        for bit, mask, sem in scatter_steps[m][step]:
            there = flip(row, (bit,))
            pltpu.make_async_remote_copy(
                block_of(cand_grads, m, flip(row, mask)), landing.at[sem], send_s.at[sem], recv_s.at[sem],
                device_id=(dp, there), device_id_type=MESH,
            ).wait_recv()
            base = (m * row_count + flip(row, mask)) * tokens
            last = step == bits - 1

            def add(c, carry):
                at = pl.multiple_of(base + c * 64, 64)
                near = pl.multiple_of(c * 64, 64)
                total = cand_grads[pl.ds(at, 64), :].astype(jnp.float32) + landing[sem, pl.ds(near, 64), :].astype(jnp.float32)
                if last:
                    row_grads[pl.ds(pl.multiple_of((micro + m) * tokens + c * 64, 64), 64), :] = total.astype(bf)
                else:
                    cand_grads[pl.ds(at, 64), :] = total.astype(bf)
                return carry

            lax.fori_loop(0, tokens // 64, add, 0)

    for copy, (source, first, at, count, low) in zip(copies, loads):
        copy.wait()
    for source, first, at, count, low in loads:
        low[pl.ds(first, width), :] = logits[:, pl.ds(at, count)].astype(bf)

    chunks = micro * 2
    gain_one, gain_two, gain_three = gains[0:1, :], gains[1:2, :], gains[2:3, :]
    scaling = math.sqrt(width)

    def project(c, carry):
        at = pl.multiple_of(c * half, half)
        near = pl.multiple_of(lax.rem(c, 2) * half, half)
        values = scaling * items[pl.ds(at, half), :].astype(jnp.float32) + positions[pl.ds(near, half), :]
        embedded[pl.ds(at, half), :] = values
        normed = (values * inverse_rms(values) * gain_one).astype(bf)
        hidden_one[pl.ds(at, half), :] = normed
        joined[pl.ds(at, half), :inner] = (dot_nn(normed, qkv_low[:, :inner]).astype(bf) * bf(0.125))
        joined[pl.ds(at, half), inner:] = dot_nn(normed, qkv_low[:, inner:]).astype(bf)
        return carry

    lax.fori_loop(0, chunks, project, 0)
    gather_wait(0)
    gather_start(1)

    lane = lax.broadcasted_iota(jnp.int32, (1, 128), 1)
    head_mask = [jnp.where(lane < 64, 1.0, 0.0).astype(bf), jnp.where(lane < 64, 0.0, 1.0).astype(bf)]
    pairs = inner // 128
    sub = 32

    def attend(m):
        masked_row = jnp.where(column < lengths[m], 0.0, MASKED)
        base = m * tokens

        def pair(hp, carry):
            lanes = [pl.ds(pl.multiple_of(k * inner + hp * 128, 128), 128) for k in range(3)]
            keys = joined[base : base + tokens, lanes[1]]
            values = joined[base : base + tokens, lanes[2]]
            for rb in range(2):
                first = base + rb * half
                span = (rb + 1) * half
                probs = probs_low if rb else probs_top
                queries = joined[first : first + half, lanes[0]]
                for h in range(2):
                    logits[:, h * tokens : h * tokens + span] = dot_nt(queries * head_mask[h], keys[:span])
                for h in range(2):
                    for s in range(half // sub):
                        value = logits[s * sub : (s + 1) * sub, h * tokens : h * tokens + span] + masked_row[:, :span]
                        allowed = (
                            lax.broadcasted_iota(jnp.int32, (sub, half), 1)
                            <= lax.broadcasted_iota(jnp.int32, (sub, half), 0) + s * sub
                        )
                        corner = jnp.where(allowed, value[:, rb * half :], MASKED)
                        value = jnp.concatenate([value[:, :half], corner], axis=1) if rb else corner
                        value = jnp.exp(value - jnp.max(value, axis=1, keepdims=True))
                        value = value * (1.0 / jnp.sum(value, axis=1, keepdims=True))
                        probs[m * 2 * pairs + hp * 2 + h, s * sub : (s + 1) * sub, :] = value.astype(bf)
                total = dot_nn(probs[m * 2 * pairs + hp * 2], values[:span] * head_mask[0]) + dot_nn(
                    probs[m * 2 * pairs + hp * 2 + 1], values[:span] * head_mask[1]
                )
                attended[first : first + half, pl.ds(pl.multiple_of(hp * 128, 128), 128)] = total.astype(bf)
            return carry

        lax.fori_loop(0, pairs, pair, 0)

    attend(0)
    gather_wait(1)
    for step in range(2, bits):
        gather_start(step)
        if step < bits - 1:
            gather_wait(step)
    attend(1)

    gelu_scale = math.sqrt(2.0 / math.pi)

    def feed(c, carry):
        at = pl.multiple_of(c * half, half)
        values = embedded[pl.ds(at, half), :] + dot_nn(attended[pl.ds(at, half), :], out_low[...])
        middle[pl.ds(at, half), :] = values
        normed = (values * inverse_rms(values) * gain_two).astype(bf)
        hidden_two[pl.ds(at, half), :] = normed
        logits[:, :ff] = dot_nn(normed, up_low[...])

        def bend(s, carry):
            for part in range(2):
                near = pl.multiple_of(s * 32 + part * 16, 16)
                there = pl.multiple_of(at + s * 32 + part * 16, 16)
                upward = logits[pl.ds(near, 16), :ff]
                square = upward * upward
                bent = jnp.tanh(gelu_scale * upward * (1.0 + 0.044715 * square))
                active[pl.ds(there, 16), :] = (0.5 * upward * (1.0 + bent)).astype(bf)
                slope[pl.ds(there, 16), :] = 0.5 * (1.0 + bent) + 0.5 * gelu_scale * upward * (1.0 - bent * bent) * (
                    1.0 + 3.0 * 0.044715 * square
                )
            return carry

        lax.fori_loop(0, half // 32, bend, 0)
        values = values + dot_nn(active[pl.ds(at, half), :], down_low[...])
        output[pl.ds(at, half), :] = values
        query[pl.ds(at, half), :] = (values * inverse_rms(values) * gain_three).astype(bf)
        return carry

    lax.fori_loop(0, chunks, feed, 0)
    gather_wait(bits - 1)
    for k in range(1, row_count):
        other = lax.rem(row + k, row_count)
        pltpu.make_async_remote_copy(
            bias.at[other], bias.at[other], send_b.at[k], recv_b.at[other],
            device_id=(dp, other), device_id_type=MESH,
        ).wait_recv()

    block = 512
    blocks = row_count * tokens // block
    fine = 16

    def loss_of(m):
        length = lengths[m]

        def one_half(rh, carry):
            first = pl.multiple_of(m * tokens + rh * half, half)
            queries = query[pl.ds(first, half), :]
            highest[...] = jnp.full_like(highest, -3.0e38)

            def score(j, carry):
                at = pl.multiple_of(j * block, block)
                value = dot_nt(queries, cand[pl.ds(pl.multiple_of(m * row_count * tokens + at, block), block), :]) + bias[j, m : m + 1, :]
                logits[:, pl.ds(at, block)] = value
                top = jnp.maximum(
                    jnp.maximum(value[:, :128], value[:, 128:256]), jnp.maximum(value[:, 256:384], value[:, 384:])
                )
                highest[...] = jnp.maximum(highest[...], top)
                return carry

            lax.fori_loop(0, blocks, score, 0)

            def soften(s, carry):
                near = pl.multiple_of(s * fine, fine)
                place = rh * half + s * fine
                own_at = pl.multiple_of(row * tokens + (place // 128) * 128, 128)
                hit = lax.broadcasted_iota(jnp.int32, (fine, 128), 1) == lax.broadcasted_iota(
                    jnp.int32, (fine, 128), 0
                ) + lax.rem(place, 128)
                valid = jnp.where(
                    lax.broadcasted_iota(jnp.int32, (fine, 1), 0) + place < length, 1.0, 0.0
                )
                top = jnp.max(highest[pl.ds(near, fine), :], axis=1, keepdims=True)
                own_logit = jnp.sum(
                    jnp.where(hit, logits[pl.ds(near, fine), pl.ds(own_at, 128)], 0.0), axis=1, keepdims=True
                )
                total = jnp.zeros((fine, 128), jnp.float32)
                for j in range(blocks):
                    value = jnp.exp(logits[pl.ds(near, fine), j * block : (j + 1) * block] - top)
                    logits[pl.ds(near, fine), j * block : (j + 1) * block] = value
                    total = total + ((value[:, :128] + value[:, 128:256]) + (value[:, 256:384] + value[:, 384:]))
                total = jnp.sum(total, axis=1, keepdims=True)
                share = valid / total
                there = pl.multiple_of(place, fine)
                for j in range(blocks):
                    grad_logits[pl.ds(there, fine), j * block : (j + 1) * block] = (
                        logits[pl.ds(near, fine), j * block : (j + 1) * block] * share
                    ).astype(bf)
                own = logits[pl.ds(near, fine), pl.ds(own_at, 128)] * share - jnp.where(hit, valid, 0.0)
                grad_logits[pl.ds(there, fine), pl.ds(own_at, 128)] = own.astype(bf)
                return carry + valid * (top + jnp.log(total) - own_logit)

            loss = lax.fori_loop(0, half // fine, soften, jnp.zeros((fine, 1), jnp.float32))
            small[3:4, :] += jnp.broadcast_to(jnp.sum(loss, axis=0, keepdims=True), (1, width))
            grad_query = dot_nn(grad_logits[pl.ds(pl.multiple_of(rh * half, half), half), :], cand[m * row_count * tokens : (m + 1) * row_count * tokens, :])
            grad, gain_part = rms_back(output[pl.ds(first, half), :], gain_three, grad_query)
            output[pl.ds(first, half), :] = grad
            small[2:3, :] += gain_part
            return carry

        lax.fori_loop(0, 2, one_half, 0)

        def to_targets(j, carry):
            at = pl.multiple_of(j * block, block)
            cand_grads[pl.ds(pl.multiple_of(m * row_count * tokens + at, block), block), :] = dot_tn(
                grad_logits[:, pl.ds(at, block)], query[m * tokens : (m + 1) * tokens, :]
            ).astype(bf)
            return carry

        lax.fori_loop(0, blocks, to_targets, 0)
        scatter_start(m, 0)
        small[4:5, :] += jnp.broadcast_to(
            jnp.sum(jnp.where(column < length, 1.0, 0.0), axis=1, keepdims=True), (1, width)
        )

    small[...] = jnp.zeros_like(small)
    loss_of(0)
    loss_of(1)
    scatter_wait(0, 0)
    if bits > 1:
        scatter_start(0, 1)

    def partner(bit):
        mine = lax.rem(row // (1 << bit), 2)
        return mine, (dp, flip(row, (bit,)))

    low = cand
    squared = {}
    al = lambda value: pl.multiple_of(value, 16)

    def summing(first, rows, sem, land):
        half_rows = rows // 2
        units = rows // (16 * devices)
        sizes = [((units + 1) // 2) * 8 * devices, (units // 2) * 8 * devices]
        parts = [p for p in range(2) if sizes[p]]
        part_orders = [list(range(1, bits)), list(range(bits - 1, 0, -1))]

        def lower(at, size):
            low[pl.ds(al(at), size), :] = acc[pl.ds(al(at), size), :].astype(bf)

        def add(at, size, off):
            acc[pl.ds(al(at), size), :] += got_sums[pl.ds(off, size), :].astype(jnp.float32)

        def send(source, at, size, target, sem, where):
            copy = pltpu.make_async_remote_copy(
                source.at[pl.ds(al(at), size)], target, send_r.at[sem], recv_r.at[sem],
                device_id=where, device_id_type=MESH,
            )
            copy.start()
            pending.append(copy)
            return copy

        def expect(at, size, sem, where):
            pltpu.make_async_remote_copy(
                gathered.at[pl.ds(al(at), size)], gathered.at[pl.ds(al(at), size)], send_r.at[sem], recv_r.at[sem],
                device_id=where, device_id_type=MESH,
            ).wait_recv()

        mine, where = partner(0)
        give = first + (1 - mine) * half_rows
        lower(give, half_rows)
        copy = send(low, give, half_rows, got_sums.at[pl.ds(land, half_rows)], sem, where)
        yield
        copy.wait_recv()
        base = first + mine * half_rows
        add(base, half_rows, land)
        sem, land = sem + 1, land + half_rows
        starts = [base, base + sizes[0]]
        for step in range(bits - 1):
            moved = []
            for p in parts:
                mine, where = partner(part_orders[p][step])
                size = sizes[p] // 2
                give = starts[p] + (1 - mine) * size
                lower(give, size)
                copy = send(low, give, size, got_sums.at[pl.ds(land, size)], sem, where)
                starts[p], sizes[p] = starts[p] + mine * size, size
                moved.append((p, copy, land))
                sem, land = sem + 1, land + size
            yield
            for p, copy, at in moved:
                copy.wait_recv()
                add(starts[p], sizes[p], at)
        moved = []
        finals = {}
        for p in parts:
            size = sizes[p] // dp_count
            finals[p] = starts[p] + dp * size
            for k in range(1, dp_count):
                other = lax.rem(dp + k, dp_count)
                give = starts[p] + other * size
                lower(give, size)
                copy = send(low, give, size, got_sums.at[pl.ds(land, size)], sem, (other, row))
                moved.append((p, copy, land, size))
                sem, land = sem + 1, land + size
        yield
        for p, copy, at, size in moved:
            copy.wait_recv()
            add(finals[p], size, at)
        moved = []
        for p in parts:
            size = sizes[p] // dp_count
            at = finals[p]
            done = acc[pl.ds(al(at), size), :]
            small[5:6, :] += jnp.sum(done * done, axis=0, keepdims=True)
            gathered[pl.ds(al(at), size), :] = done.astype(bf)
            squared[first] = True
            for k in range(1, dp_count):
                other = lax.rem(dp + k, dp_count)
                send(gathered, at, size, gathered.at[pl.ds(al(at), size)], sem, (other, row))
                moved.append((p, k, size, sem))
                sem += 1
        yield
        for p, k, size, one in moved:
            source = lax.rem(dp + dp_count - k, dp_count)
            expect(starts[p] + source * size, size, one, (source, row))
        for step in range(bits - 2, -1, -1):
            moved = []
            for p in parts:
                mine, where = partner(part_orders[p][step])
                send(gathered, starts[p], sizes[p], gathered.at[pl.ds(al(starts[p]), sizes[p])], sem, where)
                moved.append((p, mine, where, sem))
                sem += 1
            yield
            for p, mine, where, one in moved:
                bottom = starts[p] - mine * sizes[p]
                expect(bottom + (1 - mine) * sizes[p], sizes[p], one, where)
                starts[p], sizes[p] = bottom, 2 * sizes[p]
        mine, where = partner(0)
        send(gathered, first + mine * half_rows, half_rows, gathered.at[pl.ds(al(first + mine * half_rows), half_rows)], sem, where)
        yield
        expect(first + (1 - mine) * half_rows, half_rows, sem, where)

    for copy in gathers:
        copy.wait_send()
    rows_early = 2 * ff + inner
    rows_late = 3 * inner + tokens
    sems_each = send_r.shape[0] // 2
    early = summing(0, rows_early, 0, 0)
    late = summing(rows_early, rows_late, sems_each, rows_early)

    query[...] = output[...].astype(bf)
    for k in range(ff // width):
        acc[k * width : (k + 1) * width, :] = dot_tn(active[:, k * width : (k + 1) * width], query[...])
    scatter_wait(1, 0)
    if bits > 1:
        scatter_start(1, 1)

    grad_attended, grad_middle_low = 2 * tokens, 4 * tokens

    def feed_back(c, m):
        at = pl.multiple_of(m * tokens + c * half, half)
        near = pl.multiple_of(c * half, half)
        branch = query[pl.ds(at, half), :]
        for k in range(ff // width):
            active[pl.ds(at, half), k * width : (k + 1) * width] = (
                dot_nt(branch, down_low[k * width : (k + 1) * width, :])
                * slope[pl.ds(at, half), k * width : (k + 1) * width]
            ).astype(bf)
        grad_hidden = dot_nt(active[pl.ds(at, half), :], up_low[...])
        grad, gain_part = rms_back(middle[pl.ds(at, half), :], gain_two, grad_hidden)
        small[1:2, :] += gain_part
        grad = grad + output[pl.ds(at, half), :]
        output[pl.ds(at, half), :] = grad
        grad_low = grad.astype(bf)
        grad_logits[pl.ds(near, half), grad_middle_low + m * width : grad_middle_low + (m + 1) * width] = grad_low
        grad_logits[pl.ds(near, half), grad_attended + m * inner : grad_attended + (m + 1) * inner] = dot_nt(
            grad_low, out_low[...]
        ).astype(bf)

    for m in range(micro):
        lax.fori_loop(0, 2, lambda c, carry, m=m: (feed_back(c, m), carry)[1], 0)
    for k in range(ff // width):
        acc[ff + k * width : ff + (k + 1) * width, :] = dot_tn(hidden_two[...], active[:, k * width : (k + 1) * width])
    acc[2 * ff : 2 * ff + inner, :] = dot_tn(
        attended[:tokens, :], grad_logits[:, grad_middle_low : grad_middle_low + width]
    ) + dot_tn(attended[tokens:, :], grad_logits[:, grad_middle_low + width : grad_middle_low + 2 * width])
    next(early, None)
    for step in range(1, bits - 1):
        for m in range(micro):
            scatter_wait(m, step)
            scatter_start(m, step + 1)

    def attend_back(m, begin, end):
        base = m * tokens

        def pair(hp, carry):
            lanes = [pl.ds(pl.multiple_of(k * inner + hp * 128, 128), 128) for k in range(3)]
            here = pl.ds(pl.multiple_of(grad_attended + m * inner + hp * 128, 128), 128)
            keys = joined[base : base + tokens, lanes[1]]
            values = joined[base : base + tokens, lanes[2]]
            for rb in (1, 0):
                first = base + rb * half
                span = (rb + 1) * half
                probs = probs_low if rb else probs_top
                queries = joined[first : first + half, lanes[0]]
                upper = grad_logits[rb * half : (rb + 1) * half, here]
                for h in range(2):
                    logits[:, h * tokens : h * tokens + span] = dot_nt(upper * head_mask[h], values[:span])
                for h in range(2):
                    for s in range(half // sub):
                        chance = probs[m * 2 * pairs + hp * 2 + h, s * sub : (s + 1) * sub, :].astype(jnp.float32)
                        grad = logits[s * sub : (s + 1) * sub, h * tokens : h * tokens + span]
                        inner_sum = jnp.sum(chance * grad, axis=1, keepdims=True)
                        grad_logits[s * sub : (s + 1) * sub, h * tokens : h * tokens + span] = (
                            chance * (grad - inner_sum)
                        ).astype(bf)
                pieces = [grad_logits[:half, h * tokens : h * tokens + span] for h in range(2)]
                total_q = dot_nn(pieces[0], keys[:span] * head_mask[0]) + dot_nn(
                    pieces[1], keys[:span] * head_mask[1]
                )
                total_k = dot_tn(pieces[0], queries * head_mask[0]) + dot_tn(pieces[1], queries * head_mask[1])
                total_v = dot_tn(probs[m * 2 * pairs + hp * 2], upper * head_mask[0]) + dot_tn(
                    probs[m * 2 * pairs + hp * 2 + 1], upper * head_mask[1]
                )
                joined[first : first + half, lanes[0]] = (total_q * 0.125).astype(bf)
                if rb:
                    part_k[...] = total_k
                    part_v[...] = total_v
                else:
                    part_k[:half, :] += total_k
                    part_v[:half, :] += total_v
            joined[base : base + tokens, lanes[1]] = part_k[...].astype(bf)
            joined[base : base + tokens, lanes[2]] = part_v[...].astype(bf)
            return carry

        lax.fori_loop(begin, end, pair, 0)

    for m in range(micro):
        for begin in range(0, pairs, 2):
            attend_back(m, begin, min(begin + 2, pairs))
            next(early, None)

    place = rows_early + 3 * inner

    def project_back(c, carry):
        at = pl.multiple_of(c * half, half)
        near = pl.multiple_of(lax.rem(c, 2) * half, half)
        grad_hidden = dot_nt(joined[pl.ds(at, half), :], qkv_low[...])
        grad, gain_part = rms_back(embedded[pl.ds(at, half), :], gain_one, grad_hidden)
        small[0:1, :] += gain_part
        grad = grad + output[pl.ds(at, half), :]
        acc[pl.ds(pl.multiple_of(place + near, half), half), :] += grad
        row_grads[pl.ds(at, half), :] = (scaling * grad).astype(bf)
        return carry

    acc[place : place + tokens, :] = jnp.zeros((tokens, width), jnp.float32)
    lax.fori_loop(0, chunks, project_back, 0)
    next(early, None)
    for k in range(3 * inner // width):
        acc[rows_early + k * width : rows_early + (k + 1) * width, :] = dot_tn(
            hidden_one[...], joined[:, k * width : (k + 1) * width]
        )
    next(late, None)
    for m in range(micro):
        if bits > 1:
            scatter_wait(m, bits - 1)
    next(early, None)

    out_at = rows_early + rows_late
    slot_row = jnp.concatenate([slots[c : c + 1, :] for c in range(slots.shape[0])], axis=1)
    slot_index = lax.broadcasted_iota(jnp.int32, (capacity, slot_row.shape[1]), 0).astype(jnp.float32)

    def arrange(other):
        pick = one_hot(slot_index == slot_row - (other * capacity).astype(jnp.float32))
        return dot_nn(pick, row_grads[...]).astype(bf)

    def block_copy(k):
        other, where = other_device(k, dp_count, row_count)
        return pltpu.make_async_remote_copy(
            cand.at[pl.ds(al(out_at + k * capacity), capacity)], incoming.at[pl.ds(al(k * capacity), capacity)],
            send_a.at[k], recv_a.at[k], device_id=where, device_id_type=MESH,
        )

    def send_rows(k, carry):
        other, where = other_device(k, dp_count, row_count)
        cand[pl.ds(al(out_at + k * capacity), capacity), :] = arrange(other)
        block_copy(k).start()
        return carry

    lax.fori_loop(1, devices // 2, send_rows, 0)
    next(late, None)
    next(early, None)
    lax.fori_loop(devices // 2, devices, send_rows, 0)
    incoming[0:capacity, :] = arrange(dp * row_count + row)
    next(late, None)
    next(early, None)

    groups = 4
    each = devices // groups
    tile = 256
    tiles = -(-rows_here // tile)
    in_logits = logits.shape[1] // tile

    def add_table(g):
        span = each * capacity
        ids = received[:, g * span : (g + 1) * span]
        rows = incoming[g * span : (g + 1) * span, :]
        near = one_hot(lax.broadcasted_iota(jnp.int32, (tile, span), 0) == jnp.bitwise_and(ids, tile - 1))
        high = jnp.right_shift(ids, 8)

        def one(t, at_row, at_lane, ref):
            value = dot_nn(near * one_hot(high == t), rows)
            where = (pl.ds(pl.multiple_of(at_row, tile), tile), pl.ds(pl.multiple_of(at_lane, tile), tile))
            if g:
                value = value + ref[where]
            ref[where] = value
            if g == groups - 1:
                small[5:6, :] += jnp.sum(value * value, axis=0, keepdims=True)

        def first_ones(t, carry):
            one(t, 0, t * tile, logits)
            return carry

        def other_ones(t, carry):
            u = t - in_logits
            one(t, (u // (ff // tile)) * tile, lax.rem(u, ff // tile) * tile, slope)
            return carry

        lax.fori_loop(0, min(tiles, in_logits), first_ones, 0)
        if tiles > in_logits:
            lax.fori_loop(in_logits, tiles, other_ones, 0)

    for g in range(groups):
        lax.fori_loop(max(1, g * each), (g + 1) * each, lambda k, c: (block_copy(k).wait_recv(), c)[1], 0)
        add_table(g)
        next(late, None)
        next(early, None)
    stores = []
    for t in range(tiles):
        count = min(tile, rows_here - t * tile)
        if t < in_logits:
            source = logits.at[pl.ds(0, count), pl.ds(t * tile, tile)]
        else:
            u = t - in_logits
            source = slope.at[pl.ds((u // (ff // tile)) * tile, count), pl.ds((u % (ff // tile)) * tile, tile)]
        copy = pltpu.make_async_copy(source, table_grads.at[pl.ds(t * tile, count)], store_sem.at[t])
        copy.start()
        stores.append(copy)

    def spread(source, zone, mine, others, where, base):
        for k, other in enumerate(others):
            copy = pltpu.make_async_remote_copy(
                source, zone.at[mine], send_n.at[base + k], recv_n.at[base + mine],
                device_id=where(other), device_id_type=MESH,
            )
            copy.start()
            pending.append(copy)
        zone[mine] = source[...]
        for other in others:
            pltpu.make_async_remote_copy(
                source, zone.at[other], send_n.at[base], recv_n.at[base + other],
                device_id=where(other), device_id_type=MESH,
            ).wait_recv()
        return jnp.sum(zone[...], axis=0)

    spread_rows = spread(
        small, by_row, row, [lax.rem(row + k, row_count) for k in range(1, row_count)], lambda o: (dp, o), 0
    )
    row_small[...] = spread_rows
    summed[...] = spread(
        row_small, by_dp, dp, [lax.rem(dp + k, dp_count) for k in range(1, dp_count)], lambda o: (o, row), row_count
    )
    for summer in (late, early):
        for unused in summer:
            pass
    for copy in stores:
        copy.wait()
    lax.fori_loop(1, devices, lambda k, c: (block_copy(k).wait_send(), c)[1], 0)
    for copy in pending:
        copy.wait_send()


def layer(dp_count, row_count, capacity, rows_here, lengths, items, targets, correction, matrices, positions, gains,
          slots, received):
    qkv, out, up, down = matrices
    tokens, width = positions.shape
    half = tokens // 2
    inner, ff = out.shape[0], up.shape[1]
    events = 2 * tokens
    group = row_count * tokens
    devices = dp_count * row_count
    bf, f32 = jnp.bfloat16, jnp.float32
    pairs = inner // 128
    bits = row_count.bit_length() - 1
    hops = 2 * (row_count - 1)
    summed_rows = 2 * ff + 4 * inner + tokens
    sems = lambda count: pltpu.SemaphoreType.DMA((count,))
    hbm = pl.BlockSpec(memory_space=pl.ANY)
    return pl.pallas_call(
        functools.partial(layer_kernel, dp_count, row_count, capacity, rows_here),
        out_shape=(
            jax.ShapeDtypeStruct((rows_here, width), f32),
            jax.ShapeDtypeStruct((summed_rows, width), bf),
            jax.ShapeDtypeStruct((8, width), f32),
        ),
        in_specs=[pl.BlockSpec(memory_space=pltpu.SMEM), VMEM, VMEM, VMEM, hbm, hbm, hbm, hbm] + [VMEM] * 4,
        out_specs=(hbm, VMEM, VMEM),
        scratch_shapes=[
            pltpu.VMEM(qkv.shape, bf),
            pltpu.VMEM(out.shape, bf),
            pltpu.VMEM(up.shape, bf),
            pltpu.VMEM(down.shape, bf),
            pltpu.VMEM((events, width), f32),
            pltpu.VMEM((events, width), bf),
            pltpu.VMEM((events, 3 * inner), bf),
            pltpu.VMEM((4 * pairs, half, half), bf),
            pltpu.VMEM((4 * pairs, half, tokens), bf),
            pltpu.VMEM((events, inner), bf),
            pltpu.VMEM((events, width), f32),
            pltpu.VMEM((events, width), bf),
            pltpu.VMEM((events, ff), f32),
            pltpu.VMEM((events, ff), bf),
            pltpu.VMEM((events, width), f32),
            pltpu.VMEM((events, width), bf),
            pltpu.VMEM((2 * group, width), bf),
            pltpu.VMEM((row_count, 2, tokens), f32),
            pltpu.VMEM((2 * group, width), bf),
            pltpu.VMEM((hops, tokens, width), bf),
            pltpu.VMEM((half, group), f32),
            pltpu.VMEM((tokens, group), bf),
            pltpu.VMEM((half, 128), f32),
            pltpu.VMEM((2 * events, width), bf),
            pltpu.VMEM((8, width), f32),
            pltpu.VMEM((summed_rows, width), f32),
            pltpu.VMEM((summed_rows, width), bf),
            pltpu.VMEM((devices * capacity, width), bf),
            pltpu.VMEM((row_count, 8, width), f32),
            pltpu.VMEM((dp_count, 8, width), f32),
            pltpu.VMEM((8, width), f32),
            pltpu.VMEM((tokens, 128), f32),
            pltpu.VMEM((tokens, 128), f32),
            sems(2 + (inner + ff) // width),
            sems(row_count),
            sems(row_count),
            sems(hops),
            sems(hops),
            sems(hops),
            sems(hops),
            sems(2 * (4 * bits + 4 * dp_count)),
            sems(2 * (4 * bits + 4 * dp_count)),
            sems(devices),
            sems(devices),
            sems(devices),
            sems(devices),
            sems(-(-rows_here // 256)),
        ],
        name="layer",
        compiler_params=pltpu.CompilerParams(collective_id=5, has_side_effects=True, vmem_limit_bytes=62 * 2**20),
    )(lengths, items, targets, correction, qkv, out, up, down, positions, gains, slots, received)


def small_kernel(dp_count, row_count, part, summed, by_row, by_dp, send_sem, recv_sem):
    dp = lax.axis_index("dp")
    row = lax.axis_index("rows")
    barrier = pltpu.get_barrier_semaphore()
    row_places = [lax.rem(row + k, row_count) for k in range(1, row_count)]
    dp_places = [lax.rem(dp + k, dp_count) for k in range(1, dp_count)]
    for other in row_places:
        pl.semaphore_signal(barrier, inc=1, device_id=(dp, other), device_id_type=MESH)
    for other in dp_places:
        pl.semaphore_signal(barrier, inc=1, device_id=(other, row), device_id_type=MESH)
    pl.semaphore_wait(barrier, row_count + dp_count - 2)

    def spread(source, landing, mine, others, where, base):
        sends = []
        for k, other in enumerate(others):
            copy = pltpu.make_async_remote_copy(
                source, landing.at[mine], send_sem.at[base + k], recv_sem.at[base + mine],
                device_id=where(other), device_id_type=MESH,
            )
            copy.start()
            sends.append(copy)
        landing[mine] = source[...]
        for other in others:
            pltpu.make_async_remote_copy(
                source, landing.at[other], send_sem.at[base], recv_sem.at[base + other],
                device_id=where(other), device_id_type=MESH,
            ).wait_recv()
        for copy in sends:
            copy.wait_send()

    spread(part, by_row, row, row_places, lambda other: (dp, other), 0)
    summed[...] = jnp.sum(by_row[...], axis=0)
    spread(summed, by_dp, dp, dp_places, lambda other: (other, row), row_count)
    summed[...] = jnp.sum(by_dp[...], axis=0)


def small_sum(dp_count, row_count, part):
    return pl.pallas_call(
        functools.partial(small_kernel, dp_count, row_count),
        out_shape=jax.ShapeDtypeStruct(part.shape, part.dtype),
        in_specs=[VMEM],
        out_specs=VMEM,
        scratch_shapes=[
            pltpu.VMEM((row_count,) + part.shape, part.dtype),
            pltpu.VMEM((dp_count,) + part.shape, part.dtype),
            pltpu.SemaphoreType.DMA((row_count + dp_count,)),
            pltpu.SemaphoreType.DMA((row_count + dp_count,)),
        ],
        name="small_sum",
        compiler_params=pltpu.CompilerParams(collective_id=4, has_side_effects=True),
    )(part)


def grouped_layer(fetched, valid_pos, lengths, correction, weights, positions, gains):
    qkv_weight, out_weight, up_weight, down_weight = weights
    micro, tokens = valid_pos.shape
    histories = lengths.shape[1]
    length, width = positions.shape
    matrices = (rounded(qkv_weight), rounded(out_weight), rounded(up_weight), rounded(down_weight))
    scaling = math.sqrt(width)
    offset = lax.axis_index("rows") * tokens
    running = [
        jnp.zeros_like(qkv_weight),
        jnp.zeros_like(out_weight),
        jnp.zeros_like(up_weight),
        jnp.zeros_like(down_weight),
    ]
    grad_positions = jnp.zeros_like(positions)
    grad_gains = jnp.zeros_like(gains)
    loss_local = jnp.zeros((), jnp.float32)
    embed_grads = []
    target_grads = []
    for micro_index in range(micro):
        lengths_here = lengths[micro_index]
        valid_here = valid_pos[micro_index].astype(jnp.float32)
        embedded = scaling * fetched[0, micro_index].astype(jnp.float32) + jnp.tile(
            positions, (histories, 1)
        )
        output, saved_state = layer_forward(embedded, lengths_here, matrices, gains, HEADS)
        normed_three, back_three = jax.vjp(rms_norm, output, gains[2])
        query_low = rounded(normed_three)
        bias_low = jnp.where(
            valid_pos[micro_index],
            rounded(-correction[micro_index].reshape(-1)),
            jnp.asarray(MASKED, jnp.bfloat16),
        )
        candidates, cand_bias = (
            lax.all_gather(fetched[1, micro_index], "rows", axis=0, tiled=True),
            lax.all_gather(bias_low, "rows", axis=0, tiled=True),
        )
        loss_part, grad_logits, log_total = candidate_loss(
            query_low, candidates, cand_bias, valid_here, offset
        )
        loss_local = loss_local + loss_part
        grad_output, gain_three = back_three(matmul(grad_logits, candidates))
        target_grads.append(
            lax.psum_scatter(
                inner_rows(grad_logits, query_low).astype(jnp.bfloat16),
                "rows",
                scatter_dimension=0,
                tiled=True,
            ).astype(jnp.float32)
        )
        grad_embedded, grad_layer, gain_pair = layer_backward(
            grad_output, saved_state, lengths_here, matrices, HEADS
        )
        for which_one in range(4):
            running[which_one] = running[which_one] + grad_layer[which_one]
        grad_positions = grad_positions + jnp.sum(
            grad_embedded.reshape(histories, length, width), axis=0
        )
        grad_gains = grad_gains + jnp.stack([gain_pair[0], gain_pair[1], gain_three])
        embed_grads.append(scaling * grad_embedded)
    target_part = jnp.stack(target_grads)
    row_grads = jnp.concatenate([jnp.stack(embed_grads), target_part]).reshape(-1, width)
    return running, grad_positions, rounded(row_grads), grad_gains, loss_local


def local(
    item_ids,
    targets,
    lengths,
    correction,
    item_row,
    item_table,
    qkv_weight,
    out_weight,
    up_weight,
    down_weight,
    positions,
    gains,
    item_table_first,
    qkv_weight_first,
    out_weight_first,
    up_weight_first,
    down_weight_first,
    positions_first,
    gains_first,
    item_table_second,
    qkv_weight_second,
    out_weight_second,
    up_weight_second,
    down_weight_second,
    positions_second,
    gains_second,
):
    micro, histories, length = item_ids.shape
    rows_here, width = item_table.shape
    devices = lax.axis_size("dp") * lax.axis_size("rows")
    tokens = histories * length
    requests = 2 * micro * tokens
    capacity = 3 * (requests + devices) // (2 * devices) + 1
    used = -(-capacity // 8) * 8
    capacity = -(-capacity // 16) * 16
    dp_count, row_count = lax.axis_size("dp"), lax.axis_size("rows")
    position = jnp.arange(length, dtype=jnp.int32)
    valid_pos = (position[None, None, :] < lengths[:, :, None]).reshape(micro, tokens)
    wanted = jnp.where(
        valid_pos.reshape(1, -1), jnp.stack([item_ids, targets]).reshape(2, micro * tokens), -1
    ).reshape(requests, 1)
    fetched, slots, received = lookup(
        dp_count, row_count, capacity, used, wanted, item_row, item_table
    )
    received = received[:, 0, :capacity].reshape(1, devices * capacity)
    fetched = fetched.reshape(2, micro, tokens, width)
    weights = (qkv_weight, out_weight, up_weight, down_weight, positions)
    summed_rows = sum(one.size for one in weights) // width
    group = row_count * tokens
    fits = (
        histories == 1
        and micro == 2
        and row_count > 1
        and devices % 4 == 0
        and group <= 4096
        and summed_rows % (16 * devices) == 0
        and summed_rows + devices * capacity <= 2 * group
        and rows_here <= 4096 + group
    )
    if fits:
        table_grad, gathered, small = layer(
            dp_count,
            row_count,
            capacity,
            rows_here,
            lengths.reshape(micro),
            fetched[0].reshape(micro * tokens, width),
            fetched[1].reshape(micro * tokens, width),
            correction.reshape(micro, tokens),
            weights[:4],
            positions,
            gains,
            slots,
            received,
        )
        sum_gains, sum_loss, sum_count = small[:3], small[3, 0], small[4, 0]
        square_total = jnp.sum(small[5])
        order = (3, 2, 1, 0, 4)
    else:
        running, grad_positions, row_grads, grad_gains, loss_local = grouped_layer(
            fetched,
            valid_pos,
            lengths,
            correction,
            (qkv_weight, out_weight, up_weight, down_weight),
            positions,
            gains,
        )
        count_local = jnp.sum(valid_pos.astype(jnp.float32))
        incoming, gathered, square = tail_exchange(
            dp_count,
            row_count,
            capacity,
            running[0],
            running[1],
            running[2],
            running[3],
            grad_positions,
            row_grads,
            slots,
        )
        table_grad, table_square = table_gradient(
            rows_here, received, incoming.reshape(devices * capacity, width)
        )
        own_square = jnp.sum(table_square[0] + square[0])
        scalars = jnp.stack([loss_local, count_local, own_square])
        part = jnp.concatenate(
            [grad_gains.reshape(-1), jnp.pad(scalars, (0, 1024 - grad_gains.size - 3))]
        ).reshape(8, 128)
        small = small_sum(dp_count, row_count, part).reshape(-1)
        sum_gains = small[: grad_gains.size].reshape(grad_gains.shape)
        sum_loss, sum_count, square_total = (small[grad_gains.size + k] for k in range(3))
        order = (0, 2, 1, 3, 4)
    gathered = gathered.astype(jnp.float32)
    place = 0
    blocks = {}
    for which_one in order:
        like = weights[which_one]
        count = like.shape[1] // width
        piece = gathered[place : place + count * like.shape[0]]
        blocks[which_one] = jnp.concatenate(
            [piece[c * like.shape[0] : (c + 1) * like.shape[0]] for c in range(count)], axis=1
        )
        place += count * like.shape[0]
    gradients = (table_grad, blocks[0], blocks[1], blocks[2], blocks[3], blocks[4], sum_gains)
    grad_norm = jnp.sqrt(square_total + jnp.sum(sum_gains * sum_gains))
    factor = CLIP / jnp.maximum(grad_norm, CLIP)
    weights = (item_table, qkv_weight, out_weight, up_weight, down_weight, positions, gains)
    firsts = (
        item_table_first,
        qkv_weight_first,
        out_weight_first,
        up_weight_first,
        down_weight_first,
        positions_first,
        gains_first,
    )
    seconds = (
        item_table_second,
        qkv_weight_second,
        out_weight_second,
        up_weight_second,
        down_weight_second,
        positions_second,
        gains_second,
    )
    rates = (RATE, RATE, RATE, RATE, RATE, RATE, GAIN_RATE)
    decays = (DECAY, DECAY, DECAY, DECAY, DECAY, DECAY, 0.0)
    updated = [
        adam_step(
            weights[which_one],
            factor * gradients[which_one],
            firsts[which_one],
            seconds[which_one],
            rates[which_one],
            decays[which_one],
        )
        for which_one in range(7)
    ]
    return (
        updated[0][0],
        updated[1][0],
        updated[2][0],
        updated[3][0],
        updated[4][0],
        updated[5][0],
        updated[6][0],
        updated[0][1],
        updated[1][1],
        updated[2][1],
        updated[3][1],
        updated[4][1],
        updated[5][1],
        updated[6][1],
        updated[0][2],
        updated[1][2],
        updated[2][2],
        updated[3][2],
        updated[4][2],
        updated[5][2],
        updated[6][2],
        sum_loss,
        sum_count,
        grad_norm,
    )


def solution(mesh):
    placed = (
        P(None, ("dp", "rows"), None),
        P(None, ("dp", "rows"), None),
        P(None, ("dp", "rows")),
        P(None, ("dp", "rows"), None),
        P(),
        P(("dp", "rows"), None),
        P(),
        P(),
        P(),
        P(),
        P(),
        P(),
        P(("dp", "rows"), None),
        P(),
        P(),
        P(),
        P(),
        P(),
        P(),
        P(("dp", "rows"), None),
        P(),
        P(),
        P(),
        P(),
        P(),
        P(),
    )
    return jax.shard_map(
        local,
        mesh=mesh,
        in_specs=placed,
        out_specs=(
            P(("dp", "rows"), None),
            P(),
            P(),
            P(),
            P(),
            P(),
            P(),
            P(("dp", "rows"), None),
            P(),
            P(),
            P(),
            P(),
            P(),
            P(),
            P(("dp", "rows"), None),
            P(),
            P(),
            P(),
            P(),
            P(),
            P(),
            P(),
            P(),
            P(),
        ),
        check_vma=False,
    )
```

```python
import functools
import math

import jax
import jax.numpy as jnp
from jax import lax
from jax.experimental import pallas as pl
from jax.experimental.pallas import tpu as pltpu
from jax.sharding import PartitionSpec as P

MESH = pl.DeviceIdType.MESH
VMEM = pl.BlockSpec(memory_space=pltpu.VMEM)
HEADS = 8
STEP = 10


NORM_EPS = 1e-06
MASKED = -1e30
BETA_ONE = 0.9
BETA_TWO = 0.999
ADAM_EPS = 1e-08
DECAY = 0.01
RATE = 0.1
GAIN_RATE = 1.0
CLIP = 1.0


def rounded(values):
    return values.astype(jnp.bfloat16)


def matmul(first_op, second_op):
    return jnp.dot(first_op, second_op, preferred_element_type=jnp.float32)


def inner_rows(first_op, second_op):
    return lax.dot_general(
        first_op, second_op, (((0,), (0,)), ((), ())), preferred_element_type=jnp.float32
    )


def inner_cols(first_op, second_op):
    return lax.dot_general(
        first_op, second_op, (((1,), (1,)), ((), ())), preferred_element_type=jnp.float32
    )


def rms_norm(values, gain_row):
    return (
        values * lax.rsqrt(jnp.mean(values * values, axis=-1, keepdims=True) + NORM_EPS) * gain_row
    )


def gelu_tanh(values):
    return jax.nn.gelu(values)


def split_heads(joined, histories, head_count):
    pieces = joined.reshape(histories, joined.shape[0] // histories, 3, head_count, -1)
    return (pieces[:, :, 0], pieces[:, :, 1], pieces[:, :, 2])


def masked_scores(queries, key_rows, lengths_here):
    length = queries.shape[1]
    scaling = queries.shape[-1] ** (-0.5)
    scores = (
        jnp.einsum("sqhe,skhe->shqk", queries, key_rows, preferred_element_type=jnp.float32)
        * scaling
    )
    position = jnp.arange(length, dtype=jnp.int32)
    allowed = (position[None, :] <= position[:, None])[None, None] & (
        position[None, None, None, :] < lengths_here[:, None, None, None]
    )
    return jnp.where(allowed, scores, MASKED)


def attention_forward(joined, lengths_here, head_count):
    queries, key_rows, value_rows = split_heads(joined, lengths_here.shape[0], head_count)
    scores = masked_scores(queries, key_rows, lengths_here)
    highest = jnp.max(scores, axis=-1, keepdims=True)
    log_total = highest + jnp.log(jnp.sum(jnp.exp(scores - highest), axis=-1, keepdims=True))
    probabilities = rounded(jnp.exp(scores - log_total))
    attended = jnp.einsum(
        "shqk,skhe->sqhe", probabilities, value_rows, preferred_element_type=jnp.float32
    )
    return (attended.reshape(joined.shape[0], -1), log_total)


def attention_backward(joined, log_total, lengths_here, grad_attended, head_count):
    queries, key_rows, value_rows = split_heads(joined, lengths_here.shape[0], head_count)
    probabilities = jnp.exp(masked_scores(queries, key_rows, lengths_here) - log_total)
    grad_heads = grad_attended.reshape(queries.shape)
    grad_probs = jnp.einsum(
        "sqhe,skhe->shqk", grad_heads, value_rows, preferred_element_type=jnp.float32
    )
    grad_values = jnp.einsum(
        "shqk,sqhe->skhe", rounded(probabilities), grad_heads, preferred_element_type=jnp.float32
    )
    row_inner = jnp.sum(probabilities * grad_probs, axis=-1, keepdims=True)
    grad_scores = rounded(probabilities * (grad_probs - row_inner))
    scaling = queries.shape[-1] ** (-0.5)
    grad_queries = (
        jnp.einsum("shqk,skhe->sqhe", grad_scores, key_rows, preferred_element_type=jnp.float32)
        * scaling
    )
    grad_keys = (
        jnp.einsum("shqk,sqhe->skhe", grad_scores, queries, preferred_element_type=jnp.float32)
        * scaling
    )
    stacked = jnp.stack([grad_queries, grad_keys, grad_values], axis=2)
    return stacked.reshape(joined.shape[0], -1)


def layer_forward(embedded, lengths_here, matrices, gains, head_count):
    qkv_low, out_low, up_low, down_low = matrices
    normed_one, back_one = jax.vjp(rms_norm, embedded, gains[0])
    hidden_one = rounded(normed_one)
    joined = rounded(matmul(hidden_one, qkv_low))
    attended, log_total = attention_forward(joined, lengths_here, head_count)
    attended_low = rounded(attended)
    middle = embedded + matmul(attended_low, out_low)
    normed_two, back_two = jax.vjp(rms_norm, middle, gains[1])
    hidden_two = rounded(normed_two)
    upward = matmul(hidden_two, up_low)
    active, back_active = jax.vjp(gelu_tanh, upward)
    active_low = rounded(active)
    output = middle + matmul(active_low, down_low)
    return (
        output,
        (
            back_one,
            hidden_one,
            joined,
            log_total,
            attended_low,
            back_two,
            hidden_two,
            back_active,
            active_low,
        ),
    )


def layer_backward(grad_output, saved_state, lengths_here, matrices, head_count):
    (
        back_one,
        hidden_one,
        joined,
        log_total,
        attended_low,
        back_two,
        hidden_two,
        back_active,
        active_low,
    ) = saved_state
    qkv_low, out_low, up_low, down_low = matrices
    grad_branch = rounded(grad_output)
    grad_down = inner_rows(active_low, grad_branch)
    grad_upward = rounded(back_active(inner_cols(grad_branch, down_low))[0])
    grad_up = inner_rows(hidden_two, grad_upward)
    grad_middle, gain_two = back_two(inner_cols(grad_upward, up_low))
    grad_middle = grad_middle + grad_output
    grad_attn = rounded(grad_middle)
    grad_out = inner_rows(attended_low, grad_attn)
    grad_attended = rounded(inner_cols(grad_attn, out_low))
    grad_joined = rounded(
        attention_backward(joined, log_total, lengths_here, grad_attended, head_count)
    )
    grad_qkv = inner_rows(hidden_one, grad_joined)
    grad_embedded, gain_one = back_one(inner_cols(grad_joined, qkv_low))
    return (
        grad_embedded + grad_middle,
        (grad_qkv, grad_out, grad_up, grad_down),
        (gain_one, gain_two),
    )


def candidate_loss(query_low, candidates, cand_bias, valid_here, offset):
    tokens, width = query_low.shape
    block_rows = min(512, tokens)
    blocks = tokens // block_rows
    column = jnp.arange(candidates.shape[0], dtype=jnp.int32)
    bias_wide = cand_bias.astype(jnp.float32)

    def one_block(running, block_pieces):
        query_block, valid_block, start_row = block_pieces
        logits = inner_cols(query_block, candidates) + bias_wide[None]
        highest = jnp.max(logits, axis=1, keepdims=True)
        log_total = highest + jnp.log(jnp.sum(jnp.exp(logits - highest), axis=1, keepdims=True))
        target_hit = (
            column[None, :]
            == (offset + start_row + jnp.arange(block_rows, dtype=jnp.int32))[:, None]
        )
        own_logit = jnp.sum(jnp.where(target_hit, logits, 0.0), axis=1)
        grad_logits = rounded(
            (jnp.exp(logits - log_total) - target_hit.astype(jnp.float32)) * valid_block[:, None]
        )
        return (
            running + jnp.sum(valid_block * (log_total[:, 0] - own_logit)),
            (grad_logits, log_total[:, 0]),
        )

    loss_part, block_out = lax.scan(
        one_block,
        jnp.zeros((), jnp.float32),
        (
            query_low.reshape(blocks, block_rows, width),
            valid_here.reshape(blocks, block_rows),
            jnp.arange(blocks, dtype=jnp.int32) * block_rows,
        ),
    )
    return (loss_part, block_out[0].reshape(tokens, -1), block_out[1].reshape(tokens))


def adam_step(weight, gradient, first, second, rate, decay):
    first_new = BETA_ONE * first + (1.0 - BETA_ONE) * gradient
    second_new = BETA_TWO * second + (1.0 - BETA_TWO) * gradient * gradient
    stepped = (
        first_new
        / (1.0 - BETA_ONE**STEP)
        / (jnp.sqrt(second_new / (1.0 - BETA_TWO**STEP)) + ADAM_EPS)
    )
    return (weight - rate * (stepped + decay * weight), first_new, second_new)


def reduce_rows(total_rows, devices):
    unit = 16 * devices
    return -(-total_rows // unit) * unit


def tail_kernel(dp_count, row_count, padded, capacity, qkv, out, up, down, pos, row_grads, slots, incoming, gathered, square,
                outgoing, acc, low, recv0, recv1, recv2, send_a, recv_a, send_r, recv_r):
    devices = dp_count * row_count
    dp = lax.axis_index("dp")
    row = lax.axis_index("rows")
    me = dp * row_count + row
    bits = row_count.bit_length() - 1
    barrier = pltpu.get_barrier_semaphore()

    def place(k):
        other = lax.rem(me + k, devices)
        return other, (other // row_count, lax.rem(other, row_count))

    def greet(k, carry):
        other, where = place(k)
        pl.semaphore_signal(barrier, inc=1, device_id=where, device_id_type=MESH)
        return carry

    lax.fori_loop(1, devices, greet, 0)
    width = 256
    at = 0
    for ref in (qkv, up):
        for c in range(ref.shape[1] // width):
            acc[pl.ds(at, ref.shape[0]), :] = ref[:, pl.ds(c * width, width)]
            at += ref.shape[0]
    for ref in (out, down, pos):
        acc[pl.ds(at, ref.shape[0]), :] = ref[...]
        at += ref.shape[0]
    if at < padded:
        acc[pl.ds(at, padded - at), :] = jnp.zeros((padded - at, width), jnp.float32)
    pl.semaphore_wait(barrier, devices - 1)

    def a2a_send(k):
        other, where = place(k)
        return pltpu.make_async_remote_copy(
            outgoing.at[other], incoming.at[k], send_a.at[k], recv_a.at[k], device_id=where, device_id_type=MESH)

    def a2a_recv(k):
        other, where = place(k)
        return pltpu.make_async_remote_copy(
            outgoing.at[other], incoming.at[k], send_a.at[k], recv_a.at[k], device_id=where, device_id_type=MESH)

    def partner(bit):
        step = 1 << bit
        mine = lax.rem(row // step, 2)
        return mine, (dp, row + step - 2 * step * mine)

    half = padded // 2
    units = padded // (16 * devices)
    part_rows = [((units + 1) // 2) * 16 * (devices // 2), (units // 2) * 16 * (devices // 2)]
    orders = [list(range(1, bits)), list(range(bits - 1, 0, -1))]
    al = lambda v: pl.multiple_of(v, 16)

    mine, where = partner(0)
    low[pl.ds(al((1 - mine) * half), half), :] = acc[pl.ds(al((1 - mine) * half), half), :].astype(jnp.bfloat16)
    first = pltpu.make_async_remote_copy(low.at[pl.ds(al((1 - mine) * half), half)], recv0, send_r.at[0], recv_r.at[0],
                                         device_id=where, device_id_type=MESH)
    first.start()
    slot_row = jnp.concatenate([slots[c : c + 1, :] for c in range(slots.shape[0])], axis=1)
    slot_index = lax.broadcasted_iota(jnp.int32, (capacity, slot_row.shape[1]), 0).astype(jnp.float32)

    def arrange(other):
        pick = one_hot(slot_index == slot_row - (other * capacity).astype(jnp.float32))
        return jnp.dot(pick, row_grads[...], preferred_element_type=jnp.float32).astype(jnp.bfloat16)

    def send_rows(k, carry):
        other, where = place(k)
        outgoing[other] = arrange(other)
        a2a_send(k).start()
        return carry

    lax.fori_loop(1, devices, send_rows, 0)
    incoming[0] = arrange(me)
    first.wait_recv()
    base = mine * half
    pending = [first]
    starts = [base, base + part_rows[0]]
    sizes = list(part_rows)
    offs = [0, sizes[0]]
    live = [p for p in range(2) if part_rows[p] > 0]
    acc[pl.ds(al(base), half), :] = acc[pl.ds(al(base), half), :] + recv0[...].astype(jnp.float32)
    sem = 1
    scratch_at = 0
    history = []
    for step in range(bits - 1):
        copies = []
        for p in live:
            bit = orders[p][step]
            mine, where = partner(bit)
            size = sizes[p] // 2
            keep = starts[p] + mine * size
            give = starts[p] + (1 - mine) * size
            low[pl.ds(al(give), size), :] = acc[pl.ds(al(give), size), :].astype(jnp.bfloat16)
            landing = recv1.at[pl.ds(scratch_at, size)]
            copy = pltpu.make_async_remote_copy(low.at[pl.ds(al(give), size)], landing, send_r.at[sem], recv_r.at[sem],
                                                device_id=where, device_id_type=MESH)
            copy.start()
            copies.append((p, copy, keep, size, scratch_at, where))
            sem += 1
            scratch_at += size
        for p, copy, keep, size, off, where in copies:
            copy.wait_recv()
            acc[pl.ds(al(keep), size), :] = acc[pl.ds(al(keep), size), :] + recv1[pl.ds(off, size), :].astype(jnp.float32)
            history.append((p, keep, size, where))
            starts[p], sizes[p] = keep, size
            pending.append(copy)
    copies = []
    off = 0
    final = {}
    for p in live:
        size = sizes[p] // dp_count
        for k in range(1, dp_count):
            other = lax.rem(dp + k, dp_count)
            give = starts[p] + other * size
            low[pl.ds(al(give), size), :] = acc[pl.ds(al(give), size), :].astype(jnp.bfloat16)
            copy = pltpu.make_async_remote_copy(low.at[pl.ds(al(give), size)], recv2.at[pl.ds(off, size)], send_r.at[sem], recv_r.at[sem],
                                                device_id=(other, row), device_id_type=MESH)
            copy.start()
            copies.append((p, copy, off, size))
            sem += 1
            off += size
        final[p] = (starts[p] + dp * size, size)
    for p, copy, off, size in copies:
        copy.wait_recv()
        at, size = final[p]
        acc[pl.ds(al(at), size), :] = acc[pl.ds(al(at), size), :] + recv2[pl.ds(off, size), :].astype(jnp.float32)
        pending.append(copy)
    total = jnp.zeros((1, width), jnp.float32)
    for p in live:
        at, size = final[p]
        mine_low = acc[pl.ds(al(at), size), :]
        total = total + jnp.sum(mine_low * mine_low, axis=0, keepdims=True)
        gathered[pl.ds(al(at), size), :] = mine_low.astype(jnp.bfloat16)
    square[...] = jnp.broadcast_to(total, square.shape)

    copies = []
    for p in live:
        at, size = final[p]
        for k in range(1, dp_count):
            other = lax.rem(dp + k, dp_count)
            copy = pltpu.make_async_remote_copy(gathered.at[pl.ds(al(at), size)], gathered.at[pl.ds(al(at), size)], send_r.at[sem], recv_r.at[sem],
                                                device_id=(other, row), device_id_type=MESH)
            copy.start()
            copies.append((p, copy, k, sem))
            sem += 1
    for p, copy, k, s in copies:
        at, size = final[p]
        source = lax.rem(dp + dp_count - k, dp_count)
        land = starts[p] + source * size
        pltpu.make_async_remote_copy(gathered.at[pl.ds(al(at), size)], gathered.at[pl.ds(al(land), size)], send_r.at[s], recv_r.at[s],
                                     device_id=(source, row), device_id_type=MESH).wait_recv()
        pending.append(copy)
    for step in range(bits - 2, -1, -1):
        copies = []
        for p in live:
            bit = orders[p][step]
            mine, where = partner(bit)
            size = sizes[p]
            at = starts[p]
            copy = pltpu.make_async_remote_copy(gathered.at[pl.ds(al(at), size)], gathered.at[pl.ds(al(at), size)], send_r.at[sem], recv_r.at[sem],
                                                device_id=where, device_id_type=MESH)
            copy.start()
            copies.append((p, copy, sem, mine, size, where))
            sem += 1
        for p, copy, s, mine, size, where in copies:
            bottom = starts[p] - mine * size
            land = bottom + (1 - mine) * size
            pltpu.make_async_remote_copy(gathered.at[pl.ds(al(land), size)], gathered.at[pl.ds(al(land), size)], send_r.at[s], recv_r.at[s],
                                         device_id=where, device_id_type=MESH).wait_recv()
            starts[p], sizes[p] = bottom, 2 * size
            pending.append(copy)
    mine, where = partner(0)
    last = pltpu.make_async_remote_copy(gathered.at[pl.ds(al(mine * half), half)], gathered.at[pl.ds(al(mine * half), half)], send_r.at[sem], recv_r.at[sem],
                                        device_id=where, device_id_type=MESH)
    last.start()
    pltpu.make_async_remote_copy(gathered.at[pl.ds(al((1 - mine) * half), half)], gathered.at[pl.ds(al((1 - mine) * half), half)], send_r.at[sem], recv_r.at[sem],
                                 device_id=where, device_id_type=MESH).wait_recv()
    sem += 1
    pending.append(last)
    lax.fori_loop(1, devices, lambda k, c: (a2a_recv(k).wait_recv(), c)[1], 0)
    for copy in pending:
        copy.wait_send()
    lax.fori_loop(1, devices, lambda k, c: (a2a_send(k).wait_send(), c)[1], 0)


def tail_exchange(dp_count, row_count, capacity, qkv, out, up, down, pos, row_grads, slots):
    devices = dp_count * row_count
    width = out.shape[1]
    rows = sum(a.size for a in (qkv, out, up, down, pos)) // width
    padded = reduce_rows(rows, devices)
    bits = row_count.bit_length() - 1
    sems = 2 + 4 * bits + 4 * dp_count + 8
    return pl.pallas_call(
        functools.partial(tail_kernel, dp_count, row_count, padded, capacity),
        out_shape=(jax.ShapeDtypeStruct((devices, capacity, width), jnp.bfloat16), jax.ShapeDtypeStruct((padded, width), jnp.bfloat16),
                   jax.ShapeDtypeStruct((8, width), jnp.float32)),
        in_specs=[VMEM] * 7, out_specs=(VMEM,) * 3,
        scratch_shapes=[
            pltpu.VMEM((devices, capacity, width), jnp.bfloat16),
            pltpu.VMEM((padded, width), jnp.float32),
            pltpu.VMEM((padded, width), jnp.bfloat16),
            pltpu.VMEM((padded // 2, width), jnp.bfloat16),
            pltpu.VMEM((padded // 2, width), jnp.bfloat16),
            pltpu.VMEM((padded // row_count, width), jnp.bfloat16),
            pltpu.SemaphoreType.DMA((devices,)), pltpu.SemaphoreType.DMA((devices,)),
            pltpu.SemaphoreType.DMA((sems,)), pltpu.SemaphoreType.DMA((sems,)),
        ],
        name="tail_exchange",
        compiler_params=pltpu.CompilerParams(collective_id=3, has_side_effects=True, vmem_limit_bytes=56 * 2**20),
    )(qkv, out, up, down, pos, row_grads, slots)


def other_device(k, dp_count, row_count):
    devices = dp_count * row_count
    me = lax.axis_index("dp") * row_count + lax.axis_index("rows")
    other = lax.rem(me + k, devices)
    return other, (other // row_count, lax.rem(other, row_count))


def one_hot(flags):
    return jnp.where(flags, 1.0, 0.0).astype(jnp.bfloat16)


def lookup_kernel(dp_count, row_count, capacity, used, wanted, item_row, table_hbm, fetched, slots, received,
                  table, pieces, slot_col, asked, ask, got, stage, ready, landed, found_rows, asked_here,
                  table_sem, local_sem, send_q, recv_q, send_a, recv_a):
    devices = dp_count * row_count
    me = lax.axis_index("dp") * row_count + lax.axis_index("rows")
    rows_here = table.shape[0]
    events = wanted.shape[0]
    chunk = 256
    barrier = pltpu.get_barrier_semaphore()
    load_table = pltpu.make_async_copy(table_hbm, table, table_sem)
    load_table.start()

    def greet(k, carry):
        other, where = other_device(k, dp_count, row_count)
        pl.semaphore_signal(barrier, inc=1, device_id=where, device_id_type=MESH)
        return carry

    lax.fori_loop(1, devices, greet, 0)

    whole_rows = item_row.shape[0]
    lanes = item_row.shape[1]
    pieces[pl.ds(whole_rows, pieces.shape[0] - whole_rows), :] = jnp.zeros(
        (pieces.shape[0] - whole_rows, 3 * lanes), jnp.bfloat16
    )
    part = 224
    def cut(c, carry):
        at = pl.multiple_of(c * part, 16)
        values = item_row[pl.ds(at, part), :]
        for digit in range(3):
            piece = jnp.bitwise_and(jnp.right_shift(values, 8 * digit), 255)
            pieces[pl.ds(at, part), digit * lanes : (digit + 1) * lanes] = piece.astype(jnp.float32).astype(jnp.bfloat16)
        return carry
    lax.fori_loop(0, whole_rows // part, cut, 0)

    lane = lax.broadcasted_iota(jnp.int32, (chunk, lanes), 1)
    lane_f = lane.astype(jnp.float32)
    wide = lax.broadcasted_iota(jnp.int32, (chunk, pieces.shape[0]), 1)
    below = one_hot(
        lax.broadcasted_iota(jnp.int32, (chunk, chunk), 1) < lax.broadcasted_iota(jnp.int32, (chunk, chunk), 0)
    )
    diagonal = lax.broadcasted_iota(jnp.int32, (chunk, chunk), 1) == lax.broadcasted_iota(jnp.int32, (chunk, chunk), 0)
    asked[...] = jnp.zeros_like(asked)

    def route(c, counts):
        at = pl.multiple_of(c * chunk, chunk)
        ids = wanted[pl.ds(at, chunk), :]
        high = jnp.right_shift(ids, 7)
        low = jnp.bitwise_and(ids, 127)
        found = jnp.dot(one_hot(wide == high), pieces[...], preferred_element_type=jnp.float32)
        value = found[:, :lanes] + 256.0 * found[:, lanes : 2 * lanes] + 65536.0 * found[:, 2 * lanes :]
        row = jnp.sum(jnp.where(lane == low, value, 0.0), axis=1, keepdims=True)
        owner = jnp.floor((row + 0.5) * (1.0 / rows_here))
        local = row - owner * rows_here
        live = ids >= 0
        owned = jnp.logical_and(lane_f == owner, live)
        owned_low = one_hot(owned)
        before = jnp.dot(below, owned_low, preferred_element_type=jnp.float32) + counts
        rank = jnp.sum(jnp.where(owned, before, 0.0), axis=1, keepdims=True)
        slot = jnp.where(live, owner * capacity + rank, -1.0)
        slot_col[pl.ds(at, chunk), :] = slot
        slots[pl.ds(c, 1), :] = jnp.sum(jnp.where(diagonal, slot, 0.0), axis=0, keepdims=True)
        local_high = jnp.floor(local * (1.0 / 128))
        local_low = local - 128.0 * local_high
        at_rank = lane_f == rank
        both = jnp.concatenate(
            [jnp.where(at_rank, local_high, 0.0), jnp.where(at_rank, local_low, 0.0)], axis=1
        ).astype(jnp.bfloat16)
        asked[...] += lax.dot_general(owned_low, both, (((0,), (0,)), ((), ())), preferred_element_type=jnp.float32)
        return counts + jnp.sum(jnp.where(owned, 1.0, 0.0), axis=0, keepdims=True)

    lax.fori_loop(0, events // chunk, route, jnp.zeros((1, lanes), jnp.float32))
    rows_asked = (128.0 * asked[:, :lanes] + asked[:, lanes:]).astype(jnp.int32)
    for d in range(devices):
        ask[d] = rows_asked[d : d + 1, :]
    pl.semaphore_wait(barrier, devices - 1)

    def query(k, at_other):
        other, where = other_device(k, dp_count, row_count)
        return pltpu.make_async_remote_copy(
            ask.at[other], got.at[other if at_other else me], send_q.at[k], recv_q.at[other if at_other else me],
            device_id=where, device_id_type=MESH,
        )

    def answer(k):
        other, where = other_device(k, dp_count, row_count)
        return pltpu.make_async_remote_copy(
            ready.at[k], landed.at[pl.ds(pl.multiple_of(k * capacity, 16), capacity)], send_a.at[k], recv_a.at[k],
            device_id=where, device_id_type=MESH,
        )

    lax.fori_loop(1, devices, lambda k, c: (query(k, False).start(), c)[1], 0)
    got[me] = ask[me]
    stage[...] = jnp.zeros_like(stage)
    load_table.wait()
    lax.fori_loop(1, devices, lambda k, c: (query(k, True).wait_recv(), c)[1], 0)
    got[...] = jnp.clip(got[...], 0, rows_here - 1)
    to_scalars = pltpu.make_async_copy(got, asked_here, local_sem)
    to_scalars.start()

    def by_distance(k, carry):
        received[k] = got[lax.rem(me + devices - k, devices)]
        return carry

    lax.fori_loop(0, devices, by_distance, 0)
    to_scalars.wait()

    def gather(source):
        def some(c, carry):
            at = pl.multiple_of(c * 8, 8)
            for j in range(8):
                row = asked_here[source, 0, at + j]
                stage[pl.ds(at + j, 1), :] = table[pl.ds(row, 1), :]
            return carry
        lax.fori_loop(0, used // 8, some, 0)
        return stage[...].astype(jnp.bfloat16)

    groups = 4
    each = devices // groups

    def prepare(k, carry):
        ready[k] = gather(other_device(k, dp_count, row_count)[0])
        return carry

    def reply(k, carry):
        prepare(k, 0)
        answer(k).start()
        return carry

    def settle(g, begin, end):
        lax.fori_loop(max(1, g * each), (g + 1) * each, lambda k, c: (answer(k).wait_recv(), c)[1], 0)
        span = each * capacity
        at_lane = lax.broadcasted_iota(jnp.int32, (1, span), 1)
        slot = at_lane
        for j in range(each):
            inside = jnp.logical_and(at_lane >= j * capacity, at_lane < (j + 1) * capacity)
            owner = other_device(devices - g * each - j, dp_count, row_count)[0]
            slot = slot + jnp.where(inside, (owner - j) * capacity, 0)
        slot = slot.astype(jnp.float32)
        rows = landed[g * span : (g + 1) * span, :]
        some = 2 * chunk

        def place(c, carry):
            at = pl.multiple_of(c * some, some)
            value = dot_nn(one_hot(slot == slot_col[pl.ds(at, some), :]), rows)
            if not begin:
                value = value + found_rows[pl.ds(at, some), :]
            if end:
                fetched[pl.ds(at, some), :] = value.astype(jnp.bfloat16)
            else:
                found_rows[pl.ds(at, some), :] = value
            return carry

        lax.fori_loop(0, events // some, place, 0)

    lax.fori_loop(each, 2 * each, reply, 0)
    lax.fori_loop(3 * each, devices, reply, 0)
    lax.fori_loop(1, each, reply, 0)
    landed[0:capacity, :] = gather(me)
    lax.fori_loop(2 * each, 3 * each, prepare, 0)
    lax.fori_loop(each, 2 * each, lambda k, c: (answer(k).wait_send(), c)[1], 0)
    lax.fori_loop(2 * each, 3 * each, lambda k, c: (answer(k).start(), c)[1], 0)
    settle(0, True, False)
    settle(1, False, False)
    settle(3, False, False)
    settle(2, False, True)
    lax.fori_loop(1, devices, lambda k, c: (query(k, False).wait_send(), c)[1], 0)
    lax.fori_loop(1, each, lambda k, c: (answer(k).wait_send(), c)[1], 0)
    lax.fori_loop(2 * each, devices, lambda k, c: (answer(k).wait_send(), c)[1], 0)


def lookup(dp_count, row_count, capacity, used, wanted, item_row, item_table):
    devices = dp_count * row_count
    events = wanted.shape[0]
    lanes = 128
    width = item_table.shape[1]
    blocks = item_row.shape[0] // lanes
    return pl.pallas_call(
        functools.partial(lookup_kernel, dp_count, row_count, capacity, used),
        out_shape=(
            jax.ShapeDtypeStruct((events, width), jnp.bfloat16),
            jax.ShapeDtypeStruct((events // 256, 256), jnp.float32),
            jax.ShapeDtypeStruct((devices, 1, lanes), jnp.int32),
        ),
        in_specs=[VMEM, VMEM, pl.BlockSpec(memory_space=pl.ANY)],
        out_specs=(VMEM,) * 3,
        scratch_shapes=[
            pltpu.VMEM(item_table.shape, jnp.float32),
            pltpu.VMEM((-(-blocks // lanes) * lanes, 3 * lanes), jnp.bfloat16),
            pltpu.VMEM((events, 1), jnp.float32),
            pltpu.VMEM((lanes, 2 * lanes), jnp.float32),
            pltpu.VMEM((devices, 1, lanes), jnp.int32),
            pltpu.VMEM((devices, 1, lanes), jnp.int32),
            pltpu.VMEM((capacity, width), jnp.float32),
            pltpu.VMEM((devices, capacity, width), jnp.bfloat16),
            pltpu.VMEM((devices * capacity, width), jnp.bfloat16),
            pltpu.VMEM((events, width), jnp.float32),
            pltpu.SMEM((devices, 1, lanes), jnp.int32),
            pltpu.SemaphoreType.DMA,
            pltpu.SemaphoreType.DMA,
            pltpu.SemaphoreType.DMA((devices,)),
            pltpu.SemaphoreType.DMA((devices,)),
            pltpu.SemaphoreType.DMA((devices,)),
            pltpu.SemaphoreType.DMA((devices,)),
        ],
        name="lookup",
        compiler_params=pltpu.CompilerParams(collective_id=2, has_side_effects=True, vmem_limit_bytes=56 * 2**20),
    )(wanted, item_row.reshape(-1, lanes), item_table)


def table_kernel(received, incoming, grads, square):
    tile, width = grads.shape
    step = pl.program_id(0)
    rows = lax.broadcasted_iota(jnp.int32, (tile, received.shape[1]), 0) + step * tile
    grad = jnp.dot(one_hot(rows == received[...]), incoming[...], preferred_element_type=jnp.float32)
    grads[...] = grad

    @pl.when(step == 0)
    def start():
        square[...] = jnp.zeros_like(square)

    square[...] += jnp.broadcast_to(jnp.sum(grad * grad, axis=0, keepdims=True), square.shape)


def table_gradient(rows_here, received, incoming):
    width = incoming.shape[1]
    tile = 224
    return pl.pallas_call(
        table_kernel,
        grid=(rows_here // tile,),
        out_shape=(
            jax.ShapeDtypeStruct((rows_here, width), jnp.float32),
            jax.ShapeDtypeStruct((8, width), jnp.float32),
        ),
        in_specs=[
            pl.BlockSpec(received.shape, lambda i: (0, 0)),
            pl.BlockSpec(incoming.shape, lambda i: (0, 0)),
        ],
        out_specs=(
            pl.BlockSpec((tile, width), lambda i: (i, 0)),
            pl.BlockSpec((8, width), lambda i: (0, 0)),
        ),
        name="table_gradient",
        compiler_params=pltpu.CompilerParams(vmem_limit_bytes=40 * 2**20),
    )(received, incoming)


def dot_nn(first_op, second_op):
    return jnp.dot(first_op, second_op, preferred_element_type=jnp.float32)


def dot_nt(first_op, second_op):
    return lax.dot_general(
        first_op, second_op, (((1,), (1,)), ((), ())), preferred_element_type=jnp.float32
    )


def dot_tn(first_op, second_op):
    return lax.dot_general(
        first_op, second_op, (((0,), (0,)), ((), ())), preferred_element_type=jnp.float32
    )


def inverse_rms(values):
    return lax.rsqrt(jnp.mean(values * values, axis=-1, keepdims=True) + NORM_EPS)


def rms_back(values, gain_row, grad):
    scale = inverse_rms(values)
    grad_scaled = grad * gain_row
    inner = jnp.mean(values * grad_scaled, axis=-1, keepdims=True)
    gain_part = jnp.sum(grad * values * scale, axis=0, keepdims=True)
    return scale * grad_scaled - values * (scale * scale * scale * inner), gain_part


def subsets(bits):
    found = [()]
    for bit in bits:
        found = found + [one + (bit,) for one in found]
    return found


def flip(index, bits):
    for bit in bits:
        step = 1 << bit
        index = index + step - 2 * step * lax.rem(index // step, 2)
    return index


def layer_kernel(dp_count, row_count, capacity, rows_here, lengths, items, targets, correction, qkv_hbm, out_hbm,
                 up_hbm, down_hbm, positions, gains, slots, received,
                 table_grads, gathered, summed,
                 qkv_low, out_low, up_low, down_low, embedded, hidden_one, joined, probs_top, probs_low, attended,
                 middle, hidden_two, slope, active, output, query, cand, bias, cand_grads, landing, logits,
                 grad_logits, highest, row_grads, small, acc, got_sums, incoming, by_row, by_dp, row_small, squares, square_low, square_all, part_k, part_v,
                 load_sem, send_b, recv_b, send_g, recv_g, send_s, recv_s, send_r, recv_r, send_a, recv_a,
                 send_n, recv_n, send_q, recv_q, store_sem):
    devices = dp_count * row_count
    micro = 2
    tokens = positions.shape[0]
    half = tokens // 2
    width = positions.shape[1]
    inner = out_low.shape[0]
    bits = row_count.bit_length() - 1
    dp = lax.axis_index("dp")
    row = lax.axis_index("rows")
    bf = jnp.bfloat16
    barrier = pltpu.get_barrier_semaphore()

    def greet(k, carry):
        other, where = other_device(k, dp_count, row_count)
        pl.semaphore_signal(barrier, inc=1, device_id=where, device_id_type=MESH)
        return carry

    lax.fori_loop(1, devices, greet, 0)
    ff = up_low.shape[1]
    loads = [
        (qkv_hbm, 0, 0, 3 * inner, qkv_low),
        (up_hbm, 0, 3 * inner, ff, up_low),
    ]
    at = 3 * inner + ff
    for source, low in ((out_hbm, out_low), (down_hbm, down_low)):
        for k in range(source.shape[0] // width):
            loads.append((source, k * width, at, width, low))
            at += width
    copies = []
    for k, (source, first, at, count, low) in enumerate(loads):
        copy = pltpu.make_async_copy(
            source.at[pl.ds(first, width)], logits.at[:, pl.ds(at, count)], load_sem.at[k]
        )
        copy.start()
        copies.append(copy)

    column = lax.broadcasted_iota(jnp.int32, (1, tokens), 1)
    for m in range(micro):
        own_bias = jnp.where(
            column < lengths[m], (-correction[m : m + 1, :]).astype(bf).astype(jnp.float32), MASKED
        )
        bias[row, m : m + 1, :] = own_bias.astype(bf).astype(jnp.float32)
        cand[pl.ds(pl.multiple_of((m * row_count + row) * tokens, tokens), tokens), :] = targets[m * tokens : (m + 1) * tokens, :]
    pl.semaphore_wait(barrier, devices - 1)

    pending = []
    gathers = []
    for k in range(1, row_count):
        copy = pltpu.make_async_remote_copy(
            bias.at[row], bias.at[row], send_b.at[k], recv_b.at[row],
            device_id=(dp, lax.rem(row + k, row_count)), device_id_type=MESH,
        )
        copy.start()
        pending.append(copy)

    orders = [list(range(1, bits)) + [0], list(range(bits - 1, 0, -1)) + [0]]
    block_of = lambda ref, m, owner: ref.at[pl.ds(pl.multiple_of((m * row_count + owner) * tokens, tokens), tokens)]
    gather_steps = []
    count = 0
    for step in range(bits):
        here = []
        for m in range(micro):
            for mask in subsets(orders[m][:step]):
                here.append((m, orders[m][step], mask, count))
                count += 1
        gather_steps.append(here)

    def gather_start(step):
        for m, bit, mask, sem in gather_steps[step]:
            mine = flip(row, mask)
            copy = pltpu.make_async_remote_copy(
                block_of(cand, m, mine), block_of(cand, m, mine), send_g.at[sem], recv_g.at[sem],
                device_id=(dp, flip(row, (bit,))), device_id_type=MESH,
            )
            copy.start()
            gathers.append(copy)

    def gather_wait(step, only=None):
        for m, bit, mask, sem in gather_steps[step]:
            if only is not None and m != only:
                continue
            theirs = flip(flip(row, (bit,)), mask)
            pltpu.make_async_remote_copy(
                block_of(cand, m, theirs), block_of(cand, m, theirs), send_g.at[sem], recv_g.at[sem],
                device_id=(dp, flip(row, (bit,))), device_id_type=MESH,
            ).wait_recv()

    gather_start(0)

    scatter_orders = [[0] + list(range(1, bits)), [0] + list(range(bits - 1, 0, -1))]
    scatter_steps = []
    count = 0
    for m in range(micro):
        levels = []
        for step in range(bits):
            bit = scatter_orders[m][step]
            levels.append([(bit, mask, count + i) for i, mask in enumerate(subsets(scatter_orders[m][step + 1 :]))])
            count += len(levels[-1])
        scatter_steps.append(levels)

    def scatter_start(m, step):
        for bit, mask, sem in scatter_steps[m][step]:
            there = flip(row, (bit,))
            copy = pltpu.make_async_remote_copy(
                block_of(cand_grads, m, flip(there, mask)), landing.at[sem], send_s.at[sem], recv_s.at[sem],
                device_id=(dp, there), device_id_type=MESH,
            )
            copy.start()
            pending.append(copy)

    def scatter_wait(m, step):
        for bit, mask, sem in scatter_steps[m][step]:
            there = flip(row, (bit,))
            pltpu.make_async_remote_copy(
                block_of(cand_grads, m, flip(row, mask)), landing.at[sem], send_s.at[sem], recv_s.at[sem],
                device_id=(dp, there), device_id_type=MESH,
            ).wait_recv()
            base = (m * row_count + flip(row, mask)) * tokens
            last = step == bits - 1

            def add(c, carry):
                at = pl.multiple_of(base + c * 64, 64)
                near = pl.multiple_of(c * 64, 64)
                total = cand_grads[pl.ds(at, 64), :].astype(jnp.float32) + landing[sem, pl.ds(near, 64), :].astype(jnp.float32)
                if last:
                    row_grads[pl.ds(pl.multiple_of((micro + m) * tokens + c * 64, 64), 64), :] = total.astype(bf)
                else:
                    cand_grads[pl.ds(at, 64), :] = total.astype(bf)
                return carry

            lax.fori_loop(0, tokens // 64, add, 0)

    for copy, (source, first, at, count, low) in zip(copies, loads):
        copy.wait()
    for source, first, at, count, low in loads:
        low[pl.ds(first, width), :] = logits[:, pl.ds(at, count)].astype(bf)

    chunks = micro * 2
    gain_one, gain_two, gain_three = gains[0:1, :], gains[1:2, :], gains[2:3, :]
    scaling = math.sqrt(width)

    def project(c, carry):
        at = pl.multiple_of(c * half, half)
        near = pl.multiple_of(lax.rem(c, 2) * half, half)
        values = scaling * items[pl.ds(at, half), :].astype(jnp.float32) + positions[pl.ds(near, half), :]
        embedded[pl.ds(at, half), :] = values
        normed = (values * inverse_rms(values) * gain_one).astype(bf)
        hidden_one[pl.ds(at, half), :] = normed
        joined[pl.ds(at, half), :inner] = (dot_nn(normed, qkv_low[:, :inner]).astype(bf) * bf(0.125))
        joined[pl.ds(at, half), inner:] = dot_nn(normed, qkv_low[:, inner:]).astype(bf)
        return carry

    lax.fori_loop(0, chunks, project, 0)

    lane = lax.broadcasted_iota(jnp.int32, (1, 128), 1)
    head_mask = [jnp.where(lane < 64, 1.0, 0.0).astype(bf), jnp.where(lane < 64, 0.0, 1.0).astype(bf)]
    pairs = inner // 128
    sub = 32

    def attend(m, begin, end):
        masked_row = jnp.where(column < lengths[m], 0.0, MASKED)
        base = m * tokens

        def pair(hp, carry):
            lanes = [pl.ds(pl.multiple_of(k * inner + hp * 128, 128), 128) for k in range(3)]
            keys = joined[base : base + tokens, lanes[1]]
            values = joined[base : base + tokens, lanes[2]]
            for rb in range(2):
                first = base + rb * half
                span = (rb + 1) * half
                probs = probs_low if rb else probs_top
                queries = joined[first : first + half, lanes[0]]
                for h in range(2):
                    logits[:, h * tokens : h * tokens + span] = dot_nt(queries * head_mask[h], keys[:span])
                for h in range(2):
                    for s in range(half // sub):
                        value = logits[s * sub : (s + 1) * sub, h * tokens : h * tokens + span] + masked_row[:, :span]
                        allowed = (
                            lax.broadcasted_iota(jnp.int32, (sub, half), 1)
                            <= lax.broadcasted_iota(jnp.int32, (sub, half), 0) + s * sub
                        )
                        corner = jnp.where(allowed, value[:, rb * half :], MASKED)
                        value = jnp.concatenate([value[:, :half], corner], axis=1) if rb else corner
                        value = jnp.exp(value - jnp.max(value, axis=1, keepdims=True))
                        value = value * (1.0 / jnp.sum(value, axis=1, keepdims=True))
                        probs[m * 2 * pairs + hp * 2 + h, s * sub : (s + 1) * sub, :] = value.astype(bf)
                total = dot_nn(probs[m * 2 * pairs + hp * 2], values[:span] * head_mask[0]) + dot_nn(
                    probs[m * 2 * pairs + hp * 2 + 1], values[:span] * head_mask[1]
                )
                attended[first : first + half, pl.ds(pl.multiple_of(hp * 128, 128), 128)] = total.astype(bf)
            return carry

        lax.fori_loop(begin, end, pair, 0)

    middle_pair = pairs // 2
    attend(0, 0, middle_pair)
    gather_wait(0)
    gather_start(1)
    attend(0, middle_pair, pairs)
    attend(1, 0, pairs)

    gelu_scale = math.sqrt(2.0 / math.pi)

    def feed(c, carry):
        at = pl.multiple_of(c * half, half)
        values = embedded[pl.ds(at, half), :] + dot_nn(attended[pl.ds(at, half), :], out_low[...])
        middle[pl.ds(at, half), :] = values
        normed = (values * inverse_rms(values) * gain_two).astype(bf)
        hidden_two[pl.ds(at, half), :] = normed
        logits[:, :ff] = dot_nn(normed, up_low[...])

        def bend(s, carry):
            for part in range(2):
                near = pl.multiple_of(s * 32 + part * 16, 16)
                there = pl.multiple_of(at + s * 32 + part * 16, 16)
                upward = logits[pl.ds(near, 16), :ff]
                square = upward * upward
                bent = jnp.tanh(gelu_scale * upward * (1.0 + 0.044715 * square))
                active[pl.ds(there, 16), :] = (0.5 * upward * (1.0 + bent)).astype(bf)
                slope[pl.ds(there, 16), :] = 0.5 * (1.0 + bent) + 0.5 * gelu_scale * upward * (1.0 - bent * bent) * (
                    1.0 + 3.0 * 0.044715 * square
                )
            return carry

        lax.fori_loop(0, half // 32, bend, 0)
        values = values + dot_nn(active[pl.ds(at, half), :], down_low[...])
        output[pl.ds(at, half), :] = values
        query[pl.ds(at, half), :] = (values * inverse_rms(values) * gain_three).astype(bf)
        return carry

    lax.fori_loop(0, chunks - 1, feed, 0)
    for step in range(1, bits - 1):
        gather_wait(step)
        gather_start(step + 1)
    lax.fori_loop(chunks - 1, chunks, feed, 0)
    if bits > 1:
        gather_wait(bits - 1, 0)
    for k in range(1, row_count):
        other = lax.rem(row + k, row_count)
        pltpu.make_async_remote_copy(
            bias.at[other], bias.at[other], send_b.at[k], recv_b.at[other],
            device_id=(dp, other), device_id_type=MESH,
        ).wait_recv()

    block = 512
    blocks = row_count * tokens // block
    sub = 32
    diagonal = lax.broadcasted_iota(jnp.int32, (half, half), 1) == lax.broadcasted_iota(jnp.int32, (half, half), 0)

    def loss_half(m, rh):
        length = lengths[m]
        first = m * tokens + rh * half
        queries = query[first : first + half, :]
        highest[...] = jnp.full_like(highest, -3.0e38)

        def score(j, carry):
            at = pl.multiple_of(j * block, block)
            value = dot_nt(queries, cand[pl.ds(pl.multiple_of(m * row_count * tokens + at, block), block), :]) + bias[j, m : m + 1, :]
            logits[:, pl.ds(at, block)] = value
            top = jnp.maximum(
                jnp.maximum(value[:, :128], value[:, 128:256]), jnp.maximum(value[:, 256:384], value[:, 384:])
            )
            highest[...] = jnp.maximum(highest[...], top)
            return carry

        lax.fori_loop(0, blocks, score, 0)
        own_at = pl.ds(pl.multiple_of(row * tokens + rh * half, half), half)
        own_logit = jnp.sum(jnp.where(diagonal, logits[:, own_at], 0.0), axis=1, keepdims=True)
        top = jnp.max(highest[...], axis=1, keepdims=True)
        highest[...] = jnp.broadcast_to(top, highest.shape)
        part_k[:half, :] = jnp.zeros((half, 128), jnp.float32)

        def add_up(j, carry):
            for s in range(half // sub):
                rows = slice(s * sub, (s + 1) * sub)
                total = part_k[rows, :]
                for q in range(block // 128):
                    total = total + jnp.exp(
                        logits[rows, pl.ds(pl.multiple_of(j * block + q * 128, 128), 128)] - highest[rows, :]
                    )
                part_k[rows, :] = total
            return carry

        lax.fori_loop(0, blocks, add_up, 0)
        log_total = top + jnp.log(jnp.sum(part_k[:half, :], axis=1, keepdims=True))
        valid = jnp.where(lax.broadcasted_iota(jnp.int32, (half, 1), 0) + rh * half < length, 1.0, 0.0)
        highest[...] = jnp.broadcast_to(log_total, highest.shape)
        part_v[:half, :] = jnp.broadcast_to(valid, (half, 128))
        small[3:4, :] += jnp.broadcast_to(
            jnp.sum(valid * (log_total - own_logit), axis=0, keepdims=True), (1, width)
        )

        def soften(j, carry):
            for s in range(half // sub):
                rows = slice(s * sub, (s + 1) * sub)
                there = slice(rh * half + s * sub, rh * half + (s + 1) * sub)
                for q in range(block // 128):
                    at = pl.ds(pl.multiple_of(j * block + q * 128, 128), 128)
                    grad_logits[there, at] = (jnp.exp(logits[rows, at] - highest[rows, :]) * part_v[rows, :]).astype(bf)
            return carry

        lax.fori_loop(0, blocks, soften, 0)
        own = (jnp.exp(logits[:, own_at] - log_total) - jnp.where(diagonal, 1.0, 0.0)) * valid
        grad_logits[rh * half : (rh + 1) * half, own_at] = own.astype(bf)
        grad_query = dot_nn(
            grad_logits[rh * half : (rh + 1) * half, :], cand[m * row_count * tokens : (m + 1) * row_count * tokens, :]
        )
        grad, gain_part = rms_back(output[first : first + half, :], gain_three, grad_query)
        output[first : first + half, :] = grad
        small[2:3, :] += gain_part

    def loss_end(m):
        length = lengths[m]

        def to_targets(j, carry):
            at = pl.multiple_of(j * block, block)
            cand_grads[pl.ds(pl.multiple_of(m * row_count * tokens + at, block), block), :] = dot_tn(
                grad_logits[:, pl.ds(at, block)], query[m * tokens : (m + 1) * tokens, :]
            ).astype(bf)
            return carry

        lax.fori_loop(0, blocks, to_targets, 0)
        scatter_start(m, 0)
        small[4:5, :] += jnp.broadcast_to(
            jnp.sum(jnp.where(column < length, 1.0, 0.0), axis=1, keepdims=True), (1, width)
        )

    small[...] = jnp.zeros_like(small)
    squares[...] = jnp.zeros_like(squares)
    loss_half(0, 0)
    loss_half(0, 1)
    loss_end(0)
    if bits > 1:
        gather_wait(bits - 1, 1)
    loss_half(1, 0)
    scatter_wait(0, 0)
    if bits > 1:
        scatter_start(0, 1)
    loss_half(1, 1)
    loss_end(1)

    def partner(bit):
        mine = lax.rem(row // (1 << bit), 2)
        return mine, (dp, flip(row, (bit,)))

    low = cand
    squared = {}
    al = lambda value: pl.multiple_of(value, 16)

    def summing(first, rows, sem, land):
        half_rows = rows // 2
        units = rows // (16 * devices)
        sizes = [((units + 1) // 2) * 8 * devices, (units // 2) * 8 * devices]
        parts = [p for p in range(2) if sizes[p]]
        part_orders = [list(range(1, bits)), list(range(bits - 1, 0, -1))]

        def lower(at, size):
            low[pl.ds(al(at), size), :] = acc[pl.ds(al(at), size), :].astype(bf)

        def add(at, size, off):
            acc[pl.ds(al(at), size), :] += got_sums[pl.ds(off, size), :].astype(jnp.float32)

        def send(source, at, size, target, sem, where):
            copy = pltpu.make_async_remote_copy(
                source.at[pl.ds(al(at), size)], target, send_r.at[sem], recv_r.at[sem],
                device_id=where, device_id_type=MESH,
            )
            copy.start()
            pending.append(copy)
            return copy

        def expect(at, size, sem, where):
            pltpu.make_async_remote_copy(
                gathered.at[pl.ds(al(at), size)], gathered.at[pl.ds(al(at), size)], send_r.at[sem], recv_r.at[sem],
                device_id=where, device_id_type=MESH,
            ).wait_recv()

        mine, where = partner(0)
        give = first + (1 - mine) * half_rows
        lower(give, half_rows)
        copy = send(low, give, half_rows, got_sums.at[pl.ds(land, half_rows)], sem, where)
        yield
        copy.wait_recv()
        base = first + mine * half_rows
        add(base, half_rows, land)
        sem, land = sem + 1, land + half_rows
        starts = [base, base + sizes[0]]
        for step in range(bits - 1):
            moved = []
            for p in parts:
                mine, where = partner(part_orders[p][step])
                size = sizes[p] // 2
                give = starts[p] + (1 - mine) * size
                lower(give, size)
                copy = send(low, give, size, got_sums.at[pl.ds(land, size)], sem, where)
                starts[p], sizes[p] = starts[p] + mine * size, size
                moved.append((p, copy, land))
                sem, land = sem + 1, land + size
            yield
            for p, copy, at in moved:
                copy.wait_recv()
                add(starts[p], sizes[p], at)
        moved = []
        finals = {}
        for p in parts:
            size = sizes[p] // dp_count
            finals[p] = starts[p] + dp * size
            for k in range(1, dp_count):
                other = lax.rem(dp + k, dp_count)
                give = starts[p] + other * size
                lower(give, size)
                copy = send(low, give, size, got_sums.at[pl.ds(land, size)], sem, (other, row))
                moved.append((p, copy, land, size))
                sem, land = sem + 1, land + size
        yield
        for p, copy, at, size in moved:
            copy.wait_recv()
            add(finals[p], size, at)
        moved = []
        for p in parts:
            size = sizes[p] // dp_count
            at = finals[p]
            done = acc[pl.ds(al(at), size), :]
            squares[0:1, :] += jnp.sum(done * done, axis=0, keepdims=True)
            gathered[pl.ds(al(at), size), :] = done.astype(bf)
            squared[first] = True
            for k in range(1, dp_count):
                other = lax.rem(dp + k, dp_count)
                send(gathered, at, size, gathered.at[pl.ds(al(at), size)], sem, (other, row))
                moved.append((p, k, size, sem))
                sem += 1
        yield
        for p, k, size, one in moved:
            source = lax.rem(dp + dp_count - k, dp_count)
            expect(starts[p] + source * size, size, one, (source, row))
        for step in range(bits - 2, -1, -1):
            moved = []
            for p in parts:
                mine, where = partner(part_orders[p][step])
                send(gathered, starts[p], sizes[p], gathered.at[pl.ds(al(starts[p]), sizes[p])], sem, where)
                moved.append((p, mine, where, sem))
                sem += 1
            yield
            for p, mine, where, one in moved:
                bottom = starts[p] - mine * sizes[p]
                expect(bottom + (1 - mine) * sizes[p], sizes[p], one, where)
                starts[p], sizes[p] = bottom, 2 * sizes[p]
        mine, where = partner(0)
        send(gathered, first + mine * half_rows, half_rows, gathered.at[pl.ds(al(first + mine * half_rows), half_rows)], sem, where)
        yield
        expect(first + (1 - mine) * half_rows, half_rows, sem, where)

    for copy in gathers:
        copy.wait_send()
    rows_early = 2 * ff + inner
    rows_late = 3 * inner + tokens
    sems_each = send_r.shape[0] // 2
    early = summing(0, rows_early, 0, 0)
    late = summing(rows_early, rows_late, sems_each, rows_early)

    query[...] = output[...].astype(bf)
    for k in range(ff // width):
        acc[k * width : (k + 1) * width, :] = dot_tn(active[:, k * width : (k + 1) * width], query[...])
    scatter_wait(1, 0)
    if bits > 1:
        scatter_start(1, 1)

    grad_attended, grad_middle_low = 2 * tokens, 4 * tokens

    def feed_back(c, m):
        at = pl.multiple_of(m * tokens + c * half, half)
        near = pl.multiple_of(c * half, half)
        branch = query[pl.ds(at, half), :]
        for k in range(ff // width):
            active[pl.ds(at, half), k * width : (k + 1) * width] = (
                dot_nt(branch, down_low[k * width : (k + 1) * width, :])
                * slope[pl.ds(at, half), k * width : (k + 1) * width]
            ).astype(bf)
        grad_hidden = dot_nt(active[pl.ds(at, half), :], up_low[...])
        grad, gain_part = rms_back(middle[pl.ds(at, half), :], gain_two, grad_hidden)
        small[1:2, :] += gain_part
        grad = grad + output[pl.ds(at, half), :]
        output[pl.ds(at, half), :] = grad
        grad_low = grad.astype(bf)
        grad_logits[pl.ds(near, half), grad_middle_low + m * width : grad_middle_low + (m + 1) * width] = grad_low
        grad_logits[pl.ds(near, half), grad_attended + m * inner : grad_attended + (m + 1) * inner] = dot_nt(
            grad_low, out_low[...]
        ).astype(bf)

    for m in range(micro):
        lax.fori_loop(0, 2, lambda c, carry, m=m: (feed_back(c, m), carry)[1], 0)
    for k in range(ff // width):
        acc[ff + k * width : ff + (k + 1) * width, :] = dot_tn(hidden_two[...], active[:, k * width : (k + 1) * width])
    acc[2 * ff : 2 * ff + inner, :] = dot_tn(
        attended[:tokens, :], grad_logits[:, grad_middle_low : grad_middle_low + width]
    ) + dot_tn(attended[tokens:, :], grad_logits[:, grad_middle_low + width : grad_middle_low + 2 * width])
    next(early, None)
    for step in range(1, bits - 1):
        scatter_wait(0, step)
        scatter_start(0, step + 1)

    def attend_back(m, begin, end):
        base = m * tokens

        def pair(hp, carry):
            lanes = [pl.ds(pl.multiple_of(k * inner + hp * 128, 128), 128) for k in range(3)]
            here = pl.ds(pl.multiple_of(grad_attended + m * inner + hp * 128, 128), 128)
            keys = joined[base : base + tokens, lanes[1]]
            values = joined[base : base + tokens, lanes[2]]
            for rb in (1, 0):
                first = base + rb * half
                span = (rb + 1) * half
                probs = probs_low if rb else probs_top
                queries = joined[first : first + half, lanes[0]]
                upper = grad_logits[rb * half : (rb + 1) * half, here]
                for h in range(2):
                    logits[:, h * tokens : h * tokens + span] = dot_nt(upper * head_mask[h], values[:span])
                for h in range(2):
                    for s in range(half // sub):
                        chance = probs[m * 2 * pairs + hp * 2 + h, s * sub : (s + 1) * sub, :].astype(jnp.float32)
                        grad = logits[s * sub : (s + 1) * sub, h * tokens : h * tokens + span]
                        inner_sum = jnp.sum(chance * grad, axis=1, keepdims=True)
                        grad_logits[s * sub : (s + 1) * sub, h * tokens : h * tokens + span] = (
                            chance * (grad - inner_sum)
                        ).astype(bf)
                pieces = [grad_logits[:half, h * tokens : h * tokens + span] for h in range(2)]
                total_q = dot_nn(pieces[0], keys[:span] * head_mask[0]) + dot_nn(
                    pieces[1], keys[:span] * head_mask[1]
                )
                total_k = dot_tn(pieces[0], queries * head_mask[0]) + dot_tn(pieces[1], queries * head_mask[1])
                total_v = dot_tn(probs[m * 2 * pairs + hp * 2], upper * head_mask[0]) + dot_tn(
                    probs[m * 2 * pairs + hp * 2 + 1], upper * head_mask[1]
                )
                joined[first : first + half, lanes[0]] = (total_q * 0.125).astype(bf)
                if rb:
                    part_k[...] = total_k
                    part_v[...] = total_v
                else:
                    part_k[:half, :] += total_k
                    part_v[:half, :] += total_v
            joined[base : base + tokens, lanes[1]] = part_k[...].astype(bf)
            joined[base : base + tokens, lanes[2]] = part_v[...].astype(bf)
            return carry

        lax.fori_loop(begin, end, pair, 0)

    for m in range(micro):
        for begin in range(0, pairs, 2):
            attend_back(m, begin, min(begin + 2, pairs))
            next(early, None)
            if m == 0 and begin == 0:
                for step in range(1, bits - 1):
                    scatter_wait(1, step)
                    scatter_start(1, step + 1)

    place = rows_early + 3 * inner

    def project_back(c, carry):
        at = pl.multiple_of(c * half, half)
        near = pl.multiple_of(lax.rem(c, 2) * half, half)
        grad_hidden = dot_nt(joined[pl.ds(at, half), :], qkv_low[...])
        grad, gain_part = rms_back(embedded[pl.ds(at, half), :], gain_one, grad_hidden)
        small[0:1, :] += gain_part
        grad = grad + output[pl.ds(at, half), :]
        acc[pl.ds(pl.multiple_of(place + near, half), half), :] += grad
        row_grads[pl.ds(at, half), :] = (scaling * grad).astype(bf)
        return carry

    acc[place : place + tokens, :] = jnp.zeros((tokens, width), jnp.float32)
    lax.fori_loop(0, chunks, project_back, 0)
    next(early, None)
    for k in range(3 * inner // width):
        acc[rows_early + k * width : rows_early + (k + 1) * width, :] = dot_tn(
            hidden_one[...], joined[:, k * width : (k + 1) * width]
        )
    next(late, None)
    for m in range(micro):
        if bits > 1:
            scatter_wait(m, bits - 1)
    next(early, None)

    out_at = rows_early + rows_late
    slot_row = jnp.concatenate([slots[c : c + 1, :] for c in range(slots.shape[0])], axis=1)
    batch = 4
    at_row = lax.broadcasted_iota(jnp.int32, (batch * capacity, 1), 0)
    events = slot_row.shape[1]

    def arrange(first):
        target = at_row
        for j in range(batch):
            other, where = other_device(first + j, dp_count, row_count)
            inside = jnp.logical_and(at_row >= j * capacity, at_row < (j + 1) * capacity)
            target = target + jnp.where(inside, (other - j) * capacity, 0)
        target = target.astype(jnp.float32)
        total = None
        for c in range(events // tokens):
            pick = one_hot(target == slot_row[:, c * tokens : (c + 1) * tokens])
            part = dot_nn(pick, row_grads[c * tokens : (c + 1) * tokens, :])
            total = part if total is None else total + part
        cand[pl.ds(al(out_at + first * capacity), batch * capacity), :] = total.astype(bf)

    def block_copy(k):
        other, where = other_device(k, dp_count, row_count)
        return pltpu.make_async_remote_copy(
            cand.at[pl.ds(al(out_at + k * capacity), capacity)], incoming.at[pl.ds(al(k * capacity), capacity)],
            send_a.at[k], recv_a.at[k], device_id=where, device_id_type=MESH,
        )

    def send_batch(b, carry):
        arrange(b * batch)
        for j in range(batch):
            block_copy(b * batch + j).start()
        return carry

    groups = 4
    each = devices // groups
    batches = each // batch

    def send_group(g):
        if g:
            lax.fori_loop(g * batches, (g + 1) * batches, send_batch, 0)
            return
        lax.fori_loop(1, batches, send_batch, 0)
        arrange(0)
        for j in range(1, batch):
            block_copy(j).start()
        incoming[0:capacity, :] = cand[out_at : out_at + capacity, :]

    tile = 256
    tiles = -(-rows_here // tile)
    in_logits = logits.shape[1] // tile

    def add_table(g, begin, end):
        lax.fori_loop(max(1, g * each), (g + 1) * each, lambda k, c: (block_copy(k).wait_recv(), c)[1], 0)
        span = each * capacity
        ids = received[:, g * span : (g + 1) * span]
        rows = incoming[g * span : (g + 1) * span, :]
        near = one_hot(lax.broadcasted_iota(jnp.int32, (2 * tile, span), 0) == jnp.bitwise_and(ids, 2 * tile - 1))
        high = jnp.right_shift(ids, 9)

        def one(t, place, ref):
            both = dot_nn(near * one_hot(high == t), rows)
            for part in range(2):
                at_row, at_lane = place(2 * t + part)
                where = (pl.ds(pl.multiple_of(at_row, tile), tile), pl.ds(pl.multiple_of(at_lane, tile), tile))
                value = both[part * tile : (part + 1) * tile, :]
                if not begin:
                    value = value + ref[where]
                ref[where] = value
                if end:
                    squares[0:1, :] += jnp.sum(value * value, axis=0, keepdims=True)

        def first_ones(t, carry):
            one(t, lambda u: (0, u * tile), logits)
            return carry

        def other_ones(t, carry):
            one(
                t,
                lambda u: (((u - in_logits) // (ff // tile)) * tile, lax.rem(u - in_logits, ff // tile) * tile),
                slope,
            )
            return carry

        pairs_here = (tiles + 1) // 2
        lax.fori_loop(0, min(pairs_here, in_logits // 2), first_ones, 0)
        if pairs_here > in_logits // 2:
            lax.fori_loop(in_logits // 2, pairs_here, other_ones, 0)

    def spreading():
        def start(source, zone, mine, others, where, base):
            for k, other in enumerate(others):
                copy = pltpu.make_async_remote_copy(
                    source, zone.at[mine], send_n.at[base + k], recv_n.at[base + mine],
                    device_id=where(other), device_id_type=MESH,
                )
                copy.start()
                pending.append(copy)
            zone[mine] = source[...]

        def finish(source, zone, others, where, base):
            for other in others:
                pltpu.make_async_remote_copy(
                    source, zone.at[other], send_n.at[base], recv_n.at[base + other],
                    device_id=where(other), device_id_type=MESH,
                ).wait_recv()
            return jnp.sum(zone[...], axis=0)

        row_others = [lax.rem(row + k, row_count) for k in range(1, row_count)]
        dp_others = [lax.rem(dp + k, dp_count) for k in range(1, dp_count)]
        to_row, to_dp = (lambda o: (dp, o)), (lambda o: (o, row))
        start(small, by_row, row, row_others, to_row, 0)
        yield
        row_small[...] = finish(small, by_row, row_others, to_row, 0)
        start(row_small, by_dp, dp, dp_others, to_dp, row_count)
        yield
        summed[...] = finish(row_small, by_dp, dp_others, to_dp, row_count)

    spreader = spreading()
    next(spreader)
    send_group(1)
    next(late, None)
    send_group(3)
    next(early, None)
    send_group(0)
    next(late, None)
    next(early, None)
    lax.fori_loop(each, 2 * each, lambda k, c: (block_copy(k).wait_send(), c)[1], 0)
    send_group(2)
    next(spreader)
    next(late, None)
    add_table(0, True, False)
    next(late, None)
    next(early, None)
    add_table(1, False, False)
    next(spreader, None)
    next(late, None)
    next(early, None)
    add_table(3, False, False)
    next(late, None)
    next(early, None)
    add_table(2, False, True)

    stores = []
    for t in range(tiles):
        count = min(tile, rows_here - t * tile)
        if t < in_logits:
            source = logits.at[pl.ds(0, count), pl.ds(t * tile, tile)]
        else:
            u = t - in_logits
            source = slope.at[pl.ds((u // (ff // tile)) * tile, count), pl.ds((u % (ff // tile)) * tile, tile)]
        copy = pltpu.make_async_copy(source, table_grads.at[pl.ds(t * tile, count)], store_sem.at[t])
        copy.start()
        stores.append(copy)

    for first, summer in ((0, early), (rows_early, late)):
        while first not in squared:
            next(summer)
    me = dp * row_count + row
    square_low[...] = squares[0:1, :128] + squares[0:1, 128:]

    def square_copy(k, at_other):
        other, where = other_device(k, dp_count, row_count)
        place = other if at_other else me
        return pltpu.make_async_remote_copy(
            square_low, square_all.at[place], send_q.at[k], recv_q.at[place], device_id=where, device_id_type=MESH
        )

    lax.fori_loop(1, devices, lambda k, c: (square_copy(k, False).start(), c)[1], 0)
    square_all[me] = square_low[...]
    for summer in (late, early):
        for unused in summer:
            pass
    for copy in stores:
        copy.wait()
    for unused in spreader:
        pass
    lax.fori_loop(1, devices, lambda k, c: (square_copy(k, True).wait_recv(), c)[1], 0)
    summed[5:6, :128] = jnp.sum(square_all[...], axis=0)
    lax.fori_loop(1, devices, lambda k, c: (square_copy(k, False).wait_send(), c)[1], 0)
    lax.fori_loop(1, each, lambda k, c: (block_copy(k).wait_send(), c)[1], 0)
    lax.fori_loop(2 * each, devices, lambda k, c: (block_copy(k).wait_send(), c)[1], 0)
    for copy in pending:
        copy.wait_send()


def layer(dp_count, row_count, capacity, rows_here, lengths, items, targets, correction, matrices, positions, gains,
          slots, received):
    qkv, out, up, down = matrices
    tokens, width = positions.shape
    half = tokens // 2
    inner, ff = out.shape[0], up.shape[1]
    events = 2 * tokens
    group = row_count * tokens
    devices = dp_count * row_count
    bf, f32 = jnp.bfloat16, jnp.float32
    pairs = inner // 128
    bits = row_count.bit_length() - 1
    hops = 2 * (row_count - 1)
    summed_rows = 2 * ff + 4 * inner + tokens
    sems = lambda count: pltpu.SemaphoreType.DMA((count,))
    hbm = pl.BlockSpec(memory_space=pl.ANY)
    return pl.pallas_call(
        functools.partial(layer_kernel, dp_count, row_count, capacity, rows_here),
        out_shape=(
            jax.ShapeDtypeStruct((rows_here, width), f32),
            jax.ShapeDtypeStruct((summed_rows, width), bf),
            jax.ShapeDtypeStruct((8, width), f32),
        ),
        in_specs=[pl.BlockSpec(memory_space=pltpu.SMEM), VMEM, VMEM, VMEM, hbm, hbm, hbm, hbm] + [VMEM] * 4,
        out_specs=(hbm, VMEM, VMEM),
        scratch_shapes=[
            pltpu.VMEM(qkv.shape, bf),
            pltpu.VMEM(out.shape, bf),
            pltpu.VMEM(up.shape, bf),
            pltpu.VMEM(down.shape, bf),
            pltpu.VMEM((events, width), f32),
            pltpu.VMEM((events, width), bf),
            pltpu.VMEM((events, 3 * inner), bf),
            pltpu.VMEM((4 * pairs, half, half), bf),
            pltpu.VMEM((4 * pairs, half, tokens), bf),
            pltpu.VMEM((events, inner), bf),
            pltpu.VMEM((events, width), f32),
            pltpu.VMEM((events, width), bf),
            pltpu.VMEM((events, ff), f32),
            pltpu.VMEM((events, ff), bf),
            pltpu.VMEM((events, width), f32),
            pltpu.VMEM((events, width), bf),
            pltpu.VMEM((2 * group, width), bf),
            pltpu.VMEM((row_count, 2, tokens), f32),
            pltpu.VMEM((2 * group, width), bf),
            pltpu.VMEM((hops, tokens, width), bf),
            pltpu.VMEM((half, group), f32),
            pltpu.VMEM((tokens, group), bf),
            pltpu.VMEM((half, 128), f32),
            pltpu.VMEM((2 * events, width), bf),
            pltpu.VMEM((8, width), f32),
            pltpu.VMEM((summed_rows, width), f32),
            pltpu.VMEM((summed_rows, width), bf),
            pltpu.VMEM((devices * capacity, width), bf),
            pltpu.VMEM((row_count, 8, width), f32),
            pltpu.VMEM((dp_count, 8, width), f32),
            pltpu.VMEM((8, width), f32),
            pltpu.VMEM((8, width), f32),
            pltpu.VMEM((1, 128), f32),
            pltpu.VMEM((devices, 1, 128), f32),
            pltpu.VMEM((tokens, 128), f32),
            pltpu.VMEM((tokens, 128), f32),
            sems(2 + (inner + ff) // width),
            sems(row_count),
            sems(row_count),
            sems(hops),
            sems(hops),
            sems(hops),
            sems(hops),
            sems(2 * (4 * bits + 4 * dp_count)),
            sems(2 * (4 * bits + 4 * dp_count)),
            sems(devices),
            sems(devices),
            sems(devices),
            sems(devices),
            sems(devices),
            sems(devices),
            sems(-(-rows_here // 256)),
        ],
        name="layer",
        compiler_params=pltpu.CompilerParams(collective_id=5, has_side_effects=True, vmem_limit_bytes=62 * 2**20),
    )(lengths, items, targets, correction, qkv, out, up, down, positions, gains, slots, received)


def small_kernel(dp_count, row_count, part, summed, by_row, by_dp, send_sem, recv_sem):
    dp = lax.axis_index("dp")
    row = lax.axis_index("rows")
    barrier = pltpu.get_barrier_semaphore()
    row_places = [lax.rem(row + k, row_count) for k in range(1, row_count)]
    dp_places = [lax.rem(dp + k, dp_count) for k in range(1, dp_count)]
    for other in row_places:
        pl.semaphore_signal(barrier, inc=1, device_id=(dp, other), device_id_type=MESH)
    for other in dp_places:
        pl.semaphore_signal(barrier, inc=1, device_id=(other, row), device_id_type=MESH)
    pl.semaphore_wait(barrier, row_count + dp_count - 2)

    def spread(source, landing, mine, others, where, base):
        sends = []
        for k, other in enumerate(others):
            copy = pltpu.make_async_remote_copy(
                source, landing.at[mine], send_sem.at[base + k], recv_sem.at[base + mine],
                device_id=where(other), device_id_type=MESH,
            )
            copy.start()
            sends.append(copy)
        landing[mine] = source[...]
        for other in others:
            pltpu.make_async_remote_copy(
                source, landing.at[other], send_sem.at[base], recv_sem.at[base + other],
                device_id=where(other), device_id_type=MESH,
            ).wait_recv()
        for copy in sends:
            copy.wait_send()

    spread(part, by_row, row, row_places, lambda other: (dp, other), 0)
    summed[...] = jnp.sum(by_row[...], axis=0)
    spread(summed, by_dp, dp, dp_places, lambda other: (other, row), row_count)
    summed[...] = jnp.sum(by_dp[...], axis=0)


def small_sum(dp_count, row_count, part):
    return pl.pallas_call(
        functools.partial(small_kernel, dp_count, row_count),
        out_shape=jax.ShapeDtypeStruct(part.shape, part.dtype),
        in_specs=[VMEM],
        out_specs=VMEM,
        scratch_shapes=[
            pltpu.VMEM((row_count,) + part.shape, part.dtype),
            pltpu.VMEM((dp_count,) + part.shape, part.dtype),
            pltpu.SemaphoreType.DMA((row_count + dp_count,)),
            pltpu.SemaphoreType.DMA((row_count + dp_count,)),
        ],
        name="small_sum",
        compiler_params=pltpu.CompilerParams(collective_id=4, has_side_effects=True),
    )(part)


def grouped_layer(fetched, valid_pos, lengths, correction, weights, positions, gains):
    qkv_weight, out_weight, up_weight, down_weight = weights
    micro, tokens = valid_pos.shape
    histories = lengths.shape[1]
    length, width = positions.shape
    matrices = (rounded(qkv_weight), rounded(out_weight), rounded(up_weight), rounded(down_weight))
    scaling = math.sqrt(width)
    offset = lax.axis_index("rows") * tokens
    running = [
        jnp.zeros_like(qkv_weight),
        jnp.zeros_like(out_weight),
        jnp.zeros_like(up_weight),
        jnp.zeros_like(down_weight),
    ]
    grad_positions = jnp.zeros_like(positions)
    grad_gains = jnp.zeros_like(gains)
    loss_local = jnp.zeros((), jnp.float32)
    embed_grads = []
    target_grads = []
    for micro_index in range(micro):
        lengths_here = lengths[micro_index]
        valid_here = valid_pos[micro_index].astype(jnp.float32)
        embedded = scaling * fetched[0, micro_index].astype(jnp.float32) + jnp.tile(
            positions, (histories, 1)
        )
        output, saved_state = layer_forward(embedded, lengths_here, matrices, gains, HEADS)
        normed_three, back_three = jax.vjp(rms_norm, output, gains[2])
        query_low = rounded(normed_three)
        bias_low = jnp.where(
            valid_pos[micro_index],
            rounded(-correction[micro_index].reshape(-1)),
            jnp.asarray(MASKED, jnp.bfloat16),
        )
        candidates, cand_bias = (
            lax.all_gather(fetched[1, micro_index], "rows", axis=0, tiled=True),
            lax.all_gather(bias_low, "rows", axis=0, tiled=True),
        )
        loss_part, grad_logits, log_total = candidate_loss(
            query_low, candidates, cand_bias, valid_here, offset
        )
        loss_local = loss_local + loss_part
        grad_output, gain_three = back_three(matmul(grad_logits, candidates))
        target_grads.append(
            lax.psum_scatter(
                inner_rows(grad_logits, query_low).astype(jnp.bfloat16),
                "rows",
                scatter_dimension=0,
                tiled=True,
            ).astype(jnp.float32)
        )
        grad_embedded, grad_layer, gain_pair = layer_backward(
            grad_output, saved_state, lengths_here, matrices, HEADS
        )
        for which_one in range(4):
            running[which_one] = running[which_one] + grad_layer[which_one]
        grad_positions = grad_positions + jnp.sum(
            grad_embedded.reshape(histories, length, width), axis=0
        )
        grad_gains = grad_gains + jnp.stack([gain_pair[0], gain_pair[1], gain_three])
        embed_grads.append(scaling * grad_embedded)
    target_part = jnp.stack(target_grads)
    row_grads = jnp.concatenate([jnp.stack(embed_grads), target_part]).reshape(-1, width)
    return running, grad_positions, rounded(row_grads), grad_gains, loss_local


def local(
    item_ids,
    targets,
    lengths,
    correction,
    item_row,
    item_table,
    qkv_weight,
    out_weight,
    up_weight,
    down_weight,
    positions,
    gains,
    item_table_first,
    qkv_weight_first,
    out_weight_first,
    up_weight_first,
    down_weight_first,
    positions_first,
    gains_first,
    item_table_second,
    qkv_weight_second,
    out_weight_second,
    up_weight_second,
    down_weight_second,
    positions_second,
    gains_second,
):
    micro, histories, length = item_ids.shape
    rows_here, width = item_table.shape
    devices = lax.axis_size("dp") * lax.axis_size("rows")
    tokens = histories * length
    requests = 2 * micro * tokens
    capacity = 3 * (requests + devices) // (2 * devices) + 1
    used = -(-capacity // 8) * 8
    capacity = -(-capacity // 16) * 16
    dp_count, row_count = lax.axis_size("dp"), lax.axis_size("rows")
    position = jnp.arange(length, dtype=jnp.int32)
    valid_pos = (position[None, None, :] < lengths[:, :, None]).reshape(micro, tokens)
    wanted = jnp.where(
        valid_pos.reshape(1, -1), jnp.stack([item_ids, targets]).reshape(2, micro * tokens), -1
    ).reshape(requests, 1)
    fetched, slots, received = lookup(
        dp_count, row_count, capacity, used, wanted, item_row, item_table
    )
    received = received[:, 0, :capacity].reshape(1, devices * capacity)
    fetched = fetched.reshape(2, micro, tokens, width)
    weights = (qkv_weight, out_weight, up_weight, down_weight, positions)
    summed_rows = sum(one.size for one in weights) // width
    group = row_count * tokens
    fits = (
        histories == 1
        and micro == 2
        and row_count > 1
        and devices % 16 == 0
        and group <= 4096
        and summed_rows % (16 * devices) == 0
        and summed_rows + devices * capacity <= 2 * group
        and rows_here <= 4096 + group
    )
    if fits:
        table_grad, gathered, small = layer(
            dp_count,
            row_count,
            capacity,
            rows_here,
            lengths.reshape(micro),
            fetched[0].reshape(micro * tokens, width),
            fetched[1].reshape(micro * tokens, width),
            correction.reshape(micro, tokens),
            weights[:4],
            positions,
            gains,
            slots,
            received,
        )
        sum_gains, sum_loss, sum_count = small[:3], small[3, 0], small[4, 0]
        square_total = jnp.sum(small[5])
        order = (3, 2, 1, 0, 4)
    else:
        running, grad_positions, row_grads, grad_gains, loss_local = grouped_layer(
            fetched,
            valid_pos,
            lengths,
            correction,
            (qkv_weight, out_weight, up_weight, down_weight),
            positions,
            gains,
        )
        count_local = jnp.sum(valid_pos.astype(jnp.float32))
        incoming, gathered, square = tail_exchange(
            dp_count,
            row_count,
            capacity,
            running[0],
            running[1],
            running[2],
            running[3],
            grad_positions,
            row_grads,
            slots,
        )
        table_grad, table_square = table_gradient(
            rows_here, received, incoming.reshape(devices * capacity, width)
        )
        own_square = jnp.sum(table_square[0] + square[0])
        scalars = jnp.stack([loss_local, count_local, own_square])
        part = jnp.concatenate(
            [grad_gains.reshape(-1), jnp.pad(scalars, (0, 1024 - grad_gains.size - 3))]
        ).reshape(8, 128)
        small = small_sum(dp_count, row_count, part).reshape(-1)
        sum_gains = small[: grad_gains.size].reshape(grad_gains.shape)
        sum_loss, sum_count, square_total = (small[grad_gains.size + k] for k in range(3))
        order = (0, 2, 1, 3, 4)
    gathered = gathered.astype(jnp.float32)
    place = 0
    blocks = {}
    for which_one in order:
        like = weights[which_one]
        count = like.shape[1] // width
        piece = gathered[place : place + count * like.shape[0]]
        blocks[which_one] = jnp.concatenate(
            [piece[c * like.shape[0] : (c + 1) * like.shape[0]] for c in range(count)], axis=1
        )
        place += count * like.shape[0]
    gradients = (table_grad, blocks[0], blocks[1], blocks[2], blocks[3], blocks[4], sum_gains)
    grad_norm = jnp.sqrt(square_total + jnp.sum(sum_gains * sum_gains))
    factor = CLIP / jnp.maximum(grad_norm, CLIP)
    weights = (item_table, qkv_weight, out_weight, up_weight, down_weight, positions, gains)
    firsts = (
        item_table_first,
        qkv_weight_first,
        out_weight_first,
        up_weight_first,
        down_weight_first,
        positions_first,
        gains_first,
    )
    seconds = (
        item_table_second,
        qkv_weight_second,
        out_weight_second,
        up_weight_second,
        down_weight_second,
        positions_second,
        gains_second,
    )
    rates = (RATE, RATE, RATE, RATE, RATE, RATE, GAIN_RATE)
    decays = (DECAY, DECAY, DECAY, DECAY, DECAY, DECAY, 0.0)
    updated = [
        adam_step(
            weights[which_one],
            factor * gradients[which_one],
            firsts[which_one],
            seconds[which_one],
            rates[which_one],
            decays[which_one],
        )
        for which_one in range(7)
    ]
    return (
        updated[0][0],
        updated[1][0],
        updated[2][0],
        updated[3][0],
        updated[4][0],
        updated[5][0],
        updated[6][0],
        updated[0][1],
        updated[1][1],
        updated[2][1],
        updated[3][1],
        updated[4][1],
        updated[5][1],
        updated[6][1],
        updated[0][2],
        updated[1][2],
        updated[2][2],
        updated[3][2],
        updated[4][2],
        updated[5][2],
        updated[6][2],
        sum_loss,
        sum_count,
        grad_norm,
    )


def solution(mesh):
    placed = (
        P(None, ("dp", "rows"), None),
        P(None, ("dp", "rows"), None),
        P(None, ("dp", "rows")),
        P(None, ("dp", "rows"), None),
        P(),
        P(("dp", "rows"), None),
        P(),
        P(),
        P(),
        P(),
        P(),
        P(),
        P(("dp", "rows"), None),
        P(),
        P(),
        P(),
        P(),
        P(),
        P(),
        P(("dp", "rows"), None),
        P(),
        P(),
        P(),
        P(),
        P(),
        P(),
    )
    return jax.shard_map(
        local,
        mesh=mesh,
        in_specs=placed,
        out_specs=(
            P(("dp", "rows"), None),
            P(),
            P(),
            P(),
            P(),
            P(),
            P(),
            P(("dp", "rows"), None),
            P(),
            P(),
            P(),
            P(),
            P(),
            P(),
            P(("dp", "rows"), None),
            P(),
            P(),
            P(),
            P(),
            P(),
            P(),
            P(),
            P(),
            P(),
        ),
        check_vma=False,
    )
```
